512 devices in a mesh: lon: 64 (over z_hi, x, y, core), lat: 8 (over z_lo).
Axes of the slice: x: 4, y: 4, z: 16 (z_hi: 2, z_lo: 8; z = z_hi * 8 + z_lo), core: 2. Of those that a mesh axis runs over, the one named last changes fastest.
Arguments:
- field: bfloat16 [512, 1152, 512], P('lat', 'lon'), may hold values from -6 to 6
- region: int32 [512, 1152], P('lat', 'lon'), may hold values from 0 to 5, as said below
- w_qkv: bfloat16 [512, 1536], replicated, may hold values from -0.25 to 0.25
- w_proj: bfloat16 [512, 512], replicated, may hold values from -0.25 to 0.25
- w_up: bfloat16 [512, 2048], P(None, 'lat'), may hold values from -0.25 to 0.25
- w_down: bfloat16 [2048, 512], P('lat'), may hold values from -0.125 to 0.125
- position_bias: float32 [16, 72, 72], replicated, may hold values from -6 to 252
Outputs:
- result: bfloat16 [512, 1152, 512], P('lat', 'lon')
The draws below stay inside these ranges and needn't reach their ends.
Inputs may be any that keep to these rules, and one draw needn't show every extreme that they name: `region`: rows 0 to 3 of the grid carry ids 3 to 5, all other rows ids 0 to 2.
All inputs are finite; a program needn't handle non-finite values.
Results may differ from the reference program's by a relative error of at most 0.0075.
Values may be sent and summed in bfloat16 or wider, within the bound.
A program may use at most 128 MiB of HBM per device.

```python
import jax
import jax.numpy as jnp
from jax import lax

D = 512
FF = 2048
HEADS = 16
HEAD_DIM = 32
WIN_ROWS = 8
WIN_COLS = 9
WIN_TOK = 72
SHIFT = 4
LAT_ROWS = 512
LON_COLS = 1152


def draw_region(key, part):
    key = jax.random.fold_in(key, 11)
    base = jax.random.randint(key, (LAT_ROWS, LON_COLS), 0, 3)
    rows = lax.broadcasted_iota(jnp.int32, (LAT_ROWS, LON_COLS), 0)
    return (base + 3 * (rows < SHIFT).astype(jnp.int32)).astype(jnp.int32)


def draw_position_bias(key, part):
    key = jax.random.fold_in(key, 23)
    shape = (HEADS, WIN_TOK, WIN_TOK)
    return jnp.clip(jax.random.normal(key, shape, jnp.float32), -6.0, 6.0)


def levels(rng, dims, shards, low, high):
    factor_of = 1.0
    for dim, blocks in shards:
        steps = jax.random.uniform(jax.random.fold_in(jax.random.fold_in(rng, 6), dim), (blocks,), jnp.float32, low / len(shards), high / len(shards))
        factor_of = factor_of * jnp.repeat(jnp.exp(steps), dims[dim] // blocks).reshape((-1,) + (1,) * (len(dims) - 1 - dim))
    return factor_of


def bell_draw(stream_key, dims, scale, most, pieces=(), dtype=jnp.bfloat16):
    loudness = levels(stream_key, dims, pieces, -0.22, 0.18) if pieces else 1.0
    result = jax.random.normal(stream_key, dims, jnp.float32) * scale * loudness
    return jnp.minimum(jnp.maximum(result, -most), most).astype(dtype)


def setup_inputs(seed: int = 0) -> dict:
    seeds = jax.random.split(jax.random.key(seed), 8)
    field = bell_draw(seeds[0], (LAT_ROWS, LON_COLS, D), 1.0, 6.0, ((0, 8), (1, 64)))
    region = draw_region(jax.random.fold_in(seeds[7], 71), 0)
    w_qkv = bell_draw(seeds[2], (D, 3 * D), D ** -0.5, 0.25)
    w_proj = bell_draw(seeds[3], (D, D), D ** -0.5, 0.25)
    w_up = bell_draw(seeds[4], (D, FF), D ** -0.5, 0.25, ((1, 8),))
    w_down = bell_draw(seeds[5], (FF, D), FF ** -0.5, 0.125, ((0, 8),))
    position_bias = draw_position_bias(jax.random.fold_in(seeds[7], 71), 0)
    return dict(field=field, region=region, w_qkv=w_qkv, w_proj=w_proj, w_up=w_up, w_down=w_down, position_bias=position_bias)


def layer_norm(values):
    floats = values.astype(jnp.float32)
    center = lax.optimization_barrier(jnp.mean(floats, axis=-1, keepdims=True))
    spread = lax.optimization_barrier(jnp.mean((floats - center) ** 2, axis=-1, keepdims=True))
    return ((floats - center) * lax.rsqrt(spread + 1e-05)).astype(jnp.bfloat16)

def to_windows(block):
    rows, cols = (block.shape[0], block.shape[1])
    shaped = block.reshape(rows // WIN_ROWS, WIN_ROWS, cols // WIN_COLS, WIN_COLS, -1)
    return shaped.transpose(0, 2, 1, 3, 4).reshape(-1, WIN_TOK, block.shape[2])

def from_windows(wins, rows, cols):
    shaped = wins.reshape(rows // WIN_ROWS, cols // WIN_COLS, WIN_ROWS, WIN_COLS, -1)
    return shaped.transpose(0, 2, 1, 3, 4).reshape(rows, cols, -1)

def window_attention(query, keys, vals, marks, position_bias):
    count = query.shape[0]
    query_h = query.reshape(count, WIN_TOK, HEADS, HEAD_DIM).astype(jnp.float32)
    keys_h = keys.reshape(count, WIN_TOK, HEADS, HEAD_DIM).astype(jnp.float32)
    vals_h = vals.reshape(count, WIN_TOK, HEADS, HEAD_DIM).astype(jnp.float32)
    scores = jnp.einsum('wqhd,wkhd->whqk', query_h, keys_h) * HEAD_DIM ** (-0.5)
    scores = scores + position_bias[None]
    same_region = marks[:, :, None] == marks[:, None, :]
    scores = jnp.where(same_region[:, None], scores, jnp.float32(-1e+30))
    largest = lax.optimization_barrier(jnp.max(scores, axis=-1, keepdims=True))
    expo = jnp.exp(scores - largest)
    probs = (expo / lax.optimization_barrier(jnp.sum(expo, axis=-1, keepdims=True))).astype(jnp.bfloat16)
    outputs = jnp.einsum('whqk,wkhd->wqhd', probs.astype(jnp.float32), vals_h)
    return outputs.reshape(count, WIN_TOK, D).astype(jnp.bfloat16)

def band_block(band, marks, w_qkv, w_proj, w_up, w_down, position_bias):
    rows, cols = (band.shape[0], band.shape[1])
    flat = band.reshape(-1, D)
    normed = layer_norm(flat)
    qkv = jnp.dot(normed, w_qkv, preferred_element_type=jnp.float32).astype(jnp.bfloat16)
    qkv_win = to_windows(qkv.reshape(rows, cols, 3 * D))
    mark_win = to_windows(marks[:, :, None])[:, :, 0]
    attended = window_attention(qkv_win[:, :, :D], qkv_win[:, :, D:2 * D], qkv_win[:, :, 2 * D:], mark_win, position_bias)
    attended = from_windows(attended, rows, cols).reshape(-1, D)
    mixed = (flat.astype(jnp.float32) + jnp.dot(attended, w_proj, preferred_element_type=jnp.float32)).astype(jnp.bfloat16)
    normed2 = layer_norm(mixed)
    hidden = jax.nn.gelu(jnp.dot(normed2, w_up, preferred_element_type=jnp.float32), approximate=True).astype(jnp.bfloat16)
    output = mixed.astype(jnp.float32) + jnp.dot(hidden, w_down, preferred_element_type=jnp.float32)
    return output.astype(jnp.bfloat16).reshape(rows, cols, D)

def reference(field, region, w_qkv, w_proj, w_up, w_down, position_bias):
    shifted = jnp.roll(field, (-SHIFT, -SHIFT), (0, 1))
    marks = jnp.roll(region, (-SHIFT, -SHIFT), (0, 1))
    bands = shifted.reshape(LAT_ROWS // WIN_ROWS, WIN_ROWS, LON_COLS, D)
    mark_bands = marks.reshape(LAT_ROWS // WIN_ROWS, WIN_ROWS, LON_COLS)

    def one_band(pair):
        return band_block(pair[0], pair[1], w_qkv, w_proj, w_up, w_down, position_bias)
    done = lax.map(one_band, (bands, mark_bands)).reshape(LAT_ROWS, LON_COLS, D)
    return jnp.roll(done, (SHIFT, SHIFT), (0, 1))
```

```python
import jax
import jax.numpy as jnp
from jax import lax
from jax.experimental import pallas as pl
from jax.experimental.pallas import tpu as pltpu
from jax.sharding import PartitionSpec as P

MESH = pl.DeviceIdType.MESH
D = 512
HEADS = 16
ROWS = 64
COLS = 18
PITCH = 24
ID_LANES = 128
LOG2E = 1.4426950408889634
ORDER = (5, 6, 7, 8, 0, 1, 2, 3, 4)
MAIN = (5, 6, 7, 8, 0, 1, 2, 3, 4, 9, 10, 11, 12, 13)
HALO_ROWS = 256
MAIN_ROWS = 112
WIN_PITCH = 80
F32 = jnp.float32
BF16 = jnp.bfloat16


def norm(x):
    center = jnp.mean(x, axis=-1, keepdims=True)
    moved = x - center
    spread = jnp.mean(moved * moved, axis=-1, keepdims=True)
    return (moved * lax.rsqrt(spread + 1e-05)).astype(BF16)


def gelu(x):
    inner = 0.7978845608028654 * (x + 0.044715 * (x * x * x))
    return 0.5 * x * (1.0 + jnp.tanh(inner))


def kernel(
    field_h, marks_h, wqkv_h, wproj_h, wup_h, wdown_h, bias_h, out_h,
    field_v, marks_v, e, x_s, id_s, n_s, qw, idw, att, wq_v, wp_v, wu, wd,
    braw, btmp, bias_v, bias_in, out_t, acc,
    col_out, row_out, cor_out, col_in, row_in, cor_in, ret_col, ret_row, ret_cor, out_v,
    local_sem, halo_send, halo_recv, ret_send, ret_recv, w_send, w_recv, sib_send, sib_recv,
):
    lon = lax.axis_index("lon")
    lat = lax.axis_index("lat")
    core = lax.rem(lon, 2)
    west, east = lax.rem(lon + 63, 64), lax.rem(lon + 1, 64)
    north, south = lax.rem(lat + 7, 8), lax.rem(lat + 1, 8)
    sibling = lon + 1 - 2 * core
    far = lax.rem(lon + 32, 64)
    up_lon = jnp.where(lat == 7, far, lon)
    down_lon = jnp.where(lat == 0, far, lon)
    z_up = (up_lon, south)
    z_down = (down_lon, north)
    sib = (sibling, lat)

    def local(src, dst, i):
        return pltpu.make_async_copy(src, dst, local_sem.at[i])

    def remote(src, dst, ssem, rsem, dev):
        return pltpu.make_async_remote_copy(
            src_ref=src, dst_ref=dst, send_sem=ssem, recv_sem=rsem, device_id=dev, device_id_type=MESH
        )

    loads = [
        local(field_h, field_v, 0),
        local(marks_h, marks_v, 1),
        local(bias_h, bias_in, 2),
        local(wqkv_h, wq_v, 3),
        local(wproj_h, wp_v, 4),
        local(wup_h, wu.at[0], 5),
        local(wdown_h, wd.at[0], 6),
    ]
    for c in loads:
        c.start()

    partners = [(west, lat), (east, lat), (lon, north), (lon, south), (west, north), (east, south), z_up, z_down]
    barrier = pltpu.get_barrier_semaphore()
    for dev in partners:
        pl.semaphore_signal(barrier, inc=1, device_id=dev, device_id_type=MESH)
    pl.semaphore_wait(barrier, 8)

    def up(slot):
        return wu.at[slot, pl.ds(pl.multiple_of(core * 256, 256), 256), :]

    def down(slot):
        return wd.at[slot, pl.ds(pl.multiple_of(core * 128, 128), 128), :]

    def up_own():
        return wup_h.at[pl.ds(pl.multiple_of(core * 256, 256), 256), :]

    def down_own():
        return wdown_h.at[pl.ds(pl.multiple_of(core * 128, 128), 128), :]

    def chain(t):
        found = []
        for way in (0, 1):
            dev = (z_up, z_down)[way]
            for kind in (0, 1):
                if t == 3 and kind != way:
                    continue
                view = (up, down)[kind]
                if t == 0:
                    src = (up_own, down_own)[kind]()
                else:
                    src = view(t + 3 * way)
                dst = view(7 if t == 3 else t + 1 + 3 * way)
                i = t * 4 + way * 2 + kind
                found.append(remote(src, dst, w_send.at[i], w_recv.at[i], dev))
        return found

    def sib_copy(slot, kind):
        view = (up, down)[kind](slot)
        i = (slot - 1) * 2 + kind
        return remote(view, view, sib_send.at[i], sib_recv.at[i], sib)

    def progress(t):
        if t > 0:
            for c in chain(t - 1):
                c.wait_recv()
        if t < 4:
            for c in chain(t):
                c.start()
        if t > 0:
            for slot in (t, t + 3) if t < 4 else (7,):
                for kind in (0, 1):
                    sib_copy(slot, kind).start()

    progress(0)
    loads[0].wait()
    loads[1].wait()

    def spread_row(r, carry):
        x = field_v[r].astype(F32)
        m = marks_v[r].astype(F32)
        at = pl.ds(pl.multiple_of((r + 4) * PITCH, 8), COLS)
        for t in range(4):
            e[t, at, :] = x[:, 128 * t : 128 * (t + 1)]
        e[4, at, :] = m
        return carry

    lax.fori_loop(0, ROWS, spread_row, 0, unroll=4)

    def token(row, col):
        at = pl.ds(row * PITCH + col, 8, stride=PITCH)
        return jnp.concatenate([e[t, at, :] for t in range(5)], axis=-1)

    sub8 = lax.broadcasted_iota(jnp.int32, (8, D + ID_LANES), 0)

    def pack_cols(b, carry):
        parts = [token(8 + 8 * b, c) for c in range(4)]
        col_out[pl.ds(pl.multiple_of(b * 32, 32), 32), :] = jnp.concatenate(parts, axis=0).astype(BF16)
        return carry

    lax.fori_loop(0, 8, pack_cols, 0)
    send_col = remote(col_out, col_in, halo_send.at[0], halo_recv.at[0], (west, lat))
    send_col.start()
    cor_out[...] = jnp.concatenate([token(0, c) for c in range(4)], axis=0).astype(BF16)
    send_cor = remote(cor_out, cor_in, halo_send.at[1], halo_recv.at[1], (west, north))
    send_cor.start()
    pairs = []
    for g in range(7):
        pairs.append(jnp.where(sub8 < 4, token(4, 4 + 2 * g), token(0, 5 + 2 * g)))
    pairs.append(jnp.zeros_like(pairs[0]))
    row_out[...] = jnp.concatenate(pairs, axis=0).astype(BF16)
    send_row = remote(row_out, row_in, halo_send.at[2], halo_recv.at[2], (lon, north))
    send_row.start()

    loads[2].wait()

    def turn_bias(h, carry):
        braw[:, 0:72] = bias_in[h]
        first = [braw[pl.ds(c, 8, stride=9), :] for c in ORDER]
        first.append(jnp.zeros((56, 128), F32))
        btmp[...] = jnp.concatenate(first, axis=0).T
        second = [btmp[pl.ds(c, 8, stride=9), :] for c in ORDER]
        second.append(jnp.zeros((56, 128), F32))
        turned = jnp.concatenate(second, axis=0).T
        bias_v[pl.ds(pl.multiple_of(h * 72, 8), 72), :] = turned[0:72] * LOG2E
        return carry

    braw[...] = jnp.zeros_like(braw)
    lax.fori_loop(0, HEADS, turn_bias, 0)

    def keep(rows_at, block):
        x_s[rows_at, :] = block[:, 0:D]
        id_s[rows_at, :] = block[:, D:]

    def main_at(m):
        return pl.multiple_of(HALO_ROWS + MAIN_ROWS * m, 16)

    def gather_band(b, carry):
        start = HALO_ROWS + MAIN_ROWS * (b + 1)
        for i in range(7):
            pair = [token(8 + 8 * b, 4 + MAIN[2 * i + j]) for j in (0, 1)]
            keep(pl.ds(pl.multiple_of(start + 16 * i, 16), 16), jnp.concatenate(pair, axis=0).astype(BF16))
        return carry

    lax.fori_loop(0, 7, gather_band, 0)

    loads[3].wait()

    def qkv_rows(at, size):
        x = x_s[pl.ds(at, size), :].astype(F32)
        return norm(x)

    def qkv_main(m, carry):
        at = main_at(m)
        b = lax.rem(m + 7, 8)
        normed = qkv_rows(at, MAIN_ROWS)
        base = pl.multiple_of(b * 2 * WIN_PITCH, 16)
        other = pl.multiple_of(b * 2 * WIN_PITCH + WIN_PITCH + 32, 16)
        fill = jnp.zeros((8, D), F32)
        for part in range(3):
            lanes = slice(part * D, (part + 1) * D)
            res = jnp.dot(normed, wq_v[:, lanes], preferred_element_type=F32)
            qw[pl.ds(base, 80), lanes] = jnp.concatenate([res[0:72], fill], axis=0).astype(BF16)
            qw[pl.ds(other, 48), lanes] = jnp.concatenate([res[72:112], fill], axis=0).astype(BF16)
        ids = id_s[pl.ds(at, MAIN_ROWS), :].astype(F32)
        fill = jnp.zeros((8, ID_LANES), F32)
        idw[pl.ds(base, 80), :] = jnp.concatenate([ids[0:72], fill], axis=0).astype(BF16)
        idw[pl.ds(other, 48), :] = jnp.concatenate([ids[72:112], fill], axis=0).astype(BF16)
        return carry

    lax.fori_loop(1, 8, qkv_main, 0)

    send_row.wait_recv()
    halo = row_in[...].astype(F32)
    ready = []
    for c in range(14):
        piece = halo[8 * (c // 2) : 8 * (c // 2) + 8]
        if c % 2 == 0:
            piece = jnp.concatenate([piece[4:8], piece[0:4]], axis=0)
        ready.append(jnp.where(sub8 < 4, token(64, 4 + c), piece))
    for i in range(7):
        pair = [ready[MAIN[2 * i + j]] for j in (0, 1)]
        keep(pl.ds(HALO_ROWS + 16 * i, 16), jnp.concatenate(pair, axis=0).astype(BF16))
    qkv_main(0, 0)

    send_col.wait_recv()
    send_cor.wait_recv()
    keep(pl.ds(0, 224), col_in[0:224, :])
    mine = col_in[224:256, :].astype(F32)
    corner = cor_in[...].astype(F32)
    sub32 = lax.rem(lax.broadcasted_iota(jnp.int32, (32, D + ID_LANES), 0), 8)
    keep(pl.ds(224, 32), jnp.where(sub32 < 4, mine, corner).astype(BF16))

    def qkv_halo(b, carry):
        at = pl.multiple_of(b * 64, 64)
        normed = qkv_rows(at, 64)
        for part in range(3):
            lanes = slice(part * D, (part + 1) * D)
            res = jnp.dot(normed, wq_v[:, lanes], preferred_element_type=F32).astype(BF16)
            for i in (0, 1):
                dst = pl.multiple_of((4 * b + 2 * i + 1) * WIN_PITCH, 16)
                qw[pl.ds(dst, 32), lanes] = res[32 * i : 32 * i + 32]
        for i in (0, 1):
            dst = pl.multiple_of((4 * b + 2 * i + 1) * WIN_PITCH, 16)
            idw[pl.ds(dst, 32), :] = id_s[pl.ds(pl.multiple_of(b * 64 + 32 * i, 32), 32), :]
        return carry

    lax.fori_loop(0, 4, qkv_halo, 0)

    lane256 = lax.broadcasted_iota(jnp.int32, (80, 256), 1)
    block_of = lax.rem(lane256, 128) // 32
    low = lane256 < 128
    zero80 = jnp.zeros((80, 256), BF16)
    zero48 = jnp.zeros((48, 256), BF16)
    block72 = block_of[0:72]
    scale = LOG2E * 32 ** (-0.5)

    def blocks(v):
        return jnp.concatenate([jnp.where(low, v, zero80), zero48, jnp.where(low, zero80, v), zero48], axis=0)

    def window(w):
        at = pl.ds(pl.multiple_of(w * WIN_PITCH, 16), WIN_PITCH)
        ids = idw[at, :]
        wide = jnp.concatenate([ids, jnp.zeros((48, ID_LANES), BF16)], axis=0)
        same = lax.dot_general(ids, wide, (((1,), (1,)), ((), ())), preferred_element_type=F32)
        shut = (same[0:72] - 1.0) * 1e30
        halves = []
        for g in range(2):
            lanes = slice(256 * g, 256 * (g + 1))
            qg = qw[at, 256 * g : 256 * g + 256]
            kg = qw[at, D + 256 * g : D + 256 * g + 256]
            vg = qw[at, 2 * D + 256 * g : 2 * D + 256 * g + 256]
            qb = jnp.concatenate([jnp.where(block_of == j, qg, zero80) for j in range(4)], axis=0)
            scores = lax.dot_general(qb, blocks(kg), (((1,), (1,)), ((), ())), preferred_element_type=F32)
            rows = []
            for j in range(4):
                sides = []
                for t in range(2):
                    head = 8 * g + 4 * t + j
                    s = scores[80 * j : 80 * j + 72, 128 * t : 128 * t + 128] * scale
                    s = s + bias_v[72 * head : 72 * head + 72, :] + shut
                    ex = jnp.exp2(s - jnp.max(s, axis=-1, keepdims=True))
                    sides.append(ex * (1.0 / jnp.sum(ex, axis=-1, keepdims=True)))
                rows.append(jnp.concatenate(sides, axis=-1))
                rows.append(jnp.zeros((8, 256), F32))
            probs = jnp.concatenate(rows, axis=0).astype(BF16)
            res = jnp.dot(probs, blocks(vg), preferred_element_type=F32)
            o = res[0:72]
            for j in range(1, 4):
                o = jnp.where(block72 == j, res[80 * j : 80 * j + 72], o)
            halves.append(o)
        return jnp.concatenate(halves, axis=-1)

    def attend_band(b, carry):
        first = window(2 * b)
        second = window(2 * b + 1)
        m = lax.rem(b + 1, 8)
        att[pl.ds(pl.multiple_of(b * 32, 32), 32), :] = second[0:32].astype(BF16)
        att[pl.ds(main_at(m), MAIN_ROWS), :] = jnp.concatenate([first, second[32:72]], axis=0).astype(BF16)
        for t in range(1, 5):
            @pl.when(b == 2 * t - 2)
            def _():
                progress(t)
        return carry

    lax.fori_loop(0, 8, attend_band, 0)

    for slot in range(1, 8):
        for kind in (0, 1):
            sib_copy(slot, kind).wait_recv()
    loads[4].wait()
    loads[5].wait()
    loads[6].wait()

    def mlp(start, size):
        at = pl.ds(start, size)
        mixed = x_s[at, :].astype(F32) + jnp.dot(att[at, :], wp_v[...], preferred_element_type=F32)
        mixed = mixed.astype(BF16).astype(F32)
        acc[0:size, :] = mixed
        n_s[0:size, :] = norm(mixed)

        def hidden(s, carry):
            h = gelu(jnp.dot(n_s[0:size, :], wu[s], preferred_element_type=F32)).astype(BF16)
            acc[0:size, :] += jnp.dot(h, wd[s], preferred_element_type=F32)
            return carry

        lax.fori_loop(0, 8, hidden, 0)
        out_t[at, :] = acc[0:size, :].astype(BF16)

    mlp(0, 368)
    backs = [
        remote(out_t.at[pl.ds(0, 256), :], ret_col, ret_send.at[0], ret_recv.at[0], (east, lat)),
        remote(out_t.at[pl.ds(224, 32), :], ret_cor, ret_send.at[1], ret_recv.at[1], (east, south)),
        remote(out_t.at[pl.ds(256, 112), :], ret_row, ret_send.at[2], ret_recv.at[2], (lon, south)),
    ]
    for c in backs:
        c.start()
    mlp(368, 400)
    mlp(768, 384)

    def put(row, col, block):
        at = pl.ds(row * PITCH + col, 8, stride=PITCH)
        for t in range(4):
            e[t, at, :] = block[:, 128 * t : 128 * (t + 1)]

    backs[1].wait_recv()
    backs[2].wait_recv()
    north_rows = ret_row[...].astype(F32)
    for i in range(14):
        put(0, 4 + MAIN[i], north_rows[8 * i : 8 * i + 8])
    north_cor = ret_cor[...].astype(F32)
    for i in range(4):
        put(0, i, north_cor[8 * i : 8 * i + 8])

    def put_main(b, carry):
        block = out_t[pl.ds(main_at(lax.rem(b + 1, 8)), MAIN_ROWS), :].astype(F32)
        for i in range(14):
            put(8 + 8 * b, 4 + MAIN[i], block[8 * i : 8 * i + 8])
        return carry

    lax.fori_loop(0, 8, put_main, 0)
    backs[0].wait_recv()

    def put_halo(b, carry):
        block = ret_col[pl.ds(pl.multiple_of(b * 32, 32), 32), :].astype(F32)
        for i in range(4):
            put(8 + 8 * b, i, block[8 * i : 8 * i + 8])
        return carry

    lax.fori_loop(0, 8, put_halo, 0)

    def finish_row(r, carry):
        at = pl.ds(pl.multiple_of((r + 4) * PITCH, 8), COLS)
        out_v[r] = jnp.concatenate([e[t, at, :] for t in range(4)], axis=-1).astype(BF16)
        return carry

    lax.fori_loop(0, ROWS, finish_row, 0, unroll=4)
    store = local(out_v, out_h, 7)
    store.start()
    store.wait()

    for t in range(4):
        for c in chain(t):
            c.wait_send()
    for slot in range(1, 8):
        for kind in (0, 1):
            sib_copy(slot, kind).wait_send()
    for c in (send_col, send_cor, send_row, *backs):
        c.wait_send()


def block(field, region, w_qkv, w_proj, w_up, w_down, position_bias):
    lanes = lax.broadcasted_iota(jnp.int32, (ROWS, COLS, ID_LANES), 2)
    marks = (region[:, :, None] == lanes).astype(BF16)
    wide = D + ID_LANES
    vm = pltpu.VMEM
    scratch = [
        vm((ROWS, COLS, D), BF16),
        vm((ROWS, COLS, ID_LANES), BF16),
        vm((5, 72 * PITCH, 128), F32),
        vm((1152, D), BF16),
        vm((1152, ID_LANES), BF16),
        vm((400, D), BF16),
        vm((16 * WIN_PITCH, 3 * D), BF16),
        vm((16 * WIN_PITCH, ID_LANES), BF16),
        vm((1152, D), BF16),
        vm((D, 3 * D), BF16),
        vm((D, D), BF16),
        vm((8, D, 256), BF16),
        vm((8, 256, D), BF16),
        vm((72, 128), F32),
        vm((128, 128), F32),
        vm((HEADS * 72, 128), F32),
        vm((HEADS, 72, 72), F32),
        vm((1152, D), BF16),
        vm((400, D), F32),
        vm((256, wide), BF16),
        vm((64, wide), BF16),
        vm((32, wide), BF16),
        vm((256, wide), BF16),
        vm((64, wide), BF16),
        vm((32, wide), BF16),
        vm((256, D), BF16),
        vm((112, D), BF16),
        vm((32, D), BF16),
        vm((ROWS, COLS, D), BF16),
        pltpu.SemaphoreType.DMA((8,)),
        pltpu.SemaphoreType.DMA((3,)),
        pltpu.SemaphoreType.DMA((3,)),
        pltpu.SemaphoreType.DMA((3,)),
        pltpu.SemaphoreType.DMA((3,)),
        pltpu.SemaphoreType.DMA((16,)),
        pltpu.SemaphoreType.DMA((16,)),
        pltpu.SemaphoreType.DMA((14,)),
        pltpu.SemaphoreType.DMA((14,)),
    ]
    return pl.pallas_call(
        kernel,
        out_shape=jax.ShapeDtypeStruct((ROWS, COLS, D), BF16),
        in_specs=[pl.BlockSpec(memory_space=pl.ANY)] * 7,
        out_specs=pl.BlockSpec(memory_space=pl.ANY),
        scratch_shapes=scratch,
        compiler_params=pltpu.CompilerParams(
            collective_id=0, has_side_effects=True, vmem_limit_bytes=58 * 1024 * 1024
        ),
    )(field, marks, w_qkv, w_proj, w_up, w_down, position_bias)


def solution(mesh):
    placed = (P("lat", "lon", None), P("lat", "lon"), P(), P(), P(None, "lat"), P("lat", None), P())
    return jax.shard_map(
        block, mesh=mesh, in_specs=placed, out_specs=P("lat", "lon", None), check_vma=False
    )
```

```python
import jax
import jax.numpy as jnp
from jax import lax
from jax.experimental import pallas as pl
from jax.experimental.pallas import tpu as pltpu
from jax.sharding import PartitionSpec as P

MESH = pl.DeviceIdType.MESH
D = 512
HEADS = 16
ROWS = 64
COLS = 18
LOG2E = 1.4426950408889634
ORDER = (5, 6, 7, 8, 0, 1, 2, 3, 4)
PAIRS = ((5, 6), (7, 8), (0, 1), (2, 3), (4, 13), (9, 10), (11, 12))
LAST = (5, 6, 7, 8, 0, 1, 2, 3, 4, 9, 10, 11, 12, 13)
LAST_AT = 256
PAIR_AT = 368
PAIR_ROWS = 112
WIN_PITCH = 80
F32 = jnp.float32
BF16 = jnp.bfloat16
NT = (((1,), (1,)), ((), ()))


def norm(x):
    center = jnp.mean(x, axis=-1, keepdims=True)
    moved = x - center
    spread = jnp.mean(moved * moved, axis=-1, keepdims=True)
    return (moved * lax.rsqrt(spread + 1e-05)).astype(BF16)


def gelu(x):
    inner = 0.7978845608028654 * (x + 0.044715 * (x * x * x))
    return 0.5 * x * (1.0 + jnp.tanh(inner))


def swap4(x):
    return jnp.concatenate([x[4:8], x[0:4]], axis=0)


def kernel(
    field_h, region_h, wqkv_h, wproj_h, wup_h, wdown_h, bias_h, out_h,
    field_v, region_v, x_s, n_s, qw, idw, att, wq_v, wp_v, wu, wd,
    braw, btmp, bias_v, bias_in, out_t, acc, hot,
    reg_out, reg_e, reg_s, reg_se, row_out, col_in, row_in, cor_in,
    back_row, back_cor, ret_col, ret_row, ret_cor, out_v,
    local_sem, out_sem, halo_send, halo_recv, ret_send, ret_recv, w_send, w_recv, sib_send, sib_recv,
):
    lon = lax.axis_index("lon")
    lat = lax.axis_index("lat")
    core = lax.rem(lon, 2)
    west, east = lax.rem(lon + 63, 64), lax.rem(lon + 1, 64)
    north, south = lax.rem(lat + 7, 8), lax.rem(lat + 1, 8)
    sibling = lon + 1 - 2 * core
    far = lax.rem(lon + 32, 64)
    z_up = (jnp.where(lat == 7, far, lon), south)
    z_down = (jnp.where(lat == 0, far, lon), north)
    sib = (sibling, lat)

    def local(src, dst, i):
        return pltpu.make_async_copy(src, dst, local_sem.at[i])

    def remote(src, dst, ssem, rsem, dev):
        return pltpu.make_async_remote_copy(
            src_ref=src, dst_ref=dst, send_sem=ssem, recv_sem=rsem, device_id=dev, device_id_type=MESH
        )

    loads = [
        local(field_h, field_v, 0),
        local(region_h, region_v, 1),
        local(bias_h, bias_in, 2),
        local(wqkv_h, wq_v, 3),
        local(wproj_h, wp_v, 4),
        local(wup_h, wu.at[0], 5),
        local(wdown_h, wd.at[0], 6),
    ]
    for c in loads:
        c.start()

    partners = [(west, lat), (east, lat), (lon, north), (lon, south), (west, north), (east, south), z_up, z_down]
    barrier = pltpu.get_barrier_semaphore()
    for dev in partners:
        pl.semaphore_signal(barrier, inc=1, device_id=dev, device_id_type=MESH)
    pl.semaphore_wait(barrier, 8)

    def up(slot):
        return wu.at[slot, pl.ds(pl.multiple_of(core * 256, 256), 256), :]

    def down(slot):
        return wd.at[slot, pl.ds(pl.multiple_of(core * 128, 128), 128), :]

    def up_own():
        return wup_h.at[pl.ds(pl.multiple_of(core * 256, 256), 256), :]

    def down_own():
        return wdown_h.at[pl.ds(pl.multiple_of(core * 128, 128), 128), :]

    def chain(t):
        found = []
        for way in (0, 1):
            dev = (z_up, z_down)[way]
            for kind in (0, 1):
                if t == 3 and kind != way:
                    continue
                view = (up, down)[kind]
                if t == 0:
                    src = (up_own, down_own)[kind]()
                else:
                    src = view(t + 3 * way)
                dst = view(7 if t == 3 else t + 1 + 3 * way)
                i = t * 4 + way * 2 + kind
                found.append(remote(src, dst, w_send.at[i], w_recv.at[i], dev))
        return found

    def sib_copy(slot, kind):
        view = (up, down)[kind](slot)
        i = (slot - 1) * 2 + kind
        return remote(view, view, sib_send.at[i], sib_recv.at[i], sib)

    def progress(t):
        if t > 0:
            for c in chain(t - 1):
                c.wait_recv()
        if t < 4:
            for c in chain(t):
                c.start()
        if t > 0:
            for slot in (t, t + 3) if t < 4 else (7,):
                for kind in (0, 1):
                    sib_copy(slot, kind).start()

    send_col = remote(field_h.at[pl.ds(0, 4)], col_in, halo_send.at[0], halo_recv.at[0], (west, lat))
    send_row = remote(row_out.at[pl.ds(16, 64), :], row_in, halo_send.at[1], halo_recv.at[1], (lon, north))
    send_cor = remote(row_out.at[pl.ds(0, 16), :], cor_in, halo_send.at[2], halo_recv.at[2], (west, north))
    send_ids = [
        remote(reg_out, reg_e, halo_send.at[3], halo_recv.at[3], (west, lat)),
        remote(reg_out, reg_s, halo_send.at[4], halo_recv.at[4], (lon, north)),
        remote(reg_out, reg_se, halo_send.at[5], halo_recv.at[5], (west, north)),
    ]
    sub8 = lax.broadcasted_iota(jnp.int32, (8, D), 0)

    def send_halos():
        send_col.start()
        loads[1].wait()
        reg_out[...] = jnp.zeros_like(reg_out)
        reg_out[0:18, 0:64] = region_v[...]
        for c in send_ids:
            c.start()
        loads[0].wait()
        tops = [field_v[c, 0:16, :].astype(F32)[0:8] for c in range(COLS)]
        packed = [jnp.where(sub8 < 4, tops[2 * i], swap4(tops[2 * i + 1])) for i in range(9)]
        packed.append(jnp.zeros_like(packed[0]))
        row_out[...] = jnp.concatenate(packed, axis=0).astype(BF16)
        send_row.start()
        send_cor.start()

    def turn_biases():
        loads[2].wait()
        braw[...] = jnp.zeros_like(braw)

        def turn_bias(h, carry):
            braw[:, 0:72] = bias_in[h]
            first = [braw[pl.ds(c, 8, stride=9), :] for c in ORDER]
            first.append(jnp.zeros((56, 128), F32))
            btmp[...] = jnp.concatenate(first, axis=0).T
            second = [btmp[pl.ds(c, 8, stride=9), :] for c in ORDER]
            second.append(jnp.zeros((56, 128), F32))
            turned = jnp.concatenate(second, axis=0).T
            bias_v[pl.ds(pl.multiple_of(h * 72, 8), 72), :] = turned[0:72] * LOG2E
            return carry

        lax.fori_loop(0, HEADS, turn_bias, 0)

    lane24 = lax.broadcasted_iota(jnp.int32, (24, 128), 1)
    lane64 = lax.broadcasted_iota(jnp.int32, (64, 128), 1)

    def id_rows(here, below):
        moved = jnp.where(lane24 < 60, pltpu.roll(here, 124, 1), pltpu.roll(below, 60, 1))
        tall = jnp.concatenate([moved, jnp.zeros((104, 128), F32)], axis=0)
        return tall.T[0:64]

    def hot_col(table, c):
        wide = jnp.broadcast_to(table[:, c : c + 1], (64, 128))
        return (wide == lane64.astype(F32)).astype(F32)

    def put_ids(s, pos, top, low, bands):
        for b in bands:
            rows = [top[8 * b : 8 * b + 8], low[8 * b : 8 * b + 8]]
            idw[pl.ds((2 * b + s) * WIN_PITCH + 16 * pos, 16), :] = jnp.concatenate(rows, axis=0).astype(BF16)

    def main_ids(below, bands):
        table = id_rows(reg_out[...].astype(F32), below)
        zero = jnp.zeros((64, 128), F32)
        for i, (a, z) in enumerate(PAIRS):
            first, second = hot_col(table, a + 4), hot_col(table, z + 4)
            if i < 4:
                put_ids(0, i, first, second, bands)
            elif i == 4:
                put_ids(0, 4, first, zero, bands)
                put_ids(1, 4, second, zero, bands)
            else:
                put_ids(1, i - 3, first, second, bands)

    def halo_ids():
        table = id_rows(reg_e[...].astype(F32), reg_se[...].astype(F32))
        for i in (0, 1):
            put_ids(1, i, hot_col(table, 2 * i), hot_col(table, 2 * i + 1), range(8))

    def gather_main():
        for i, pair in enumerate(PAIRS):
            rows = [field_v[c + 4].astype(F32)[4:60] for c in pair]
            block = jnp.concatenate(rows, axis=0)
            at = pl.ds(PAIR_AT + PAIR_ROWS * i, PAIR_ROWS)
            x_s[at, :] = block.astype(BF16)
            n_s[at, :] = norm(block)

    def scatter(part, i, res):
        lanes = part
        for b in range(7):
            first, second = res[8 * b : 8 * b + 8], res[56 + 8 * b : 64 + 8 * b]
            if i == 4:
                fill = jnp.zeros_like(first)
                for s, piece in ((0, first), (1, second)):
                    both = jnp.concatenate([piece, fill], axis=0).astype(BF16)
                    qw[pl.ds((2 * b + s) * WIN_PITCH + 64, 16), lanes] = both
            else:
                s, pos = (0, i) if i < 4 else (1, i - 3)
                both = jnp.concatenate([first, second], axis=0).astype(BF16)
                qw[pl.ds((2 * b + s) * WIN_PITCH + 16 * pos, 16), lanes] = both

    def qkv_main():
        loads[3].wait()

        def step(n, carry):
            lanes = pl.ds(pl.multiple_of(n * 256, 256), 256)
            res = jnp.dot(n_s[pl.ds(PAIR_AT, 784), :], wq_v[:, lanes], preferred_element_type=F32)
            for i in range(7):
                scatter(lanes, i, res[PAIR_ROWS * i : PAIR_ROWS * (i + 1)])
            return carry

        lax.fori_loop(0, 6, step, 0)

    def gather_halo():
        send_row.wait_recv()
        below = row_in[...].astype(F32)
        ready = {}
        for c in range(14):
            piece = below[8 * (c // 2) : 8 * (c // 2) + 8]
            if c % 2 == 0:
                piece = swap4(piece)
            mine = swap4(field_v[c + 4, 48:64, :].astype(F32)[8:16])
            ready[c] = jnp.where(sub8 < 4, mine, piece)
        block = jnp.concatenate([ready[c] for c in LAST], axis=0)
        at = pl.ds(LAST_AT, PAIR_ROWS)
        x_s[at, :] = block.astype(BF16)
        n_s[at, :] = norm(block)
        send_cor.wait_recv()
        corner = cor_in[...].astype(F32)
        send_col.wait_recv()
        for c in range(4):
            piece = corner[8 * (c // 2) : 8 * (c // 2) + 8]
            piece = piece[0:4] if c % 2 == 0 else piece[4:8]
            block = jnp.concatenate([col_in[c].astype(F32)[4:64], piece], axis=0)
            at = pl.ds(64 * c, 64)
            x_s[at, :] = block.astype(BF16)
            n_s[at, :] = norm(block)

    def qkv_halo():
        def step(n, carry):
            lanes = pl.ds(pl.multiple_of(n * 256, 256), 256)
            res = jnp.dot(n_s[pl.ds(0, PAIR_AT), :], wq_v[:, lanes], preferred_element_type=F32)
            for i in range(2):
                for b in range(8):
                    both = [res[64 * (2 * i + j) + 8 * b : 64 * (2 * i + j) + 8 * b + 8] for j in (0, 1)]
                    at = pl.ds((2 * b + 1) * WIN_PITCH + 16 * i, 16)
                    qw[at, lanes] = jnp.concatenate(both, axis=0).astype(BF16)
            last = res[LAST_AT:PAIR_AT]
            fill = jnp.zeros((8, 256), F32)
            qw[pl.ds(14 * WIN_PITCH, 80), lanes] = jnp.concatenate([last[0:72], fill], axis=0).astype(BF16)
            tail = [last[72:104], last[104:112], fill]
            qw[pl.ds(15 * WIN_PITCH + 32, 48), lanes] = jnp.concatenate(tail, axis=0).astype(BF16)
            return carry

        lax.fori_loop(0, 6, step, 0)

    lane256 = lax.broadcasted_iota(jnp.int32, (80, 256), 1)
    block_of = lax.rem(lane256, 128) // 32
    low = lane256 < 128
    zero80 = jnp.zeros((80, 256), BF16)
    zero48 = jnp.zeros((48, 256), BF16)
    block72 = block_of[0:72]
    scale = LOG2E * 32 ** (-0.5)

    def blocks(v):
        return jnp.concatenate([jnp.where(low, v, zero80), zero48, jnp.where(low, zero80, v), zero48], axis=0)

    def window(w):
        at = pl.ds(pl.multiple_of(w * WIN_PITCH, 16), WIN_PITCH)
        ids = idw[at, :]
        wide = jnp.concatenate([ids, jnp.zeros((48, 128), BF16)], axis=0)
        same = lax.dot_general(ids, wide, NT, preferred_element_type=F32)
        shut = (same[0:72] - 1.0) * 1e30
        halves = []
        for g in range(2):
            qg = qw[at, 256 * g : 256 * g + 256]
            kg = qw[at, D + 256 * g : D + 256 * g + 256]
            vg = qw[at, 2 * D + 256 * g : 2 * D + 256 * g + 256]
            qb = jnp.concatenate([jnp.where(block_of == j, qg, zero80) for j in range(4)], axis=0)
            scores = lax.dot_general(qb, blocks(kg), NT, preferred_element_type=F32)
            rows = []
            for j in range(4):
                sides = []
                for t in range(2):
                    head = 8 * g + 4 * t + j
                    s = scores[80 * j : 80 * j + 72, 128 * t : 128 * t + 128] * scale
                    s = s + bias_v[72 * head : 72 * head + 72, :] + shut
                    ex = jnp.exp2(s - jnp.max(s, axis=-1, keepdims=True))
                    sides.append(ex * (1.0 / jnp.sum(ex, axis=-1, keepdims=True)))
                rows.append(jnp.concatenate(sides, axis=-1))
                rows.append(jnp.zeros((8, 256), F32))
            probs = jnp.concatenate(rows, axis=0).astype(BF16)
            res = jnp.dot(probs, blocks(vg), preferred_element_type=F32)
            o = res[0:72]
            for j in range(1, 4):
                o = jnp.where(block72 == j, res[80 * j : 80 * j + 72], o)
            halves.append(o)
        return jnp.concatenate(halves, axis=-1)

    def attend_band(b, carry):
        att[pl.ds(pl.multiple_of(2 * b * WIN_PITCH, 16), 72), :] = window(2 * b)
        att[pl.ds(pl.multiple_of(2 * b * WIN_PITCH + WIN_PITCH, 16), 72), :] = window(2 * b + 1)
        for t in range(1, 5):
            @pl.when(b == 2 * t - 2)
            def _():
                progress(t)
        return carry

    def attention():
        lax.fori_loop(0, 8, attend_band, 0)

    def attended(w, pos):
        return att[w * WIN_PITCH + 8 * pos : w * WIN_PITCH + 8 * pos + 8, :]

    def order_attended():
        for c in range(4):
            block = [attended(2 * b + 1, c) for b in range(8)]
            n_s[64 * c : 64 * c + 64, :] = jnp.concatenate(block, axis=0).astype(BF16)
        block = [att[14 * WIN_PITCH : 14 * WIN_PITCH + 72, :], att[15 * WIN_PITCH + 32 : 15 * WIN_PITCH + 72, :]]
        n_s[LAST_AT:PAIR_AT, :] = jnp.concatenate(block, axis=0).astype(BF16)
        for i, pair in enumerate(PAIRS):
            block = []
            for j in (0, 1):
                s, pos = (0, 2 * i + j) if i < 4 else (1, 2 * (i - 3) + j)
                if i == 4:
                    s, pos = j, 8
                block += [attended(2 * b + s, pos) for b in range(7)]
            n_s[PAIR_AT + 112 * i : PAIR_AT + 112 * i + 112, :] = jnp.concatenate(block, axis=0).astype(BF16)

    def await_weights():
        for slot in range(1, 8):
            for kind in (0, 1):
                sib_copy(slot, kind).wait_recv()
        for c in loads[4:7]:
            c.wait()

    def mlp(start, size):
        at = pl.ds(start, size)
        mixed = x_s[at, :].astype(F32) + jnp.dot(n_s[at, :], wp_v[...], preferred_element_type=F32)
        mixed = mixed.astype(BF16).astype(F32)
        acc[0:size, :] = mixed
        n_s[at, :] = norm(mixed)

        def hidden(s, carry):
            h = gelu(jnp.dot(n_s[at, :], wu[s], preferred_element_type=F32)).astype(BF16)
            acc[0:size, :] += jnp.dot(h, wd[s], preferred_element_type=F32)
            return carry

        lax.fori_loop(0, 8, hidden, 0)
        out_t[at, :] = acc[0:size, :].astype(BF16)

    backs = [
        remote(out_t.at[pl.ds(0, 256), :], ret_col, ret_send.at[0], ret_recv.at[0], (east, lat)),
        remote(back_cor, ret_cor, ret_send.at[1], ret_recv.at[1], (east, south)),
        remote(back_row, ret_row, ret_send.at[2], ret_recv.at[2], (lon, south)),
    ]

    def send_back():
        backs[0].start()
        ends = [out_t[64 * c + 48 : 64 * c + 64, :].astype(F32)[8:16] for c in range(4)]
        packed = [jnp.where(sub8 < 4, swap4(ends[2 * i]), ends[2 * i + 1]) for i in range(2)]
        back_cor[...] = jnp.concatenate(packed, axis=0).astype(BF16)
        backs[1].start()
        last = out_t[LAST_AT:PAIR_AT, :].astype(F32)
        packed = []
        for i in range(7):
            packed.append(jnp.where(sub8 < 4, swap4(last[16 * i : 16 * i + 8]), last[16 * i + 8 : 16 * i + 16]))
        packed.append(jnp.zeros_like(packed[0]))
        back_row[...] = jnp.concatenate(packed, axis=0).astype(BF16)
        backs[2].start()

    stores = []

    def store_col(c):
        found = pltpu.make_async_copy(out_v.at[c], out_h.at[c], out_sem.at[c])
        found.start()
        stores.append(found)

    def head4(packed, i):
        piece = packed[8 * (i // 2) : 8 * (i // 2) + 8]
        return piece[0:4] if i % 2 == 0 else piece[4:8]

    def finish_main():
        backs[2].wait_recv()
        above = ret_row[...].astype(F32)
        last = out_t[LAST_AT:PAIR_AT, :].astype(F32)
        for i, pair in enumerate(PAIRS):
            block = out_t[PAIR_AT + 112 * i : PAIR_AT + 112 * i + 112, :].astype(F32)
            for j, c in enumerate(pair):
                k = LAST.index(c)
                parts = [head4(above, k), block[56 * j : 56 * j + 56], last[8 * k : 8 * k + 4]]
                out_v[c + 4] = jnp.concatenate(parts, axis=0).astype(BF16)
                store_col(c + 4)

    def finish_halo():
        backs[1].wait_recv()
        above = ret_cor[...].astype(F32)
        backs[0].wait_recv()
        for c in range(4):
            block = ret_col[64 * c : 64 * c + 64, :].astype(F32)
            out_v[c] = jnp.concatenate([head4(above, c), block[0:60]], axis=0).astype(BF16)
            store_col(c)

    def send_ids_done():
        for c in send_ids:
            c.wait_recv()

    send_halos()
    progress(0)
    turn_biases()
    main_ids(jnp.zeros((24, 128), F32), range(7))
    gather_main()
    qkv_main()
    send_ids_done()
    main_ids(reg_s[...].astype(F32), range(7, 8))
    halo_ids()
    gather_halo()
    qkv_halo()
    attention()
    order_attended()
    await_weights()
    mlp(0, 368)
    send_back()
    mlp(368, 400)
    mlp(768, 384)
    finish_main()
    finish_halo()

    for c in stores:
        c.wait()
    for t in range(4):
        for c in chain(t):
            c.wait_send()
    for slot in range(1, 8):
        for kind in (0, 1):
            sib_copy(slot, kind).wait_send()
    for c in (send_col, send_cor, send_row, *send_ids, *backs):
        c.wait_send()


def block(field, region, w_qkv, w_proj, w_up, w_down, position_bias):
    vm = pltpu.VMEM
    dma = pltpu.SemaphoreType.DMA
    scratch = [
        vm((COLS, ROWS, D), BF16),
        vm((COLS, ROWS), jnp.int32),
        vm((1152, D), BF16),
        vm((1152, D), BF16),
        vm((16 * WIN_PITCH, 3 * D), BF16),
        vm((16 * WIN_PITCH, 128), BF16),
        vm((16 * WIN_PITCH, D), F32),
        vm((D, 3 * D), BF16),
        vm((D, D), BF16),
        vm((8, D, 256), BF16),
        vm((8, 256, D), BF16),
        vm((72, 128), F32),
        vm((128, 128), F32),
        vm((HEADS * 72, 128), F32),
        vm((HEADS, 72, 72), F32),
        vm((1152, D), BF16),
        vm((784, D), F32),
        vm((8, 128), F32),
        vm((24, 128), jnp.int32),
        vm((24, 128), jnp.int32),
        vm((24, 128), jnp.int32),
        vm((24, 128), jnp.int32),
        vm((80, D), BF16),
        vm((4, ROWS, D), BF16),
        vm((64, D), BF16),
        vm((16, D), BF16),
        vm((64, D), BF16),
        vm((16, D), BF16),
        vm((256, D), BF16),
        vm((64, D), BF16),
        vm((16, D), BF16),
        vm((COLS, ROWS, D), BF16),
        dma((8,)),
        dma((COLS,)),
        dma((6,)),
        dma((6,)),
        dma((3,)),
        dma((3,)),
        dma((16,)),
        dma((16,)),
        dma((14,)),
        dma((14,)),
    ]
    done = pl.pallas_call(
        kernel,
        out_shape=jax.ShapeDtypeStruct((COLS, ROWS, D), BF16),
        in_specs=[pl.BlockSpec(memory_space=pl.ANY)] * 7,
        out_specs=pl.BlockSpec(memory_space=pl.ANY),
        scratch_shapes=scratch,
        compiler_params=pltpu.CompilerParams(
            collective_id=0, has_side_effects=True, vmem_limit_bytes=58 * 1024 * 1024
        ),
    )(field.transpose(1, 0, 2), region.T, w_qkv, w_proj, w_up, w_down, position_bias)
    return done.transpose(1, 0, 2)


def solution(mesh):
    placed = (P("lat", "lon", None), P("lat", "lon"), P(), P(), P(None, "lat"), P("lat", None), P())
    return jax.shard_map(
        block, mesh=mesh, in_specs=placed, out_specs=P("lat", "lon", None), check_vma=False
    )
```

```python
import jax
import jax.numpy as jnp
from jax import lax
from jax.experimental import pallas as pl
from jax.experimental.pallas import tpu as pltpu
from jax.sharding import PartitionSpec as P

MESH = pl.DeviceIdType.MESH
D = 512
HEADS = 16
ROWS = 64
COLS = 18
LOG2E = 1.4426950408889634
ORDER = (5, 6, 7, 8, 0, 1, 2, 3, 4)
PAIRS = ((5, 6), (7, 8), (0, 1), (2, 3), (4, 13), (9, 10), (11, 12))
LAST = (5, 6, 7, 8, 0, 1, 2, 3, 4, 9, 10, 11, 12, 13)
LAST_AT = 256
PAIR_AT = 368
PAIR_ROWS = 112
WIN_PITCH = 80
F32 = jnp.float32
BF16 = jnp.bfloat16
NT = (((1,), (1,)), ((), ()))


def norm(x):
    center = jnp.mean(x, axis=-1, keepdims=True)
    moved = x - center
    spread = jnp.mean(moved * moved, axis=-1, keepdims=True)
    return (moved * lax.rsqrt(spread + 1e-05)).astype(BF16)


def gelu(x):
    half = 0.5 * x
    return half + half * jnp.tanh(x * (0.7978845608028654 + 0.0356774081363001 * (x * x)))


def swap4(x):
    return jnp.concatenate([x[4:8], x[0:4]], axis=0)


def kernel(
    field_h, region_h, wqkv_h, wproj_h, wup_h, wdown_h, bias_h, out_h,
    field_v, region_v, x_s, n_s, qw, idw, att, wq_v, wp_v, wu, wd,
    braw, btmp, bias_v, bias_in, out_t, acc, hid, rel_in, rel_back,
    reg_out, reg_e, reg_s, reg_se, row_out, col_in, row_in, cor_in,
    back_row, back_cor, ret_col, ret_row, ret_cor, out_v,
    local_sem, out_sem, halo_send, halo_recv, ret_send, ret_recv, z_send, z_recv, xy_send, xy_recv,
    sib_send, sib_recv, rel_send, rel_recv,
):
    lon = lax.axis_index("lon")
    lat = lax.axis_index("lat")
    core = lax.rem(lon, 2)
    z_hi = lon // 32
    x, y = lax.rem(lon // 8, 4), lax.rem(lon // 2, 4)
    west, east = lax.rem(lon + 63, 64), lax.rem(lon + 1, 64)
    north, south = lax.rem(lat + 7, 8), lax.rem(lat + 1, 8)
    half = z_hi * 32
    other = 32 - half
    is_first = lax.rem(lon, 32) == 0
    is_last = lax.rem(lon, 32) == 31
    chip = lax.rem(lon, 32) // 2
    sib = (lon + 1 - 2 * core, lat)

    def along_z(steps):
        to = lat + steps + 16
        return (lax.rem(z_hi + to // 8, 2) * 32 + lax.rem(lon, 32), lax.rem(to, 8))

    def in_plane(to_x, to_y):
        return (half + lax.rem(to_x, 4) * 8 + lax.rem(to_y, 4) * 2 + core, lat)

    z_to = [along_z(steps) for steps in (1, -1, 2, -2, 3, -3, 4, -4)]
    x_to = [in_plane(x + steps, y) for steps in (1, 3, 2)]
    y_to = [in_plane(x, y + steps) for steps in (1, 3, 2)]

    def local(src, dst, i):
        return pltpu.make_async_copy(src, dst, local_sem.at[i])

    def remote(src, dst, ssem, rsem, dev):
        return pltpu.make_async_remote_copy(
            src_ref=src, dst_ref=dst, send_sem=ssem, recv_sem=rsem, device_id=dev, device_id_type=MESH
        )

    loads = [
        local(field_h, field_v, 0),
        local(region_h, region_v, 1),
        local(bias_h, bias_in, 2),
        local(wqkv_h, wq_v, 3),
        local(wproj_h, wp_v, 4),
        local(wup_h, wu.at[0], 5),
        local(wdown_h, wd.at[0], 6),
    ]
    for c in loads:
        c.start()

    partners = [(west, lat), (east, lat), (lon, north), (lon, south), (west, north), (east, south), sib]
    partners += z_to + x_to + y_to
    barrier = pltpu.get_barrier_semaphore()

    def greet(dev):
        pl.semaphore_signal(barrier, inc=1, device_id=dev, device_id_type=MESH)

    def greet_plane(first):
        def step(i, carry):
            greet((first + 2 * i, lat))
            return carry

        lax.fori_loop(0, 16, step, 0)

    for dev in partners:
        greet(dev)

    @pl.when(is_first)
    def _():
        greet_plane(other + 1)

    @pl.when(is_last)
    def _():
        greet_plane(other)

    @pl.when(jnp.logical_and(core == 0, jnp.logical_not(is_first)))
    def _():
        greet((half, lat))

    @pl.when(jnp.logical_and(core == 1, jnp.logical_not(is_last)))
    def _():
        greet((half + 31, lat))

    pl.semaphore_wait(barrier, len(partners) + 1 + jnp.where(jnp.logical_or(is_first, is_last), 15, 0))

    z_sends = []
    for i, dev in enumerate(z_to):
        slot = min(i + 1, 7)
        if i != 7:
            z_sends.append((slot, remote(wup_h.at[x, core], wu.at[slot, x, core], z_send.at[2 * i], z_recv.at[2 * i], dev)))
        if i != 6:
            j = 2 * i + 1
            z_sends.append((slot, remote(wdown_h.at[y, core], wd.at[slot, y, core], z_send.at[j], z_recv.at[j], dev)))
    xy_sends, sib_sends = {}, {}
    for group in range(1, 5):
        slots = pl.ds(2 * group - 1, 2 if group < 4 else 1)
        mine_up, mine_down = wu.at[slots, x, core], wd.at[slots, y, core]
        found = []
        for j in range(3):
            i = (group - 1) * 6 + 2 * j
            found.append(remote(mine_up, mine_up, xy_send.at[i], xy_recv.at[i], x_to[j]))
            found.append(remote(mine_down, mine_down, xy_send.at[i + 1], xy_recv.at[i + 1], y_to[j]))
        xy_sends[group] = found
        found = []
        for kind, ref in enumerate((wu, wd)):
            i = (group - 1) * 2 + kind
            view = ref.at[slots, :, core]
            found.append(remote(view, view, sib_send.at[i], sib_recv.at[i], sib))
        sib_sends[group] = found

    def progress(group):
        if group < 5:
            for slot, c in z_sends:
                if (slot + 1) // 2 == group:
                    c.wait_recv()
            for c in xy_sends[group]:
                c.start()
        if group > 1:
            for c in xy_sends[group - 1]:
                c.wait_recv()
            for c in sib_sends[group - 1]:
                c.start()

    def await_weights(groups):
        for group in groups:
            for c in sib_sends[group]:
                c.wait_recv()

    def piece(ref, r):
        return ref.at[r // 4, pl.ds(pl.multiple_of(lax.rem(r, 4) * 16, 16), 16)]

    def push_col(r):
        return remote(piece(field_h, r), rel_in, rel_send.at[r], rel_recv.at[0], (half + 2 * r, lat))

    def rows16(ref, r):
        return ref.at[pl.ds(pl.multiple_of(r * 16, 16), 16), :]

    def push_back(r):
        return remote(rows16(out_t, r), rel_back, rel_send.at[r], rel_recv.at[0], (half + 1 + 2 * r, lat))

    own_col = remote(piece(field_h, 0), piece(col_in, 0), rel_send.at[16], halo_recv.at[0], (other + 31, lat))
    pass_col = remote(rel_in, piece(col_in, chip), rel_send.at[16], halo_recv.at[0], (other + 31, lat))
    own_back = remote(rows16(out_t, 15), rows16(ret_col, 15), rel_send.at[16], ret_recv.at[0], (other, lat))
    pass_back = remote(rel_back, rows16(ret_col, chip), rel_send.at[16], ret_recv.at[0], (other, lat))

    def every(low, high, act):
        def step(r, carry):
            act(r)
            return carry

        lax.fori_loop(low, high, step, 0)

    def start_col():
        @pl.when(is_first)
        def _():
            own_col.start()
            every(1, 16, lambda r: push_col(r).start())

        @pl.when(jnp.logical_not(is_first))
        def _():
            send_col.start()

    def relay_col():
        @pl.when(jnp.logical_and(core == 0, jnp.logical_not(is_first)))
        def _():
            pltpu.make_async_copy(rel_in, rel_in, rel_recv.at[0]).wait()
            pass_col.start()

    def start_back():
        @pl.when(is_last)
        def _():
            own_back.start()
            every(0, 15, lambda r: push_back(r).start())

        @pl.when(jnp.logical_not(is_last))
        def _():
            backs[0].start()

    def relay_back():
        @pl.when(jnp.logical_and(core == 1, jnp.logical_not(is_last)))
        def _():
            pltpu.make_async_copy(rel_back, rel_back, rel_recv.at[0]).wait()
            pass_back.start()

    def relays_done():
        @pl.when(is_first)
        def _():
            own_col.wait_send()
            every(1, 16, lambda r: push_col(r).wait_send())

        @pl.when(is_last)
        def _():
            own_back.wait_send()
            every(0, 15, lambda r: push_back(r).wait_send())

        @pl.when(jnp.logical_not(is_first))
        def _():
            send_col.wait_send()

        @pl.when(jnp.logical_not(is_last))
        def _():
            backs[0].wait_send()

        @pl.when(jnp.logical_and(core == 0, jnp.logical_not(is_first)))
        def _():
            pass_col.wait_send()

        @pl.when(jnp.logical_and(core == 1, jnp.logical_not(is_last)))
        def _():
            pass_back.wait_send()

    send_col = remote(field_h.at[pl.ds(0, 4)], col_in, halo_send.at[0], halo_recv.at[0], (west, lat))
    send_row = remote(row_out.at[pl.ds(16, 64), :], row_in, halo_send.at[1], halo_recv.at[1], (lon, north))
    send_cor = remote(row_out.at[pl.ds(0, 16), :], cor_in, halo_send.at[2], halo_recv.at[2], (west, north))
    send_ids = [
        remote(reg_out, reg_e, halo_send.at[3], halo_recv.at[3], (west, lat)),
        remote(reg_out, reg_s, halo_send.at[4], halo_recv.at[4], (lon, north)),
        remote(reg_out, reg_se, halo_send.at[5], halo_recv.at[5], (west, north)),
    ]
    sub8 = lax.broadcasted_iota(jnp.int32, (8, D), 0)
    scale = LOG2E * 32 ** (-0.5)

    def send_halos():
        start_col()
        for _, c in z_sends:
            c.start()
        loads[1].wait()
        reg_out[...] = jnp.zeros_like(reg_out)
        reg_out[0:18, 0:64] = region_v[...]
        for c in send_ids:
            c.start()
        loads[0].wait()
        tops = [field_v[c, 0:16, :].astype(F32)[0:8] for c in range(COLS)]
        packed = [jnp.where(sub8 < 4, tops[2 * i], swap4(tops[2 * i + 1])) for i in range(9)]
        packed.append(jnp.zeros_like(packed[0]))
        row_out[...] = jnp.concatenate(packed, axis=0).astype(BF16)
        send_row.start()
        send_cor.start()

    def turn_biases():
        loads[2].wait()
        braw[...] = jnp.zeros_like(braw)

        def turn_bias(h, carry):
            braw[:, 0:72] = bias_in[h]
            first = [braw[pl.ds(c, 8, stride=9), :] for c in ORDER]
            first.append(jnp.zeros((56, 128), F32))
            btmp[...] = jnp.concatenate(first, axis=0).T
            second = [btmp[pl.ds(c, 8, stride=9), :] for c in ORDER]
            bias_v[pl.ds(pl.multiple_of(h * 72, 8), 72), :] = jnp.concatenate(second, axis=0) * LOG2E
            return carry

        lax.fori_loop(0, HEADS, turn_bias, 0)

    lane24 = lax.broadcasted_iota(jnp.int32, (24, 128), 1)
    lane64 = lax.broadcasted_iota(jnp.int32, (64, 128), 1)

    def id_rows(here, below):
        moved = jnp.where(lane24 < 60, pltpu.roll(here, 124, 1), pltpu.roll(below, 60, 1))
        tall = jnp.concatenate([moved, jnp.zeros((104, 128), F32)], axis=0)
        return tall.T[0:64]

    def hot_col(table, c):
        wide = jnp.broadcast_to(table[:, c : c + 1], (64, 128))
        return (wide == lane64.astype(F32)).astype(F32)

    def put_ids(s, pos, top, low, bands):
        for b in bands:
            rows = [top[8 * b : 8 * b + 8], low[8 * b : 8 * b + 8]]
            idw[pl.ds((2 * b + s) * WIN_PITCH + 16 * pos, 16), :] = jnp.concatenate(rows, axis=0).astype(BF16)

    def main_ids(below, bands):
        table = id_rows(reg_out[...].astype(F32), below)
        zero = jnp.zeros((64, 128), F32)
        for i, (a, z) in enumerate(PAIRS):
            first, second = hot_col(table, a + 4), hot_col(table, z + 4)
            if i < 4:
                put_ids(0, i, first, second, bands)
            elif i == 4:
                put_ids(0, 4, first, zero, bands)
                put_ids(1, 4, second, zero, bands)
            else:
                put_ids(1, i - 3, first, second, bands)

    def halo_ids():
        table = id_rows(reg_e[...].astype(F32), reg_se[...].astype(F32))
        for i in (0, 1):
            put_ids(1, i, hot_col(table, 2 * i), hot_col(table, 2 * i + 1), range(8))

    def gather_main():
        for i, pair in enumerate(PAIRS):
            rows = [field_v[c + 4].astype(F32)[4:60] for c in pair]
            block = jnp.concatenate(rows, axis=0)
            at = pl.ds(PAIR_AT + PAIR_ROWS * i, PAIR_ROWS)
            x_s[at, :] = block.astype(BF16)
            n_s[at, :] = norm(block)

    def scatter(part, i, res):
        lanes = part
        for b in range(7):
            first, second = res[8 * b : 8 * b + 8], res[56 + 8 * b : 64 + 8 * b]
            if i == 4:
                fill = jnp.zeros_like(first)
                for s, piece in ((0, first), (1, second)):
                    both = jnp.concatenate([piece, fill], axis=0).astype(BF16)
                    qw[pl.ds((2 * b + s) * WIN_PITCH + 64, 16), lanes] = both
            else:
                s, pos = (0, i) if i < 4 else (1, i - 3)
                both = jnp.concatenate([first, second], axis=0).astype(BF16)
                qw[pl.ds((2 * b + s) * WIN_PITCH + 16 * pos, 16), lanes] = both

    def qkv_main():
        loads[3].wait()

        def step(n, carry):
            lanes = pl.ds(pl.multiple_of(n * 256, 256), 256)
            res = jnp.dot(n_s[pl.ds(PAIR_AT, 784), :], wq_v[:, lanes], preferred_element_type=F32)
            res = res * jnp.where(n < 2, scale, 1.0)
            for i in range(7):
                scatter(lanes, i, res[PAIR_ROWS * i : PAIR_ROWS * (i + 1)])
            return carry

        lax.fori_loop(0, 6, step, 0)

    def gather_halo():
        send_row.wait_recv()
        below = row_in[...].astype(F32)
        ready = {}
        for c in range(14):
            piece = below[8 * (c // 2) : 8 * (c // 2) + 8]
            if c % 2 == 0:
                piece = swap4(piece)
            mine = swap4(field_v[c + 4, 48:64, :].astype(F32)[8:16])
            ready[c] = jnp.where(sub8 < 4, mine, piece)
        block = jnp.concatenate([ready[c] for c in LAST], axis=0)
        at = pl.ds(LAST_AT, PAIR_ROWS)
        x_s[at, :] = block.astype(BF16)
        n_s[at, :] = norm(block)
        send_cor.wait_recv()
        corner = cor_in[...].astype(F32)
        send_col.wait_recv()
        for c in range(4):
            piece = corner[8 * (c // 2) : 8 * (c // 2) + 8]
            piece = piece[0:4] if c % 2 == 0 else piece[4:8]
            block = jnp.concatenate([col_in[c].astype(F32)[4:64], piece], axis=0)
            at = pl.ds(64 * c, 64)
            x_s[at, :] = block.astype(BF16)
            n_s[at, :] = norm(block)

    def qkv_halo():
        def step(n, carry):
            lanes = pl.ds(pl.multiple_of(n * 256, 256), 256)
            res = jnp.dot(n_s[pl.ds(0, PAIR_AT), :], wq_v[:, lanes], preferred_element_type=F32)
            res = res * jnp.where(n < 2, scale, 1.0)
            for i in range(2):
                for b in range(8):
                    both = [res[64 * (2 * i + j) + 8 * b : 64 * (2 * i + j) + 8 * b + 8] for j in (0, 1)]
                    at = pl.ds((2 * b + 1) * WIN_PITCH + 16 * i, 16)
                    qw[at, lanes] = jnp.concatenate(both, axis=0).astype(BF16)
            last = res[LAST_AT:PAIR_AT]
            fill = jnp.zeros((8, 256), F32)
            qw[pl.ds(14 * WIN_PITCH, 80), lanes] = jnp.concatenate([last[0:72], fill], axis=0).astype(BF16)
            tail = [last[72:104], last[104:112], fill]
            qw[pl.ds(15 * WIN_PITCH + 32, 48), lanes] = jnp.concatenate(tail, axis=0).astype(BF16)
            return carry

        lax.fori_loop(0, 6, step, 0)

    lane256 = lax.broadcasted_iota(jnp.int32, (80, 256), 1)
    block_of = lax.rem(lane256, 128) // 32

    def window(w):
        at = pl.ds(pl.multiple_of(w * WIN_PITCH, 16), WIN_PITCH)
        zero80 = jnp.zeros((80, 256), BF16)
        zero128 = jnp.zeros((128, 128), BF16)
        fill = jnp.zeros((48, D), BF16)
        ids = idw[at, :]
        wide = jnp.concatenate([ids, jnp.zeros((48, 128), BF16)], axis=0)
        same = lax.dot_general(ids, wide, NT, preferred_element_type=F32)
        shut = (same[0:72] - 1.0) * 1e30
        query = jnp.concatenate([qw[at, 0:D], fill], axis=0).T
        value = jnp.concatenate([qw[at, 2 * D : 3 * D], fill], axis=0).T
        outs = [None] * HEADS
        for g in range(2):
            keys = qw[at, D + 256 * g : D + 256 * g + 256]
            a, b = query[256 * g : 256 * g + 128], query[256 * g + 128 : 256 * g + 256]
            sides = [jnp.concatenate([a, zero128], axis=1), jnp.concatenate([zero128, b], axis=1)]
            masked = jnp.concatenate([jnp.where(block_of == j, keys, zero80) for j in range(4)], axis=0)
            scores = jnp.dot(masked, jnp.concatenate(sides, axis=0), preferred_element_type=F32)
            for j in range(4):
                raised, sums = [], []
                for t in range(2):
                    head = 8 * g + 4 * t + j
                    s = scores[80 * j : 80 * j + 72, 128 * t : 128 * t + 128]
                    s = s + bias_v[72 * head : 72 * head + 72, :] + shut
                    ex = jnp.exp2(s - jnp.max(s, axis=0, keepdims=True))
                    sums.append(1.0 / jnp.sum(ex, axis=0, keepdims=True))
                    raised.append(ex)
                both = [jnp.concatenate(raised, axis=-1), jnp.zeros((8, 256), F32)]
                probs = jnp.concatenate(both, axis=0).astype(BF16)
                at_v = 256 * g + 32 * j
                left = [value[at_v : at_v + 32, 0:80], value[at_v + 128 : at_v + 160, 0:80]]
                res = jnp.dot(jnp.concatenate(left, axis=0), probs, preferred_element_type=F32)
                outs[8 * g + j] = res[0:32, 0:128] * sums[0]
                outs[8 * g + 4 + j] = res[32:64, 128:256] * sums[1]
        att[pl.ds(pl.multiple_of(w * WIN_PITCH, 16), 72), :] = jnp.concatenate(outs, axis=0).T[0:72]

    def attend(i, carry):
        for u in range(4):
            window(8 * lax.rem(i, 2) + 2 * u + i // 2)

        @pl.when(i == 2)
        def _():
            progress(4)

        return carry

    def attention(start, stop):
        lax.fori_loop(start, stop, attend, 0)

    def attended(w, pos):
        return att[w * WIN_PITCH + 8 * pos : w * WIN_PITCH + 8 * pos + 8, :]

    def order_attended():
        for c in range(4):
            block = [attended(2 * b + 1, c) for b in range(8)]
            n_s[64 * c : 64 * c + 64, :] = jnp.concatenate(block, axis=0).astype(BF16)
        block = [att[14 * WIN_PITCH : 14 * WIN_PITCH + 72, :], att[15 * WIN_PITCH + 32 : 15 * WIN_PITCH + 72, :]]
        n_s[LAST_AT:PAIR_AT, :] = jnp.concatenate(block, axis=0).astype(BF16)
        for i, pair in enumerate(PAIRS):
            block = []
            for j in (0, 1):
                s, pos = (0, 2 * i + j) if i < 4 else (1, 2 * (i - 3) + j)
                if i == 4:
                    s, pos = j, 8
                block += [attended(2 * b + s, pos) for b in range(7)]
            n_s[PAIR_AT + 112 * i : PAIR_AT + 112 * i + 112, :] = jnp.concatenate(block, axis=0).astype(BF16)

    def project(at):
        mixed = x_s[at, :].astype(F32) + jnp.dot(n_s[at, :], wp_v[...], preferred_element_type=F32)
        mixed = mixed.astype(BF16)
        x_s[at, :] = mixed
        n_s[at, :] = norm(mixed.astype(F32))

    def raise_hidden(at, size, slots):
        for slot in slots:
            inner = jnp.dot(n_s[at, :], wu[slot].reshape(D, 256), preferred_element_type=F32)
            hid[0:size, 256 * slot : 256 * slot + 256] = gelu(inner).astype(BF16)

    def lower_hidden(size, low, high):
        weights = wd[low:high].reshape(256 * (high - low), D)
        return jnp.dot(hid[0:size, 256 * low : 256 * high], weights, preferred_element_type=F32)

    def mlp_border():
        at, size = pl.ds(0, PAIR_AT), PAIR_AT
        project(at)
        await_weights((1, 2))
        raise_hidden(at, size, range(0, 5))
        acc[...] = x_s[at, :].astype(F32) + lower_hidden(size, 0, 5)
        progress(5)
        await_weights((3, 4))
        raise_hidden(at, size, range(5, 8))
        out_t[at, :] = (acc[...] + lower_hidden(size, 5, 8)).astype(BF16)

    def mlp(start, size):
        at = pl.ds(start, size)
        project(at)
        raise_hidden(at, size, range(8))
        out_t[at, :] = (x_s[at, :].astype(F32) + lower_hidden(size, 0, 8)).astype(BF16)

    backs = [
        remote(out_t.at[pl.ds(0, 256), :], ret_col, ret_send.at[0], ret_recv.at[0], (east, lat)),
        remote(back_cor, ret_cor, ret_send.at[1], ret_recv.at[1], (east, south)),
        remote(back_row, ret_row, ret_send.at[2], ret_recv.at[2], (lon, south)),
    ]

    def send_back():
        start_back()
        ends = [out_t[64 * c + 48 : 64 * c + 64, :].astype(F32)[8:16] for c in range(4)]
        packed = [jnp.where(sub8 < 4, swap4(ends[2 * i]), ends[2 * i + 1]) for i in range(2)]
        back_cor[...] = jnp.concatenate(packed, axis=0).astype(BF16)
        backs[1].start()
        last = out_t[LAST_AT:PAIR_AT, :].astype(F32)
        packed = []
        for i in range(7):
            packed.append(jnp.where(sub8 < 4, swap4(last[16 * i : 16 * i + 8]), last[16 * i + 8 : 16 * i + 16]))
        packed.append(jnp.zeros_like(packed[0]))
        back_row[...] = jnp.concatenate(packed, axis=0).astype(BF16)
        backs[2].start()

    stores = []

    def store_col(c):
        found = pltpu.make_async_copy(out_v.at[c], out_h.at[c], out_sem.at[c])
        found.start()
        stores.append(found)

    def head4(packed, i):
        piece = packed[8 * (i // 2) : 8 * (i // 2) + 8]
        return piece[0:4] if i % 2 == 0 else piece[4:8]

    def finish_main():
        backs[2].wait_recv()
        above = ret_row[...].astype(F32)
        last = out_t[LAST_AT:PAIR_AT, :].astype(F32)
        for i, pair in enumerate(PAIRS):
            block = out_t[PAIR_AT + 112 * i : PAIR_AT + 112 * i + 112, :].astype(F32)
            for j, c in enumerate(pair):
                k = LAST.index(c)
                parts = [head4(above, k), block[56 * j : 56 * j + 56], last[8 * k : 8 * k + 4]]
                out_v[c + 4] = jnp.concatenate(parts, axis=0).astype(BF16)
                store_col(c + 4)

    def finish_halo():
        backs[1].wait_recv()
        above = ret_cor[...].astype(F32)
        backs[0].wait_recv()
        for c in range(4):
            block = ret_col[64 * c : 64 * c + 64, :].astype(F32)
            out_v[c] = jnp.concatenate([head4(above, c), block[0:60]], axis=0).astype(BF16)
            store_col(c)

    def send_ids_done():
        for c in send_ids:
            c.wait_recv()

    send_halos()
    turn_biases()
    relay_col()
    progress(1)
    main_ids(jnp.zeros((24, 128), F32), range(7))
    gather_main()
    qkv_main()
    progress(2)
    attention(0, 1)
    send_ids_done()
    main_ids(reg_s[...].astype(F32), range(7, 8))
    halo_ids()
    gather_halo()
    qkv_halo()
    progress(3)
    attention(1, 4)
    order_attended()
    for c in loads[4:7]:
        c.wait()
    mlp_border()
    send_back()
    mlp(368, 400)
    relay_back()
    mlp(768, 384)
    finish_main()
    finish_halo()

    for c in stores:
        c.wait()
    relays_done()
    for _, c in z_sends:
        c.wait_send()
    for group in range(1, 5):
        for c in xy_sends[group] + sib_sends[group]:
            c.wait_send()
    for c in (send_cor, send_row, *send_ids, *backs[1:]):
        c.wait_send()


def block(field, region, w_qkv, w_proj, w_up, w_down, position_bias):
    vm = pltpu.VMEM
    dma = pltpu.SemaphoreType.DMA
    scratch = [
        vm((COLS, ROWS, D), BF16),
        vm((COLS, ROWS), jnp.int32),
        vm((1152, D), BF16),
        vm((1152, D), BF16),
        vm((16 * WIN_PITCH, 3 * D), BF16),
        vm((16 * WIN_PITCH, 128), BF16),
        vm((16 * WIN_PITCH, D), F32),
        vm((D, 3 * D), BF16),
        vm((D, D), BF16),
        vm((8, 4, 2, 64, 256), BF16),
        vm((8, 4, 2, 32, D), BF16),
        vm((72, 128), F32),
        vm((128, 128), F32),
        vm((HEADS * 72, 128), F32),
        vm((HEADS, 72, 72), F32),
        vm((1152, D), BF16),
        vm((PAIR_AT, D), F32),
        vm((400, 2048), BF16),
        vm((16, D), BF16),
        vm((16, D), BF16),
        vm((24, 128), jnp.int32),
        vm((24, 128), jnp.int32),
        vm((24, 128), jnp.int32),
        vm((24, 128), jnp.int32),
        vm((80, D), BF16),
        vm((4, ROWS, D), BF16),
        vm((64, D), BF16),
        vm((16, D), BF16),
        vm((64, D), BF16),
        vm((16, D), BF16),
        vm((256, D), BF16),
        vm((64, D), BF16),
        vm((16, D), BF16),
        vm((COLS, ROWS, D), BF16),
        dma((8,)),
        dma((COLS,)),
        dma((6,)),
        dma((6,)),
        dma((3,)),
        dma((3,)),
        dma((16,)),
        dma((16,)),
        dma((24,)),
        dma((24,)),
        dma((8,)),
        dma((8,)),
        dma((17,)),
        dma((1,)),
    ]
    done = pl.pallas_call(
        kernel,
        out_shape=jax.ShapeDtypeStruct((COLS, ROWS, D), BF16),
        in_specs=[pl.BlockSpec(memory_space=pl.ANY)] * 7,
        out_specs=pl.BlockSpec(memory_space=pl.ANY),
        scratch_shapes=scratch,
        compiler_params=pltpu.CompilerParams(
            collective_id=0, has_side_effects=True, vmem_limit_bytes=58 * 1024 * 1024
        ),
    )(
        field.transpose(1, 0, 2), region.T, w_qkv, w_proj,
        w_up.reshape(4, 2, 64, 256), w_down.reshape(4, 2, 32, D), position_bias,
    )
    return done.transpose(1, 0, 2)


def solution(mesh):
    placed = (P("lat", "lon", None), P("lat", "lon"), P(), P(), P(None, "lat"), P("lat", None), P())
    return jax.shard_map(
        block, mesh=mesh, in_specs=placed, out_specs=P("lat", "lon", None), check_vma=False
    )
```

```python
import jax
import jax.numpy as jnp
from jax import lax
from jax.experimental import pallas as pl
from jax.experimental.pallas import tpu as pltpu
from jax.sharding import PartitionSpec as P

MESH = pl.DeviceIdType.MESH
D = 512
HEADS = 16
ROWS = 64
COLS = 18
LOG2E = 1.4426950408889634
ORDER = (5, 6, 7, 8, 0, 1, 2, 3, 4)
PAIRS = ((5, 6), (7, 8), (0, 1), (2, 3), (4, 13), (9, 10), (11, 12))
LAST = (5, 6, 7, 8, 0, 1, 2, 3, 4, 9, 10, 11, 12, 13)
LAST_AT = 256
PAIR_AT = 368
PAIR_ROWS = 112
WIN_PITCH = 80
F32 = jnp.float32
BF16 = jnp.bfloat16
NT = (((1,), (1,)), ((), ()))


def norm(x):
    center = jnp.mean(x, axis=-1, keepdims=True)
    moved = x - center
    spread = jnp.mean(moved * moved, axis=-1, keepdims=True)
    return (moved * lax.rsqrt(spread + 1e-05)).astype(BF16)


def gelu(x):
    half = 0.5 * x
    return half + half * jnp.tanh(x * (0.7978845608028654 + 0.0356774081363001 * (x * x)))


def swap4(x):
    return jnp.concatenate([x[4:8], x[0:4]], axis=0)


def kernel(
    field_h, region_h, wqkv_h, wproj_h, wup_h, wdown_h, bias_h, out_h,
    field_v, region_v, x_s, n_s, qw, idw, att, wq_v, wp_v, wu, wd,
    braw, btmp, bias_v, bias_in, out_t, x_e, acc, hid, rel_in, rel_back,
    reg_out, reg_e, reg_s, reg_se, row_out, col_in, row_in, cor_in,
    back_row, back_cor, ret_col, ret_row, ret_cor, out_v,
    local_sem, out_sem, halo_send, halo_recv, ret_send, ret_recv, z_send, z_recv, xy_send, xy_recv,
    sib_send, sib_recv, rel_send, rel_recv,
):
    lon = lax.axis_index("lon")
    lat = lax.axis_index("lat")
    core = lax.rem(lon, 2)
    z_hi = lon // 32
    x, y = lax.rem(lon // 8, 4), lax.rem(lon // 2, 4)
    west, east = lax.rem(lon + 63, 64), lax.rem(lon + 1, 64)
    north, south = lax.rem(lat + 7, 8), lax.rem(lat + 1, 8)
    half = z_hi * 32
    other = 32 - half
    is_first = lax.rem(lon, 32) == 0
    is_last = lax.rem(lon, 32) == 31
    chip = lax.rem(lon, 32) // 2
    sib = (lon + 1 - 2 * core, lat)

    def along_z(steps):
        to = lat + steps + 16
        return (lax.rem(z_hi + to // 8, 2) * 32 + lax.rem(lon, 32), lax.rem(to, 8))

    def in_plane(to_x, to_y):
        return (half + lax.rem(to_x, 4) * 8 + lax.rem(to_y, 4) * 2 + core, lat)

    z_to = [along_z(steps) for steps in (1, -1, 2, -2, 3, -3, 4, -4)]
    x_to = [in_plane(x + steps, y) for steps in (1, 3, 2)]
    y_to = [in_plane(x, y + steps) for steps in (1, 3, 2)]

    def local(src, dst, i):
        return pltpu.make_async_copy(src, dst, local_sem.at[i])

    def remote(src, dst, ssem, rsem, dev):
        return pltpu.make_async_remote_copy(
            src_ref=src, dst_ref=dst, send_sem=ssem, recv_sem=rsem, device_id=dev, device_id_type=MESH
        )

    loads = [
        local(field_h, field_v, 0),
        local(region_h, region_v, 1),
        local(bias_h, bias_in, 2),
        local(wqkv_h, wq_v, 3),
        local(wproj_h, wp_v, 4),
        local(wup_h, wu.at[0], 5),
        local(wdown_h, wd.at[0], 6),
    ]
    for c in loads:
        c.start()

    partners = [(west, lat), (east, lat), (lon, north), (lon, south), (west, north), (east, south), sib]
    partners += z_to + x_to + y_to
    barrier = pltpu.get_barrier_semaphore()

    def greet(dev):
        pl.semaphore_signal(barrier, inc=1, device_id=dev, device_id_type=MESH)

    def greet_plane(first):
        def step(i, carry):
            greet((first + 2 * i, lat))
            return carry

        lax.fori_loop(0, 16, step, 0)

    for dev in partners:
        greet(dev)

    @pl.when(is_first)
    def _():
        greet_plane(other + 1)

    @pl.when(is_last)
    def _():
        greet_plane(other)

    @pl.when(jnp.logical_and(core == 0, jnp.logical_not(is_first)))
    def _():
        greet((half, lat))

    @pl.when(jnp.logical_and(core == 1, jnp.logical_not(is_last)))
    def _():
        greet((half + 31, lat))

    pl.semaphore_wait(barrier, len(partners) + 1 + jnp.where(jnp.logical_or(is_first, is_last), 15, 0))

    z_sends = []
    for i, dev in enumerate(z_to):
        slot = min(i + 1, 7)
        if i != 7:
            z_sends.append((slot, remote(wup_h.at[x, core], wu.at[slot, x, core], z_send.at[2 * i], z_recv.at[2 * i], dev)))
        if i != 6:
            j = 2 * i + 1
            z_sends.append((slot, remote(wdown_h.at[y, core], wd.at[slot, y, core], z_send.at[j], z_recv.at[j], dev)))
    xy_sends, sib_sends = {}, {}
    for group in range(1, 5):
        slots = pl.ds(2 * group - 1, 2 if group < 4 else 1)
        mine_up, mine_down = wu.at[slots, x, core], wd.at[slots, y, core]
        found = []
        for j in range(3):
            i = (group - 1) * 6 + 2 * j
            found.append(remote(mine_up, mine_up, xy_send.at[i], xy_recv.at[i], x_to[j]))
            found.append(remote(mine_down, mine_down, xy_send.at[i + 1], xy_recv.at[i + 1], y_to[j]))
        xy_sends[group] = found
        found = []
        for kind, ref in enumerate((wu, wd)):
            i = (group - 1) * 2 + kind
            view = ref.at[slots, :, core]
            found.append(remote(view, view, sib_send.at[i], sib_recv.at[i], sib))
        sib_sends[group] = found

    def spread(groups):
        for group in groups:
            for slot, c in z_sends:
                if (slot + 1) // 2 == group:
                    c.wait_recv()
            for c in xy_sends[group]:
                c.start()

    def share(groups):
        for group in groups:
            for c in xy_sends[group]:
                c.wait_recv()
            for c in sib_sends[group]:
                c.start()

    def await_weights(groups):
        for group in groups:
            for c in sib_sends[group]:
                c.wait_recv()

    def piece(ref, r):
        return ref.at[r // 4, pl.ds(pl.multiple_of(lax.rem(r, 4) * 16, 16), 16)]

    def push_col(r):
        return remote(piece(field_h, r), rel_in, rel_send.at[r], rel_recv.at[0], (half + 2 * r, lat))

    def rows16(ref, r):
        return ref.at[pl.ds(pl.multiple_of(r * 16, 16), 16), :]

    def push_back(r):
        return remote(rows16(x_s, r), rel_back, rel_send.at[r], rel_recv.at[0], (half + 1 + 2 * r, lat))

    own_col = remote(piece(field_h, 0), piece(col_in, 0), rel_send.at[16], halo_recv.at[0], (other + 31, lat))
    pass_col = remote(rel_in, piece(col_in, chip), rel_send.at[16], halo_recv.at[0], (other + 31, lat))
    own_back = remote(rows16(x_s, 15), rows16(ret_col, 15), rel_send.at[16], ret_recv.at[0], (other, lat))
    pass_back = remote(rel_back, rows16(ret_col, chip), rel_send.at[16], ret_recv.at[0], (other, lat))

    def every(low, high, act):
        def step(r, carry):
            act(r)
            return carry

        lax.fori_loop(low, high, step, 0)

    def start_col():
        @pl.when(is_first)
        def _():
            own_col.start()
            every(1, 16, lambda r: push_col(r).start())

        @pl.when(jnp.logical_not(is_first))
        def _():
            send_col.start()

    def relay_col():
        @pl.when(jnp.logical_and(core == 0, jnp.logical_not(is_first)))
        def _():
            pltpu.make_async_copy(rel_in, rel_in, rel_recv.at[0]).wait()
            pass_col.start()

    def start_back():
        @pl.when(is_last)
        def _():
            own_back.start()
            every(0, 15, lambda r: push_back(r).start())

        @pl.when(jnp.logical_not(is_last))
        def _():
            backs[0].start()

    def relay_back():
        @pl.when(jnp.logical_and(core == 1, jnp.logical_not(is_last)))
        def _():
            pltpu.make_async_copy(rel_back, rel_back, rel_recv.at[0]).wait()
            pass_back.start()

    def relays_done():
        @pl.when(is_first)
        def _():
            own_col.wait_send()
            every(1, 16, lambda r: push_col(r).wait_send())

        @pl.when(is_last)
        def _():
            own_back.wait_send()
            every(0, 15, lambda r: push_back(r).wait_send())

        @pl.when(jnp.logical_not(is_first))
        def _():
            send_col.wait_send()

        @pl.when(jnp.logical_not(is_last))
        def _():
            backs[0].wait_send()

        @pl.when(jnp.logical_and(core == 0, jnp.logical_not(is_first)))
        def _():
            pass_col.wait_send()

        @pl.when(jnp.logical_and(core == 1, jnp.logical_not(is_last)))
        def _():
            pass_back.wait_send()

    send_col = remote(field_h.at[pl.ds(0, 4)], col_in, halo_send.at[0], halo_recv.at[0], (west, lat))
    send_row = remote(row_out.at[pl.ds(16, 64), :], row_in, halo_send.at[1], halo_recv.at[1], (lon, north))
    send_cor = remote(row_out.at[pl.ds(0, 16), :], cor_in, halo_send.at[2], halo_recv.at[2], (west, north))
    send_ids = [
        remote(reg_out, reg_e, halo_send.at[3], halo_recv.at[3], (west, lat)),
        remote(reg_out, reg_s, halo_send.at[4], halo_recv.at[4], (lon, north)),
        remote(reg_out, reg_se, halo_send.at[5], halo_recv.at[5], (west, north)),
    ]
    sub8 = lax.broadcasted_iota(jnp.int32, (8, D), 0)
    scale = LOG2E * 32 ** (-0.5)

    def send_halos():
        start_col()
        for _, c in z_sends[0:8]:
            c.start()
        loads[1].wait()
        reg_out[...] = jnp.zeros_like(reg_out)
        reg_out[0:18, 0:64] = region_v[...]
        for c in send_ids:
            c.start()
        loads[0].wait()
        tops = [field_v[c, 0:16, :].astype(F32)[0:8] for c in range(COLS)]
        packed = [jnp.where(sub8 < 4, tops[2 * i], swap4(tops[2 * i + 1])) for i in range(9)]
        packed.append(jnp.zeros_like(packed[0]))
        row_out[...] = jnp.concatenate(packed, axis=0).astype(BF16)
        send_row.start()
        send_cor.start()

    def turn_biases():
        loads[2].wait()
        braw[...] = jnp.zeros_like(braw)

        def turn_bias(h, carry):
            braw[:, 0:72] = bias_in[h]
            first = [braw[pl.ds(c, 8, stride=9), :] for c in ORDER]
            first.append(jnp.zeros((56, 128), F32))
            btmp[...] = jnp.concatenate(first, axis=0).T
            second = [btmp[pl.ds(c, 8, stride=9), :] for c in ORDER]
            bias_v[pl.ds(pl.multiple_of(h * 72, 8), 72), :] = jnp.concatenate(second, axis=0) * LOG2E
            return carry

        lax.fori_loop(0, HEADS, turn_bias, 0)

    lane24 = lax.broadcasted_iota(jnp.int32, (24, 128), 1)
    lane64 = lax.broadcasted_iota(jnp.int32, (64, 128), 1)

    def id_rows(here, below):
        moved = jnp.where(lane24 < 60, pltpu.roll(here, 124, 1), pltpu.roll(below, 60, 1))
        tall = jnp.concatenate([moved, jnp.zeros((104, 128), F32)], axis=0)
        return tall.T[0:64]

    def hot_col(table, c):
        wide = jnp.broadcast_to(table[:, c : c + 1], (64, 128))
        return (wide == lane64.astype(F32)).astype(F32)

    def put_ids(s, pos, top, low, bands):
        for b in bands:
            rows = [top[8 * b : 8 * b + 8], low[8 * b : 8 * b + 8]]
            idw[pl.ds((2 * b + s) * WIN_PITCH + 16 * pos, 16), :] = jnp.concatenate(rows, axis=0).astype(BF16)

    def main_ids(below, bands):
        table = id_rows(reg_out[...].astype(F32), below)
        zero = jnp.zeros((64, 128), F32)
        for i, (a, z) in enumerate(PAIRS):
            first, second = hot_col(table, a + 4), hot_col(table, z + 4)
            if i < 4:
                put_ids(0, i, first, second, bands)
            elif i == 4:
                put_ids(0, 4, first, zero, bands)
                put_ids(1, 4, second, zero, bands)
            else:
                put_ids(1, i - 3, first, second, bands)

    def halo_ids():
        table = id_rows(reg_e[...].astype(F32), reg_se[...].astype(F32))
        for i in (0, 1):
            put_ids(1, i, hot_col(table, 2 * i), hot_col(table, 2 * i + 1), range(8))

    def gather_main():
        for i, pair in enumerate(PAIRS):
            rows = [field_v[c + 4].astype(F32)[4:60] for c in pair]
            block = jnp.concatenate(rows, axis=0)
            at = pl.ds(PAIR_AT + PAIR_ROWS * i, PAIR_ROWS)
            x_s[at, :] = block.astype(BF16)
            n_s[at, :] = norm(block)

    def scatter(part, i, res):
        lanes = part
        for b in range(7):
            first, second = res[8 * b : 8 * b + 8], res[56 + 8 * b : 64 + 8 * b]
            if i == 4:
                fill = jnp.zeros_like(first)
                for s, piece in ((0, first), (1, second)):
                    both = jnp.concatenate([piece, fill], axis=0).astype(BF16)
                    qw[pl.ds((2 * b + s) * WIN_PITCH + 64, 16), lanes] = both
            else:
                s, pos = (0, i) if i < 4 else (1, i - 3)
                both = jnp.concatenate([first, second], axis=0).astype(BF16)
                qw[pl.ds((2 * b + s) * WIN_PITCH + 16 * pos, 16), lanes] = both

    def qkv_main():
        loads[3].wait()

        def step(n, carry):
            lanes = pl.ds(pl.multiple_of(n * 256, 256), 256)
            res = jnp.dot(n_s[pl.ds(PAIR_AT, 784), :], wq_v[:, lanes], preferred_element_type=F32)
            for i in range(7):
                scatter(lanes, i, res[PAIR_ROWS * i : PAIR_ROWS * (i + 1)])
            return carry

        lax.fori_loop(0, 6, step, 0)

    def gather_halo():
        send_row.wait_recv()
        below = row_in[...].astype(F32)
        ready = {}
        for c in range(14):
            piece = below[8 * (c // 2) : 8 * (c // 2) + 8]
            if c % 2 == 0:
                piece = swap4(piece)
            mine = swap4(field_v[c + 4, 48:64, :].astype(F32)[8:16])
            ready[c] = jnp.where(sub8 < 4, mine, piece)
        block = jnp.concatenate([ready[c] for c in LAST], axis=0)
        at = pl.ds(LAST_AT, PAIR_ROWS)
        x_s[at, :] = block.astype(BF16)
        n_s[at, :] = norm(block)
        send_cor.wait_recv()
        corner = cor_in[...].astype(F32)
        send_col.wait_recv()
        for c in range(4):
            piece = corner[8 * (c // 2) : 8 * (c // 2) + 8]
            piece = piece[0:4] if c % 2 == 0 else piece[4:8]
            block = jnp.concatenate([col_in[c].astype(F32)[4:64], piece], axis=0)
            at = pl.ds(64 * c, 64)
            x_s[at, :] = block.astype(BF16)
            n_s[at, :] = norm(block)

    def qkv_halo():
        def step(n, carry):
            lanes = pl.ds(pl.multiple_of(n * 256, 256), 256)
            res = jnp.dot(n_s[pl.ds(0, PAIR_AT), :], wq_v[:, lanes], preferred_element_type=F32)
            for i in range(2):
                for b in range(8):
                    both = [res[64 * (2 * i + j) + 8 * b : 64 * (2 * i + j) + 8 * b + 8] for j in (0, 1)]
                    at = pl.ds((2 * b + 1) * WIN_PITCH + 16 * i, 16)
                    qw[at, lanes] = jnp.concatenate(both, axis=0).astype(BF16)
            last = res[LAST_AT:PAIR_AT]
            fill = jnp.zeros((8, 256), F32)
            qw[pl.ds(14 * WIN_PITCH, 80), lanes] = jnp.concatenate([last[0:72], fill], axis=0).astype(BF16)
            tail = [last[72:104], last[104:112], fill]
            qw[pl.ds(15 * WIN_PITCH + 32, 48), lanes] = jnp.concatenate(tail, axis=0).astype(BF16)
            return carry

        lax.fori_loop(0, 6, step, 0)

    lane256 = lax.broadcasted_iota(jnp.int32, (80, 256), 1)
    block_of = lax.rem(lane256, 128) // 32

    def window(w):
        at = pl.ds(pl.multiple_of(w * WIN_PITCH, 16), WIN_PITCH)
        zero80 = jnp.zeros((80, 256), BF16)
        zero128 = jnp.zeros((128, 128), BF16)
        fill = jnp.zeros((48, D), BF16)
        ids = idw[at, :]
        wide = jnp.concatenate([ids, jnp.zeros((48, 128), BF16)], axis=0)
        same = lax.dot_general(ids, wide, NT, preferred_element_type=F32)
        shut = (same[0:72] - 1.0) * 1e30
        query = jnp.concatenate([qw[at, 0:D], fill], axis=0).T
        value = jnp.concatenate([qw[at, 2 * D : 3 * D], fill], axis=0).T
        outs = [None] * HEADS
        for g in range(2):
            keys = qw[at, D + 256 * g : D + 256 * g + 256]
            a, b = query[256 * g : 256 * g + 128], query[256 * g + 128 : 256 * g + 256]
            sides = [jnp.concatenate([a, zero128], axis=1), jnp.concatenate([zero128, b], axis=1)]
            masked = jnp.concatenate([jnp.where(block_of == j, keys, zero80) for j in range(4)], axis=0)
            scores = jnp.dot(masked, jnp.concatenate(sides, axis=0), preferred_element_type=F32)
            for j in range(4):
                raised, sums = [], []
                for t in range(2):
                    head = 8 * g + 4 * t + j
                    s = scores[80 * j : 80 * j + 72, 128 * t : 128 * t + 128] * scale
                    s = s + bias_v[72 * head : 72 * head + 72, :] + shut
                    ex = jnp.exp2(s - jnp.max(s, axis=0, keepdims=True))
                    sums.append(1.0 / jnp.sum(ex, axis=0, keepdims=True))
                    raised.append(ex)
                both = [jnp.concatenate(raised, axis=-1), jnp.zeros((8, 256), F32)]
                probs = jnp.concatenate(both, axis=0).astype(BF16)
                at_v = 256 * g + 32 * j
                left = [value[at_v : at_v + 32, 0:80], value[at_v + 128 : at_v + 160, 0:80]]
                res = jnp.dot(jnp.concatenate(left, axis=0), probs, preferred_element_type=F32)
                outs[8 * g + j] = res[0:32, 0:128] * sums[0]
                outs[8 * g + 4 + j] = res[32:64, 128:256] * sums[1]
        att[pl.ds(pl.multiple_of(w * WIN_PITCH, 16), 72), :] = jnp.concatenate(outs, axis=0).T[0:72]

    def attend(i, carry):
        for u in range(4):
            window(8 * lax.rem(i, 2) + 2 * u + i // 2)
        return carry

    def attention(start, stop):
        lax.fori_loop(start, stop, attend, 0)

    def attended(w, pos):
        return att[w * WIN_PITCH + 8 * pos : w * WIN_PITCH + 8 * pos + 8, :]

    def order_halo():
        for c in range(4):
            block = [attended(2 * b + 1, c) for b in range(8)]
            n_s[64 * c : 64 * c + 64, :] = jnp.concatenate(block, axis=0).astype(BF16)

    def order_main():
        block = [att[14 * WIN_PITCH : 14 * WIN_PITCH + 72, :], att[15 * WIN_PITCH + 32 : 15 * WIN_PITCH + 72, :]]
        n_s[LAST_AT:PAIR_AT, :] = jnp.concatenate(block, axis=0).astype(BF16)
        for i, pair in enumerate(PAIRS):
            block = []
            for j in (0, 1):
                s, pos = (0, 2 * i + j) if i < 4 else (1, 2 * (i - 3) + j)
                if i == 4:
                    s, pos = j, 8
                block += [attended(2 * b + s, pos) for b in range(7)]
            n_s[PAIR_AT + 112 * i : PAIR_AT + 112 * i + 112, :] = jnp.concatenate(block, axis=0).astype(BF16)

    def project(start, size):
        at = pl.ds(start, size)
        mixed = x_s[at, :].astype(F32) + jnp.dot(n_s[at, :], wp_v[...], preferred_element_type=F32)
        mixed = mixed.astype(BF16)
        x_s[at, :] = mixed
        return mixed

    def raise_hidden(at, size, slots):
        for slot in slots:
            inner = jnp.dot(n_s[at, :], wu[slot].reshape(D, 256), preferred_element_type=F32)
            hid[0:size, 256 * slot : 256 * slot + 256] = gelu(inner).astype(BF16)

    def lower_hidden(size, low, high):
        weights = wd[low:high].reshape(256 * (high - low), D)
        return jnp.dot(hid[0:size, 256 * low : 256 * high], weights, preferred_element_type=F32)

    def mlp_near(start, size):
        at = pl.ds(start, size)
        n_s[at, :] = norm(project(start, size).astype(F32))
        raise_hidden(at, size, range(0, 5))
        acc[start - PAIR_AT : start - PAIR_AT + size, :] = x_s[at, :].astype(F32) + lower_hidden(size, 0, 5)

    def mlp_far(start, size):
        at = pl.ds(start, size)
        raise_hidden(at, size, range(5, 8))
        total = acc[start - PAIR_AT : start - PAIR_AT + size, :] + lower_hidden(size, 5, 8)
        out_t[at, :] = total.astype(BF16)

    def mlp_edge():
        at, size = pl.ds(0, PAIR_AT), PAIR_AT
        raise_hidden(at, size, range(8))
        out_t[at, :] = (x_e[...].astype(F32) + lower_hidden(size, 0, 8)).astype(BF16)

    backs = [
        remote(x_s.at[pl.ds(0, 256), :], ret_col, ret_send.at[0], ret_recv.at[0], (east, lat)),
        remote(back_cor, ret_cor, ret_send.at[1], ret_recv.at[1], (east, south)),
        remote(back_row, ret_row, ret_send.at[2], ret_recv.at[2], (lon, south)),
    ]

    def send_back_cols():
        loads[4].wait()
        order_halo()
        project(0, 256)
        start_back()
        ends = [x_s[64 * c + 48 : 64 * c + 64, :].astype(F32)[8:16] for c in range(4)]
        packed = [jnp.where(sub8 < 4, swap4(ends[2 * i]), ends[2 * i + 1]) for i in range(2)]
        back_cor[...] = jnp.concatenate(packed, axis=0).astype(BF16)
        backs[1].start()

    def send_back_rows():
        order_main()
        last = project(LAST_AT, PAIR_ROWS).astype(F32)
        packed = []
        for i in range(7):
            packed.append(jnp.where(sub8 < 4, swap4(last[16 * i : 16 * i + 8]), last[16 * i + 8 : 16 * i + 16]))
        packed.append(jnp.zeros_like(packed[0]))
        back_row[...] = jnp.concatenate(packed, axis=0).astype(BF16)
        backs[2].start()

    stores = []

    def store_col(c):
        found = pltpu.make_async_copy(out_v.at[c], out_h.at[c], out_sem.at[c])
        found.start()
        stores.append(found)

    def head4(packed, i):
        piece = packed[8 * (i // 2) : 8 * (i // 2) + 8]
        return piece[0:4] if i % 2 == 0 else piece[4:8]

    def take_back():
        backs[2].wait_recv()
        above = ret_row[...].astype(F32)
        last = x_s[LAST_AT:PAIR_AT, :].astype(F32)
        block = []
        for k in range(14):
            block += [last[8 * k : 8 * k + 4], head4(above, k)]
        block = jnp.concatenate(block, axis=0)
        x_e[LAST_AT:PAIR_AT, :] = block.astype(BF16)
        n_s[LAST_AT:PAIR_AT, :] = norm(block)
        backs[1].wait_recv()
        above = ret_cor[...].astype(F32)
        backs[0].wait_recv()
        for c in range(4):
            block = jnp.concatenate([ret_col[64 * c : 64 * c + 64, :].astype(F32)[0:60], head4(above, c)], axis=0)
            x_e[64 * c : 64 * c + 64, :] = block.astype(BF16)
            n_s[64 * c : 64 * c + 64, :] = norm(block)

    def finish():
        for c in range(4):
            block = out_t[64 * c : 64 * c + 64, :].astype(F32)
            out_v[c] = jnp.concatenate([block[60:64], block[0:60]], axis=0).astype(BF16)
            store_col(c)
        ends = out_t[LAST_AT:PAIR_AT, :].astype(F32)
        for i, pair in enumerate(PAIRS):
            block = out_t[PAIR_AT + 112 * i : PAIR_AT + 112 * i + 112, :].astype(F32)
            for j, c in enumerate(pair):
                k = LAST.index(c)
                parts = [ends[8 * k + 4 : 8 * k + 8], block[56 * j : 56 * j + 56], ends[8 * k : 8 * k + 4]]
                out_v[c + 4] = jnp.concatenate(parts, axis=0).astype(BF16)
                store_col(c + 4)

    def send_ids_done():
        for c in send_ids:
            c.wait_recv()

    send_halos()
    turn_biases()
    for _, c in z_sends[8:]:
        c.start()
    relay_col()
    main_ids(jnp.zeros((24, 128), F32), range(7))
    gather_main()
    qkv_main()
    spread((1, 2))
    attention(0, 1)
    send_ids_done()
    main_ids(reg_s[...].astype(F32), range(7, 8))
    halo_ids()
    gather_halo()
    qkv_halo()
    attention(2, 3)
    spread((3, 4))
    attention(3, 4)
    share((1, 2))
    send_back_cols()
    attention(1, 2)
    send_back_rows()
    relay_back()
    share((3, 4))
    for c in loads[5:7]:
        c.wait()
    await_weights((1, 2))
    mlp_near(368, 400)
    mlp_near(768, 384)
    await_weights((3, 4))
    mlp_far(368, 400)
    mlp_far(768, 384)
    take_back()
    mlp_edge()
    finish()

    for c in stores:
        c.wait()
    relays_done()
    for _, c in z_sends:
        c.wait_send()
    for group in range(1, 5):
        for c in xy_sends[group] + sib_sends[group]:
            c.wait_send()
    for c in (send_cor, send_row, *send_ids, *backs[1:]):
        c.wait_send()


def block(field, region, w_qkv, w_proj, w_up, w_down, position_bias):
    vm = pltpu.VMEM
    dma = pltpu.SemaphoreType.DMA
    scratch = [
        vm((COLS, ROWS, D), BF16),
        vm((COLS, ROWS), jnp.int32),
        vm((1152, D), BF16),
        vm((1152, D), BF16),
        vm((16 * WIN_PITCH, 3 * D), BF16),
        vm((16 * WIN_PITCH, 128), BF16),
        vm((16 * WIN_PITCH, D), F32),
        vm((D, 3 * D), BF16),
        vm((D, D), BF16),
        vm((8, 4, 2, 64, 256), BF16),
        vm((8, 4, 2, 32, D), BF16),
        vm((72, 128), F32),
        vm((128, 128), F32),
        vm((HEADS * 72, 128), F32),
        vm((HEADS, 72, 72), F32),
        vm((1152, D), BF16),
        vm((PAIR_AT, D), BF16),
        vm((784, D), F32),
        vm((784, 2048), BF16),
        vm((16, D), BF16),
        vm((16, D), BF16),
        vm((24, 128), jnp.int32),
        vm((24, 128), jnp.int32),
        vm((24, 128), jnp.int32),
        vm((24, 128), jnp.int32),
        vm((80, D), BF16),
        vm((4, ROWS, D), BF16),
        vm((64, D), BF16),
        vm((16, D), BF16),
        vm((64, D), BF16),
        vm((16, D), BF16),
        vm((256, D), BF16),
        vm((64, D), BF16),
        vm((16, D), BF16),
        vm((COLS, ROWS, D), BF16),
        dma((8,)),
        dma((COLS,)),
        dma((6,)),
        dma((6,)),
        dma((3,)),
        dma((3,)),
        dma((16,)),
        dma((16,)),
        dma((24,)),
        dma((24,)),
        dma((8,)),
        dma((8,)),
        dma((17,)),
        dma((1,)),
    ]
    done = pl.pallas_call(
        kernel,
        out_shape=jax.ShapeDtypeStruct((COLS, ROWS, D), BF16),
        in_specs=[pl.BlockSpec(memory_space=pl.ANY)] * 7,
        out_specs=pl.BlockSpec(memory_space=pl.ANY),
        scratch_shapes=scratch,
        compiler_params=pltpu.CompilerParams(
            collective_id=0, has_side_effects=True, vmem_limit_bytes=58 * 1024 * 1024
        ),
    )(
        field.transpose(1, 0, 2), region.T, w_qkv, w_proj,
        w_up.reshape(4, 2, 64, 256), w_down.reshape(4, 2, 32, D), position_bias,
    )
    return done.transpose(1, 0, 2)


def solution(mesh):
    placed = (P("lat", "lon", None), P("lat", "lon"), P(), P(), P(None, "lat"), P("lat", None), P())
    return jax.shard_map(
        block, mesh=mesh, in_specs=placed, out_specs=P("lat", "lon", None), check_vma=False
    )
```

```python
import jax
import jax.numpy as jnp
from jax import lax
from jax.experimental import pallas as pl
from jax.experimental.pallas import tpu as pltpu
from jax.sharding import PartitionSpec as P

MESH = pl.DeviceIdType.MESH
D = 512
HEADS = 16
ROWS = 64
COLS = 18
LOG2E = 1.4426950408889634
ORDER = (5, 6, 7, 8, 0, 1, 2, 3, 4)
PAIRS = ((5, 6), (7, 8), (0, 1), (2, 3), (4, 13), (9, 10), (11, 12))
LAST = (5, 6, 7, 8, 0, 1, 2, 3, 4, 9, 10, 11, 12, 13)
LAST_AT = 256
PAIR_AT = 368
PAIR_ROWS = 112
WIN_PITCH = 80
F32 = jnp.float32
BF16 = jnp.bfloat16
NT = (((1,), (1,)), ((), ()))


def norm(x):
    center = jnp.mean(x, axis=-1, keepdims=True)
    moved = x - center
    spread = jnp.mean(moved * moved, axis=-1, keepdims=True)
    return (moved * lax.rsqrt(spread + 1e-05)).astype(BF16)


def gelu(x):
    half = 0.5 * x
    return half + half * jnp.tanh(x * (0.7978845608028654 + 0.0356774081363001 * (x * x)))


def swap4(x):
    return jnp.concatenate([x[4:8], x[0:4]], axis=0)


def kernel(
    field_h, region_h, wqkv_h, wproj_h, wup_h, wdown_h, bias_h, out_h,
    field_v, region_v, x_s, n_s, qw, idw, att, wq_v, wp_v, wu, wd,
    braw, btmp, bias_v, bias_in, out_t, x_e, acc, hid, rel_in, rel_far,
    far_in, far_row, reg_f, reg_fs, far_cor, x_f, n_f,
    reg_out, reg_e, reg_s, reg_se, row_out, col_in, row_in, cor_in,
    back_row, back_cor, ret_col, ret_row, ret_cor, out_v,
    local_sem, out_sem, halo_send, halo_recv, ret_send, ret_recv, z_send, z_recv, xy_send, xy_recv,
    sib_send, sib_recv, rel_send, rel_recv, far_send, far_recv,
):
    lon = lax.axis_index("lon")
    lat = lax.axis_index("lat")
    core = lax.rem(lon, 2)
    z_hi = lon // 32
    x, y = lax.rem(lon // 8, 4), lax.rem(lon // 2, 4)
    west, east = lax.rem(lon + 63, 64), lax.rem(lon + 1, 64)
    north, south = lax.rem(lat + 7, 8), lax.rem(lat + 1, 8)
    half = z_hi * 32
    other = 32 - half
    is_first = lax.rem(lon, 32) == 0
    is_last = lax.rem(lon, 32) == 31
    chip = lax.rem(lon, 32) // 2
    sib = (lon + 1 - 2 * core, lat)

    def along_z(steps):
        to = lat + steps + 16
        return (lax.rem(z_hi + to // 8, 2) * 32 + lax.rem(lon, 32), lax.rem(to, 8))

    def in_plane(to_x, to_y):
        return (half + lax.rem(to_x, 4) * 8 + lax.rem(to_y, 4) * 2 + core, lat)

    z_to = [along_z(steps) for steps in (1, -1, 2, -2, 3, -3, 4, -4)]
    x_to = [in_plane(x + steps, y) for steps in (1, 3, 2)]
    y_to = [in_plane(x, y + steps) for steps in (1, 3, 2)]

    def local(src, dst, i):
        return pltpu.make_async_copy(src, dst, local_sem.at[i])

    def remote(src, dst, ssem, rsem, dev):
        return pltpu.make_async_remote_copy(
            src_ref=src, dst_ref=dst, send_sem=ssem, recv_sem=rsem, device_id=dev, device_id_type=MESH
        )

    loads = [
        local(field_h, field_v, 0),
        local(region_h, region_v, 1),
        local(bias_h, bias_in, 2),
        local(wqkv_h, wq_v, 3),
        local(wproj_h, wp_v, 4),
        local(wup_h, wu.at[0], 5),
        local(wdown_h, wd.at[0], 6),
    ]
    for c in loads:
        c.start()

    partners = [(west, lat), (east, lat), (lon, north), (lon, south), (west, north), (east, south), (west, south), sib]
    partners += z_to + x_to + y_to
    barrier = pltpu.get_barrier_semaphore()

    def greet(dev):
        pl.semaphore_signal(barrier, inc=1, device_id=dev, device_id_type=MESH)

    def greet_plane(first, count):
        def step(i, carry):
            greet((first + 2 * i, lat))
            return carry

        lax.fori_loop(0, count, step, 0)

    for dev in partners:
        greet(dev)
    near_relay = jnp.logical_and(core == 0, jnp.logical_not(is_first))
    far_relay = jnp.logical_and(core == 1, chip < 10)

    @pl.when(is_first)
    def _():
        greet_plane(other + 1, 10)

    @pl.when(is_last)
    def _():
        greet_plane(other, 16)

    @pl.when(near_relay)
    def _():
        greet((half, lat))

    @pl.when(far_relay)
    def _():
        greet((half + 31, lat))

    more = jnp.where(jnp.logical_or(core == 0, far_relay), 1, 0)
    more = more + jnp.where(is_first, 15, 0) + jnp.where(is_last, 10, 0)
    pl.semaphore_wait(barrier, len(partners) + more)

    z_sends = []
    for i, dev in enumerate(z_to):
        slot = min(i + 1, 7)
        if i != 7:
            z_sends.append((slot, remote(wup_h.at[x, core], wu.at[slot, x, core], z_send.at[2 * i], z_recv.at[2 * i], dev)))
        if i != 6:
            j = 2 * i + 1
            z_sends.append((slot, remote(wdown_h.at[y, core], wd.at[slot, y, core], z_send.at[j], z_recv.at[j], dev)))
    xy_sends, sib_sends = {}, {}
    for group in range(1, 5):
        slots = pl.ds(2 * group - 1, 2 if group < 4 else 1)
        mine_up, mine_down = wu.at[slots, x, core], wd.at[slots, y, core]
        found = []
        for j in range(3):
            i = (group - 1) * 6 + 2 * j
            found.append(remote(mine_up, mine_up, xy_send.at[i], xy_recv.at[i], x_to[j]))
            found.append(remote(mine_down, mine_down, xy_send.at[i + 1], xy_recv.at[i + 1], y_to[j]))
        xy_sends[group] = found
        found = []
        for kind, ref in enumerate((wu, wd)):
            i = (group - 1) * 2 + kind
            view = ref.at[slots, :, core]
            found.append(remote(view, view, sib_send.at[i], sib_recv.at[i], sib))
        sib_sends[group] = found

    def spread(groups):
        for group in groups:
            for slot, c in z_sends:
                if (slot + 1) // 2 == group:
                    c.wait_recv()
            for c in xy_sends[group]:
                c.start()

    def share(groups):
        for group in groups:
            for c in xy_sends[group]:
                c.wait_recv()
            for c in sib_sends[group]:
                c.start()

    def await_weights(groups):
        for group in groups:
            for c in sib_sends[group]:
                c.wait_recv()

    def piece(ref, r):
        return ref.at[r // 4, pl.ds(pl.multiple_of(lax.rem(r, 4) * 16, 16), 16)]

    def far_piece(ref, first, r):
        return ref.at[first + r // 2, pl.ds(pl.multiple_of(lax.rem(r, 2) * 32, 32), 32)]

    def push_col(r):
        return remote(piece(field_h, r), rel_in, rel_send.at[r], rel_recv.at[0], (half + 2 * r, lat))

    def push_far(r):
        return remote(far_piece(field_h, 13, r), rel_far, rel_send.at[r], rel_recv.at[0], (half + 1 + 2 * r, lat))

    own_col = remote(piece(field_h, 0), piece(col_in, 0), rel_send.at[16], halo_recv.at[0], (other + 31, lat))
    pass_col = remote(rel_in, piece(col_in, chip), rel_send.at[16], halo_recv.at[0], (other + 31, lat))
    near_chip = jnp.where(far_relay, chip, 0)
    pass_far = remote(rel_far, far_piece(far_in, 0, near_chip), rel_send.at[16], far_recv.at[0], (other, lat))
    far_sends = [
        remote(reg_out, reg_f, far_send.at[0], far_recv.at[1], (other, lat)),
        remote(reg_out, reg_fs, far_send.at[1], far_recv.at[2], (other, north)),
        remote(row_out.at[pl.ds(48, 32), :], far_row, far_send.at[2], far_recv.at[3], (other, north)),
    ]
    pass_far_all = remote(far_in, far_in, far_send.at[0], far_recv.at[0], (other, lat))
    far_back = remote(far_cor, ret_cor, far_send.at[3], ret_recv.at[1], (lon, south))

    def every(low, high, act):
        def step(r, carry):
            act(r)
            return carry

        lax.fori_loop(low, high, step, 0)

    def start_col():
        @pl.when(is_first)
        def _():
            own_col.start()
            every(1, 16, lambda r: push_col(r).start())

        @pl.when(jnp.logical_not(is_first))
        def _():
            send_col.start()

        @pl.when(is_last)
        def _():
            every(0, 10, lambda r: push_far(r).start())

    def relay():
        @pl.when(near_relay)
        def _():
            pltpu.make_async_copy(rel_in, rel_in, rel_recv.at[0]).wait()
            pass_col.start()

        @pl.when(far_relay)
        def _():
            pltpu.make_async_copy(rel_far, rel_far, rel_recv.at[0]).wait()
            pass_far.start()

    def start_back():
        @pl.when(jnp.logical_not(is_last))
        def _():
            backs[0].start()
            backs[1].start()

    def relays_done():
        @pl.when(is_first)
        def _():
            own_col.wait_send()
            every(1, 16, lambda r: push_col(r).wait_send())
            far_back.wait_send()

        @pl.when(jnp.logical_not(is_first))
        def _():
            send_col.wait_send()

        @pl.when(is_last)
        def _():
            every(0, 10, lambda r: push_far(r).wait_send())
            for c in far_sends:
                c.wait_send()

        @pl.when(jnp.logical_not(is_last))
        def _():
            backs[0].wait_send()
            backs[1].wait_send()

        @pl.when(near_relay)
        def _():
            pass_col.wait_send()

        @pl.when(far_relay)
        def _():
            pass_far.wait_send()

    send_col = remote(field_h.at[pl.ds(0, 4)], col_in, halo_send.at[0], halo_recv.at[0], (west, lat))
    send_row = remote(row_out, row_in, halo_send.at[1], halo_recv.at[1], (lon, north))
    send_cor = remote(row_out.at[pl.ds(0, 16), :], cor_in, halo_send.at[2], halo_recv.at[2], (west, north))
    send_ids = [
        remote(reg_out, reg_e, halo_send.at[3], halo_recv.at[3], (west, lat)),
        remote(reg_out, reg_s, halo_send.at[4], halo_recv.at[4], (lon, north)),
        remote(reg_out, reg_se, halo_send.at[5], halo_recv.at[5], (west, north)),
    ]
    sub8 = lax.broadcasted_iota(jnp.int32, (8, D), 0)
    scale = LOG2E * 32 ** (-0.5)

    def send_halos():
        start_col()
        for _, c in z_sends[0:8]:
            c.start()
        loads[1].wait()
        reg_out[...] = jnp.zeros_like(reg_out)
        reg_out[0:18, 0:64] = region_v[...]
        for c in send_ids:
            c.start()

        @pl.when(is_last)
        def _():
            for c in far_sends[0:2]:
                c.start()

        loads[0].wait()
        tops = [field_v[c, 0:16, :].astype(F32)[0:8] for c in range(COLS)]
        packed = [jnp.where(sub8 < 4, tops[2 * i], swap4(tops[2 * i + 1])) for i in range(9)]
        packed.append(jnp.zeros_like(packed[0]))
        row_out[...] = jnp.concatenate(packed, axis=0).astype(BF16)
        send_row.start()
        send_cor.start()

        @pl.when(is_last)
        def _():
            far_sends[2].start()

    def turn_biases():
        loads[2].wait()
        braw[...] = jnp.zeros_like(braw)

        def turn_bias(h, carry):
            braw[:, 0:72] = bias_in[h]
            first = [braw[pl.ds(c, 8, stride=9), :] for c in ORDER]
            first.append(jnp.zeros((56, 128), F32))
            btmp[...] = jnp.concatenate(first, axis=0).T
            second = [btmp[pl.ds(c, 8, stride=9), :] for c in ORDER]
            bias_v[pl.ds(pl.multiple_of(h * 72, 8), 72), :] = jnp.concatenate(second, axis=0) * LOG2E
            return carry

        lax.fori_loop(0, HEADS, turn_bias, 0)

    lane24 = lax.broadcasted_iota(jnp.int32, (24, 128), 1)
    lane64 = lax.broadcasted_iota(jnp.int32, (64, 128), 1)

    def id_rows(here, below):
        moved = jnp.where(lane24 < 60, pltpu.roll(here, 124, 1), pltpu.roll(below, 60, 1))
        tall = jnp.concatenate([moved, jnp.zeros((104, 128), F32)], axis=0)
        return tall.T[0:64]

    def hot_col(table, c):
        wide = jnp.broadcast_to(table[:, c : c + 1], (64, 128))
        return (wide == lane64.astype(F32)).astype(F32)

    def window_of(b, s):
        return 2 * b + s if s < 2 else 16 + b

    def put_ids(s, pos, top, low, bands):
        for b in bands:
            rows = [top[8 * b : 8 * b + 8], low[8 * b : 8 * b + 8]]
            idw[pl.ds(window_of(b, s) * WIN_PITCH + 16 * pos, 16), :] = jnp.concatenate(rows, axis=0).astype(BF16)

    def main_ids(below, bands):
        table = id_rows(reg_out[...].astype(F32), below)
        zero = jnp.zeros((64, 128), F32)
        for i, (a, z) in enumerate(PAIRS):
            first, second = hot_col(table, a + 4), hot_col(table, z + 4)
            if i < 4:
                put_ids(0, i, first, second, bands)
            elif i == 4:
                put_ids(0, 4, first, zero, bands)
                put_ids(1, 4, second, zero, bands)
            else:
                put_ids(1, i - 3, first, second, bands)

    def far_ids():
        table = id_rows(reg_out[...].astype(F32), reg_s[...].astype(F32))
        for i in (0, 1):
            put_ids(2, i, hot_col(table, 2 * i), hot_col(table, 2 * i + 1), range(8))
        table = id_rows(reg_f[...].astype(F32), reg_fs[...].astype(F32))
        put_ids(2, 2, hot_col(table, 13), hot_col(table, 14), range(8))
        put_ids(2, 3, hot_col(table, 15), hot_col(table, 16), range(8))
        put_ids(2, 4, hot_col(table, 17), jnp.zeros((64, 128), F32), range(8))

    def halo_ids():
        table = id_rows(reg_e[...].astype(F32), reg_se[...].astype(F32))
        for i in (0, 1):
            put_ids(1, i, hot_col(table, 2 * i), hot_col(table, 2 * i + 1), range(8))

    def gather_main():
        for i, pair in enumerate(PAIRS):
            rows = [field_v[c + 4].astype(F32)[4:60] for c in pair]
            block = jnp.concatenate(rows, axis=0)
            at = pl.ds(PAIR_AT + PAIR_ROWS * i, PAIR_ROWS)
            x_s[at, :] = block.astype(BF16)
            n_s[at, :] = norm(block)

    def scatter(part, i, res):
        lanes = part
        for b in range(7):
            first, second = res[8 * b : 8 * b + 8], res[56 + 8 * b : 64 + 8 * b]
            if i == 4:
                fill = jnp.zeros_like(first)
                for s, piece in ((0, first), (1, second)):
                    both = jnp.concatenate([piece, fill], axis=0).astype(BF16)
                    qw[pl.ds((2 * b + s) * WIN_PITCH + 64, 16), lanes] = both
            else:
                s, pos = (0, i) if i < 4 else (1, i - 3)
                both = jnp.concatenate([first, second], axis=0).astype(BF16)
                qw[pl.ds((2 * b + s) * WIN_PITCH + 16 * pos, 16), lanes] = both

    def gather_last():
        send_row.wait_recv()
        below = row_in[...].astype(F32)
        ready = {}
        for c in range(14):
            piece = below[16 + 8 * (c // 2) : 24 + 8 * (c // 2)]
            if c % 2 == 0:
                piece = swap4(piece)
            mine = swap4(field_v[c + 4, 48:64, :].astype(F32)[8:16])
            ready[c] = jnp.where(sub8 < 4, mine, piece)
        block = jnp.concatenate([ready[c] for c in LAST], axis=0)
        at = pl.ds(LAST_AT, PAIR_ROWS)
        x_s[at, :] = block.astype(BF16)
        n_s[at, :] = norm(block)

    def qkv_main():
        loads[3].wait()

        def step(n, carry):
            lanes = pl.ds(pl.multiple_of(n * 256, 256), 256)
            res = jnp.dot(n_s[pl.ds(LAST_AT, 896), :], wq_v[:, lanes], preferred_element_type=F32)
            for i in range(7):
                scatter(lanes, i, res[PAIR_ROWS * (i + 1) : PAIR_ROWS * (i + 2)])
            last = res[0:PAIR_ROWS]
            fill = jnp.zeros((8, 256), F32)
            qw[pl.ds(14 * WIN_PITCH, 80), lanes] = jnp.concatenate([last[0:72], fill], axis=0).astype(BF16)
            qw[pl.ds(15 * WIN_PITCH + 32, 48), lanes] = jnp.concatenate([last[72:112], fill], axis=0).astype(BF16)
            return carry

        lax.fori_loop(0, 6, step, 0)

    def gather_halo():
        send_cor.wait_recv()
        corner = cor_in[...].astype(F32)
        send_col.wait_recv()
        for c in range(4):
            piece = corner[8 * (c // 2) : 8 * (c // 2) + 8]
            piece = piece[0:4] if c % 2 == 0 else piece[4:8]
            block = jnp.concatenate([col_in[c].astype(F32)[4:64], piece], axis=0)
            at = pl.ds(64 * c, 64)
            x_s[at, :] = block.astype(BF16)
            n_s[at, :] = norm(block)

    def qkv_halo():
        def step(n, carry):
            lanes = pl.ds(pl.multiple_of(n * 256, 256), 256)
            res = jnp.dot(n_s[pl.ds(0, LAST_AT), :], wq_v[:, lanes], preferred_element_type=F32)
            for i in range(2):
                for b in range(8):
                    both = [res[64 * (2 * i + j) + 8 * b : 64 * (2 * i + j) + 8 * b + 8] for j in (0, 1)]
                    at = pl.ds((2 * b + 1) * WIN_PITCH + 16 * i, 16)
                    qw[at, lanes] = jnp.concatenate(both, axis=0).astype(BF16)
            return carry

        lax.fori_loop(0, 6, step, 0)

    lane256 = lax.broadcasted_iota(jnp.int32, (80, 256), 1)
    block_of = lax.rem(lane256, 128) // 32

    def window(w):
        at = pl.ds(pl.multiple_of(w * WIN_PITCH, 16), WIN_PITCH)
        zero80 = jnp.zeros((80, 256), BF16)
        zero128 = jnp.zeros((128, 128), BF16)
        fill = jnp.zeros((48, D), BF16)
        ids = idw[at, :]
        wide = jnp.concatenate([ids, jnp.zeros((48, 128), BF16)], axis=0)
        same = lax.dot_general(ids, wide, NT, preferred_element_type=F32)
        shut = (same[0:72] - 1.0) * 1e30
        query = jnp.concatenate([qw[at, 0:D], fill], axis=0).T
        value = jnp.concatenate([qw[at, 2 * D : 3 * D], fill], axis=0).T
        outs = [None] * HEADS
        for g in range(2):
            keys = qw[at, D + 256 * g : D + 256 * g + 256]
            a, b = query[256 * g : 256 * g + 128], query[256 * g + 128 : 256 * g + 256]
            sides = [jnp.concatenate([a, zero128], axis=1), jnp.concatenate([zero128, b], axis=1)]
            masked = jnp.concatenate([jnp.where(block_of == j, keys, zero80) for j in range(4)], axis=0)
            scores = jnp.dot(masked, jnp.concatenate(sides, axis=0), preferred_element_type=F32)
            for j in range(4):
                raised, sums = [], []
                for t in range(2):
                    head = 8 * g + 4 * t + j
                    s = scores[80 * j : 80 * j + 72, 128 * t : 128 * t + 128] * scale
                    s = s + bias_v[72 * head : 72 * head + 72, :] + shut
                    ex = jnp.exp2(s - jnp.max(s, axis=0, keepdims=True))
                    sums.append(1.0 / jnp.sum(ex, axis=0, keepdims=True))
                    raised.append(ex)
                both = [jnp.concatenate(raised, axis=-1), jnp.zeros((8, 256), F32)]
                probs = jnp.concatenate(both, axis=0).astype(BF16)
                at_v = 256 * g + 32 * j
                left = [value[at_v : at_v + 32, 0:80], value[at_v + 128 : at_v + 160, 0:80]]
                res = jnp.dot(jnp.concatenate(left, axis=0), probs, preferred_element_type=F32)
                outs[8 * g + j] = res[0:32, 0:128] * sums[0]
                outs[8 * g + 4 + j] = res[32:64, 128:256] * sums[1]
        att[pl.ds(pl.multiple_of(w * WIN_PITCH, 16), 72), :] = jnp.concatenate(outs, axis=0).T[0:72]

    def attend(i, carry):
        for u in range(4):
            window(jnp.where(i < 4, 8 * lax.rem(i, 2) + 2 * u + i // 2, 4 * i + u))
        return carry

    def attention(start, stop):
        lax.fori_loop(start, stop, attend, 0)

    def attended(w, pos):
        return att[w * WIN_PITCH + 8 * pos : w * WIN_PITCH + 8 * pos + 8, :]

    def order_halo(ref, s):
        for c in range(4):
            block = [attended(window_of(b, s), c) for b in range(8)]
            ref[64 * c : 64 * c + 64, :] = jnp.concatenate(block, axis=0).astype(BF16)

    def order_main():
        block = [att[14 * WIN_PITCH : 14 * WIN_PITCH + 72, :], att[15 * WIN_PITCH + 32 : 15 * WIN_PITCH + 72, :]]
        n_s[LAST_AT:PAIR_AT, :] = jnp.concatenate(block, axis=0).astype(BF16)
        for i, pair in enumerate(PAIRS):
            block = []
            for j in (0, 1):
                s, pos = (0, 2 * i + j) if i < 4 else (1, 2 * (i - 3) + j)
                if i == 4:
                    s, pos = j, 8
                block += [attended(2 * b + s, pos) for b in range(7)]
            n_s[PAIR_AT + 112 * i : PAIR_AT + 112 * i + 112, :] = jnp.concatenate(block, axis=0).astype(BF16)

    def project(start, size):
        at = pl.ds(start, size)
        mixed = x_s[at, :].astype(F32) + jnp.dot(n_s[at, :], wp_v[...], preferred_element_type=F32)
        mixed = mixed.astype(BF16)
        x_s[at, :] = mixed
        return mixed

    def raise_hidden(at, size, slots):
        for slot in slots:
            inner = jnp.dot(n_s[at, :], wu[slot].reshape(D, 256), preferred_element_type=F32)
            hid[0:size, 256 * slot : 256 * slot + 256] = gelu(inner).astype(BF16)

    def lower_hidden(size, low, high):
        weights = wd[low:high].reshape(256 * (high - low), D)
        return jnp.dot(hid[0:size, 256 * low : 256 * high], weights, preferred_element_type=F32)

    def mlp_near(start, size):
        at = pl.ds(start, size)
        n_s[at, :] = norm(project(start, size).astype(F32))
        raise_hidden(at, size, range(0, 5))
        acc[start - PAIR_AT : start - PAIR_AT + size, :] = x_s[at, :].astype(F32) + lower_hidden(size, 0, 5)

    def mlp_far(start, size):
        at = pl.ds(start, size)
        raise_hidden(at, size, range(5, 8))
        total = acc[start - PAIR_AT : start - PAIR_AT + size, :] + lower_hidden(size, 5, 8)
        out_t[at, :] = total.astype(BF16)

    def mlp_edge():
        at, size = pl.ds(0, PAIR_AT), PAIR_AT
        raise_hidden(at, size, range(8))
        out_t[at, :] = (x_e[...].astype(F32) + lower_hidden(size, 0, 8)).astype(BF16)

    backs = [
        remote(x_s.at[pl.ds(0, 256), :], ret_col, ret_send.at[0], ret_recv.at[0], (east, lat)),
        remote(back_cor, ret_cor, ret_send.at[1], ret_recv.at[1], (east, south)),
        remote(back_row, ret_row, ret_send.at[2], ret_recv.at[2], (lon, south)),
    ]

    def pack_ends(ref):
        ends = [ref[64 * c + 48 : 64 * c + 64, :].astype(F32)[8:16] for c in range(4)]
        packed = [jnp.where(sub8 < 4, swap4(ends[2 * i]), ends[2 * i + 1]) for i in range(2)]
        return jnp.concatenate(packed, axis=0).astype(BF16)

    def send_back_cols():
        loads[4].wait()
        order_halo(n_s, 1)
        project(0, 256)
        back_cor[...] = pack_ends(x_s)
        start_back()

    def far_rows(packed, i):
        piece = packed[8 * (i // 2) : 8 * (i // 2) + 8]
        return piece[0:4] if i % 2 == 0 else piece[4:8]

    def far_work():
        for c in (*far_sends, pass_far_all):
            c.wait_recv()
        far_ids()
        below = row_in[0:16, :].astype(F32)
        for c in range(4):
            block = jnp.concatenate([field_v[c].astype(F32)[4:64], far_rows(below, c)], axis=0)
            x_f[64 * c : 64 * c + 64, :] = block.astype(BF16)
            n_f[64 * c : 64 * c + 64, :] = norm(block)
        below = far_row[...].astype(F32)
        for k in range(5):
            block = jnp.concatenate([far_in[k].astype(F32)[4:64], far_rows(below, k + 1)], axis=0)
            n_f[256 + 64 * k : 320 + 64 * k, :] = norm(block)

        def step(n, carry):
            lanes = pl.ds(pl.multiple_of(n * 256, 256), 256)
            res = jnp.dot(n_f[...], wq_v[:, lanes], preferred_element_type=F32)
            for i in range(5):
                for b in range(8):
                    first = res[128 * i + 8 * b : 128 * i + 8 * b + 8]
                    second = res[128 * i + 64 + 8 * b : 128 * i + 72 + 8 * b] if i < 4 else jnp.zeros_like(first)
                    at = pl.ds((16 + b) * WIN_PITCH + 16 * i, 16)
                    qw[at, lanes] = jnp.concatenate([first, second], axis=0).astype(BF16)
            return carry

        lax.fori_loop(0, 6, step, 0)
        attention(4, 6)
        order_halo(n_f, 2)
        mixed = x_f[...].astype(F32) + jnp.dot(n_f[0:256, :], wp_v[...], preferred_element_type=F32)
        ret_col[...] = mixed.astype(BF16)
        far_cor[...] = pack_ends(ret_col)
        far_back.start()

    def far_windows():
        @pl.when(is_first)
        def _():
            far_work()

    def send_back_rows():
        order_main()
        last = project(LAST_AT, PAIR_ROWS).astype(F32)
        packed = []
        for i in range(7):
            packed.append(jnp.where(sub8 < 4, swap4(last[16 * i : 16 * i + 8]), last[16 * i + 8 : 16 * i + 16]))
        packed.append(jnp.zeros_like(packed[0]))
        back_row[...] = jnp.concatenate(packed, axis=0).astype(BF16)
        backs[2].start()

    stores = []

    def store_col(c):
        found = pltpu.make_async_copy(out_v.at[c], out_h.at[c], out_sem.at[c])
        found.start()
        stores.append(found)

    def head4(packed, i):
        piece = packed[8 * (i // 2) : 8 * (i // 2) + 8]
        return piece[0:4] if i % 2 == 0 else piece[4:8]

    def take_back():
        backs[2].wait_recv()
        above = ret_row[...].astype(F32)
        last = x_s[LAST_AT:PAIR_AT, :].astype(F32)
        block = []
        for k in range(14):
            block += [last[8 * k : 8 * k + 4], head4(above, k)]
        block = jnp.concatenate(block, axis=0)
        x_e[LAST_AT:PAIR_AT, :] = block.astype(BF16)
        n_s[LAST_AT:PAIR_AT, :] = norm(block)
        backs[1].wait_recv()
        above = ret_cor[...].astype(F32)

        @pl.when(jnp.logical_not(is_first))
        def _():
            backs[0].wait_recv()

        for c in range(4):
            block = jnp.concatenate([ret_col[64 * c : 64 * c + 64, :].astype(F32)[0:60], head4(above, c)], axis=0)
            x_e[64 * c : 64 * c + 64, :] = block.astype(BF16)
            n_s[64 * c : 64 * c + 64, :] = norm(block)

    def finish():
        for c in range(4):
            block = out_t[64 * c : 64 * c + 64, :].astype(F32)
            out_v[c] = jnp.concatenate([block[60:64], block[0:60]], axis=0).astype(BF16)
            store_col(c)
        ends = out_t[LAST_AT:PAIR_AT, :].astype(F32)
        for i, pair in enumerate(PAIRS):
            block = out_t[PAIR_AT + 112 * i : PAIR_AT + 112 * i + 112, :].astype(F32)
            for j, c in enumerate(pair):
                k = LAST.index(c)
                parts = [ends[8 * k + 4 : 8 * k + 8], block[56 * j : 56 * j + 56], ends[8 * k : 8 * k + 4]]
                out_v[c + 4] = jnp.concatenate(parts, axis=0).astype(BF16)
                store_col(c + 4)

    def send_ids_done():
        for c in send_ids:
            c.wait_recv()

    send_halos()
    turn_biases()
    for _, c in z_sends[8:]:
        c.start()
    gather_main()
    relay()
    gather_last()
    qkv_main()
    spread((1, 2))
    send_ids_done()
    main_ids(reg_s[...].astype(F32), range(8))
    halo_ids()
    attention(0, 2)
    spread((3, 4))
    gather_halo()
    qkv_halo()
    attention(2, 4)
    share((1, 2))
    send_back_cols()
    send_back_rows()
    share((3, 4))
    for c in loads[5:7]:
        c.wait()
    await_weights((1, 2))
    mlp_near(368, 400)
    mlp_near(768, 384)
    await_weights((3, 4))
    mlp_far(368, 400)
    mlp_far(768, 384)
    far_windows()
    take_back()
    mlp_edge()
    finish()

    for c in stores:
        c.wait()
    relays_done()
    for _, c in z_sends:
        c.wait_send()
    for group in range(1, 5):
        for c in xy_sends[group] + sib_sends[group]:
            c.wait_send()
    for c in (send_cor, send_row, *send_ids, backs[2]):
        c.wait_send()


def block(field, region, w_qkv, w_proj, w_up, w_down, position_bias):
    vm = pltpu.VMEM
    dma = pltpu.SemaphoreType.DMA
    scratch = [
        vm((COLS, ROWS, D), BF16),
        vm((COLS, ROWS), jnp.int32),
        vm((1152, D), BF16),
        vm((1152, D), BF16),
        vm((24 * WIN_PITCH, 3 * D), BF16),
        vm((24 * WIN_PITCH, 128), BF16),
        vm((24 * WIN_PITCH, D), F32),
        vm((D, 3 * D), BF16),
        vm((D, D), BF16),
        vm((8, 4, 2, 64, 256), BF16),
        vm((8, 4, 2, 32, D), BF16),
        vm((72, 128), F32),
        vm((128, 128), F32),
        vm((HEADS * 72, 128), F32),
        vm((HEADS, 72, 72), F32),
        vm((1152, D), BF16),
        vm((PAIR_AT, D), BF16),
        vm((784, D), F32),
        vm((784, 2048), BF16),
        vm((16, D), BF16),
        vm((32, D), BF16),
        vm((5, ROWS, D), BF16),
        vm((32, D), BF16),
        vm((24, 128), jnp.int32),
        vm((24, 128), jnp.int32),
        vm((16, D), BF16),
        vm((256, D), BF16),
        vm((576, D), BF16),
        vm((24, 128), jnp.int32),
        vm((24, 128), jnp.int32),
        vm((24, 128), jnp.int32),
        vm((24, 128), jnp.int32),
        vm((80, D), BF16),
        vm((4, ROWS, D), BF16),
        vm((80, D), BF16),
        vm((16, D), BF16),
        vm((64, D), BF16),
        vm((16, D), BF16),
        vm((256, D), BF16),
        vm((64, D), BF16),
        vm((16, D), BF16),
        vm((COLS, ROWS, D), BF16),
        dma((8,)),
        dma((COLS,)),
        dma((6,)),
        dma((6,)),
        dma((3,)),
        dma((3,)),
        dma((16,)),
        dma((16,)),
        dma((24,)),
        dma((24,)),
        dma((8,)),
        dma((8,)),
        dma((17,)),
        dma((1,)),
        dma((4,)),
        dma((4,)),
    ]
    done = pl.pallas_call(
        kernel,
        out_shape=jax.ShapeDtypeStruct((COLS, ROWS, D), BF16),
        in_specs=[pl.BlockSpec(memory_space=pl.ANY)] * 7,
        out_specs=pl.BlockSpec(memory_space=pl.ANY),
        scratch_shapes=scratch,
        compiler_params=pltpu.CompilerParams(
            collective_id=0, has_side_effects=True, vmem_limit_bytes=58 * 1024 * 1024
        ),
    )(
        field.transpose(1, 0, 2), region.T, w_qkv, w_proj,
        w_up.reshape(4, 2, 64, 256), w_down.reshape(4, 2, 32, D), position_bias,
    )
    return done.transpose(1, 0, 2)


def solution(mesh):
    placed = (P("lat", "lon", None), P("lat", "lon"), P(), P(), P(None, "lat"), P("lat", None), P())
    return jax.shard_map(
        block, mesh=mesh, in_specs=placed, out_specs=P("lat", "lon", None), check_vma=False
    )
```

```python
import jax
import jax.numpy as jnp
from jax import lax
from jax.experimental import pallas as pl
from jax.experimental.pallas import tpu as pltpu
from jax.sharding import PartitionSpec as P

MESH = pl.DeviceIdType.MESH
D = 512
HEADS = 16
ROWS = 64
COLS = 18
LOG2E = 1.4426950408889634
ORDER = (5, 6, 7, 8, 0, 1, 2, 3, 4)
PAIRS = ((5, 6), (7, 8), (0, 1), (2, 3), (4, 13), (9, 10), (11, 12))
LAST = (5, 6, 7, 8, 0, 1, 2, 3, 4, 9, 10, 11, 12, 13)
LAST_AT = 256
PAIR_AT = 368
PAIR_ROWS = 112
WIN_PITCH = 80
F32 = jnp.float32
BF16 = jnp.bfloat16
NT = (((1,), (1,)), ((), ()))


def norm(x):
    center = jnp.mean(x, axis=-1, keepdims=True)
    moved = x - center
    spread = jnp.mean(moved * moved, axis=-1, keepdims=True)
    return (moved * lax.rsqrt(spread + 1e-05)).astype(BF16)


def gelu(x):
    half = 0.5 * x
    return half + half * jnp.tanh(x * (0.7978845608028654 + 0.0356774081363001 * (x * x)))


def swap4(x):
    return jnp.concatenate([x[4:8], x[0:4]], axis=0)


def kernel(
    field_h, region_h, wqkv_h, wproj_h, wup_h, wdown_h, bias_h, out_h,
    field_v, region_v, x_s, n_s, qw, idw, att, wq_v, wp_v, wu, wd,
    braw, btmp, bias_v, bias_in, out_t, x_e, acc, hid, rel_in, rel_far,
    far_in, far_row, reg_f, reg_fs, far_cor, x_f, n_f,
    reg_out, reg_e, reg_s, reg_se, row_out, col_in, row_in, cor_in,
    back_row, back_cor, ret_col, ret_row, ret_cor,
    local_sem, halo_send, halo_recv, ret_send, ret_recv, z_send, z_recv, xy_send, xy_recv,
    sib_send, sib_recv, rel_send, rel_recv, far_send, far_recv,
):
    lon = lax.axis_index("lon")
    lat = lax.axis_index("lat")
    core = lax.rem(lon, 2)
    z_hi = lon // 32
    x, y = lax.rem(lon // 8, 4), lax.rem(lon // 2, 4)
    west, east = lax.rem(lon + 63, 64), lax.rem(lon + 1, 64)
    north, south = lax.rem(lat + 7, 8), lax.rem(lat + 1, 8)
    half = z_hi * 32
    other = 32 - half
    is_first = lax.rem(lon, 32) == 0
    is_last = lax.rem(lon, 32) == 31
    chip = lax.rem(lon, 32) // 2
    sib = (lon + 1 - 2 * core, lat)

    def along_z(steps):
        to = lat + steps + 16
        return (lax.rem(z_hi + to // 8, 2) * 32 + lax.rem(lon, 32), lax.rem(to, 8))

    def in_plane(to_x, to_y):
        return (half + lax.rem(to_x, 4) * 8 + lax.rem(to_y, 4) * 2 + core, lat)

    z_to = [along_z(steps) for steps in (1, -1, 2, -2, 3, -3, 4, -4)]
    x_to = [in_plane(x + steps, y) for steps in (1, 3, 2)]
    y_to = [in_plane(x, y + steps) for steps in (1, 3, 2)]

    def local(src, dst, i):
        return pltpu.make_async_copy(src, dst, local_sem.at[i])

    def remote(src, dst, ssem, rsem, dev):
        return pltpu.make_async_remote_copy(
            src_ref=src, dst_ref=dst, send_sem=ssem, recv_sem=rsem, device_id=dev, device_id_type=MESH
        )

    loads = [
        local(field_h, field_v, 0),
        local(region_h, region_v, 1),
        local(bias_h, bias_in, 2),
        local(wqkv_h, wq_v, 3),
        local(wproj_h, wp_v, 4),
        local(wup_h, wu.at[0], 5),
        local(wdown_h, wd.at[0], 6),
    ]
    for c in loads:
        c.start()

    partners = [(west, lat), (east, lat), (lon, north), (lon, south), (west, north), (east, south), (west, south), sib]
    partners += z_to + x_to + y_to
    barrier = pltpu.get_barrier_semaphore()

    def greet(dev):
        pl.semaphore_signal(barrier, inc=1, device_id=dev, device_id_type=MESH)

    def greet_plane(first, count):
        def step(i, carry):
            greet((first + 2 * i, lat))
            return carry

        lax.fori_loop(0, count, step, 0)

    for dev in partners:
        greet(dev)
    near_relay = jnp.logical_and(core == 0, jnp.logical_not(is_first))
    far_relay = jnp.logical_and(core == 1, chip < 10)

    @pl.when(is_first)
    def _():
        greet_plane(other + 1, 10)

    @pl.when(is_last)
    def _():
        greet_plane(other, 16)

    @pl.when(near_relay)
    def _():
        greet((half, lat))

    @pl.when(far_relay)
    def _():
        greet((half + 31, lat))

    more = jnp.where(jnp.logical_or(core == 0, far_relay), 1, 0)
    more = more + jnp.where(is_first, 15, 0) + jnp.where(is_last, 10, 0)
    def turn_biases():
        loads[2].wait()
        braw[...] = jnp.zeros_like(braw)

        def turn_bias(h, carry):
            braw[:, 0:72] = bias_in[h]
            first = [braw[pl.ds(c, 8, stride=9), :] for c in ORDER]
            first.append(jnp.zeros((56, 128), F32))
            btmp[...] = jnp.concatenate(first, axis=0).T
            second = [btmp[pl.ds(c, 8, stride=9), :] for c in ORDER]
            bias_v[pl.ds(pl.multiple_of(h * 72, 8), 72), :] = jnp.concatenate(second, axis=0) * LOG2E
            return carry

        lax.fori_loop(0, HEADS, turn_bias, 0)

    turn_biases()
    pl.semaphore_wait(barrier, len(partners) + more)

    z_sends = []
    for i, dev in enumerate(z_to):
        slot = min(i + 1, 7)
        if i != 7:
            z_sends.append((slot, remote(wup_h.at[x, core], wu.at[slot, x, core], z_send.at[2 * i], z_recv.at[2 * i], dev)))
        if i != 6:
            j = 2 * i + 1
            z_sends.append((slot, remote(wdown_h.at[y, core], wd.at[slot, y, core], z_send.at[j], z_recv.at[j], dev)))
    xy_sends, sib_sends = {}, {}
    for group in range(1, 5):
        slots = pl.ds(2 * group - 1, 2 if group < 4 else 1)
        mine_up, mine_down = wu.at[slots, x, core], wd.at[slots, y, core]
        found = []
        for j in range(3):
            i = (group - 1) * 6 + 2 * j
            found.append(remote(mine_up, mine_up, xy_send.at[i], xy_recv.at[i], x_to[j]))
            found.append(remote(mine_down, mine_down, xy_send.at[i + 1], xy_recv.at[i + 1], y_to[j]))
        xy_sends[group] = found
        found = []
        for kind, ref in enumerate((wu, wd)):
            i = (group - 1) * 2 + kind
            view = ref.at[slots, :, core]
            found.append(remote(view, view, sib_send.at[i], sib_recv.at[i], sib))
        sib_sends[group] = found

    def spread(groups):
        for group in groups:
            for slot, c in z_sends:
                if (slot + 1) // 2 == group:
                    c.wait_recv()
            for c in xy_sends[group]:
                c.start()

    def share(groups):
        for group in groups:
            for c in xy_sends[group]:
                c.wait_recv()
            for c in sib_sends[group]:
                c.start()

    def await_weights(groups):
        for group in groups:
            for c in sib_sends[group]:
                c.wait_recv()

    def piece(ref, r):
        return ref.at[r // 4, pl.ds(pl.multiple_of(lax.rem(r, 4) * 16, 16), 16)]

    def far_piece(ref, first, r):
        return ref.at[first + r // 2, pl.ds(pl.multiple_of(lax.rem(r, 2) * 32, 32), 32)]

    def push_col(r):
        return remote(piece(field_h, r), rel_in, rel_send.at[r], rel_recv.at[0], (half + 2 * r, lat))

    def push_far(r):
        return remote(far_piece(field_h, 13, r), rel_far, rel_send.at[r], rel_recv.at[0], (half + 1 + 2 * r, lat))

    own_col = remote(piece(field_h, 0), piece(col_in, 0), rel_send.at[16], halo_recv.at[0], (other + 31, lat))
    pass_col = remote(rel_in, piece(col_in, chip), rel_send.at[16], halo_recv.at[0], (other + 31, lat))
    near_chip = jnp.where(far_relay, chip, 0)
    pass_far = remote(rel_far, far_piece(far_in, 0, near_chip), rel_send.at[16], far_recv.at[0], (other, lat))
    far_sends = [
        remote(reg_out, reg_f, far_send.at[0], far_recv.at[1], (other, lat)),
        remote(reg_out, reg_fs, far_send.at[1], far_recv.at[2], (other, north)),
        remote(row_out.at[pl.ds(48, 32), :], far_row, far_send.at[2], far_recv.at[3], (other, north)),
    ]
    pass_far_all = remote(far_in, far_in, far_send.at[0], far_recv.at[0], (other, lat))
    far_back = remote(far_cor, ret_cor, far_send.at[3], ret_recv.at[1], (lon, south))

    def every(low, high, act):
        def step(r, carry):
            act(r)
            return carry

        lax.fori_loop(low, high, step, 0)

    def start_col():
        @pl.when(is_first)
        def _():
            own_col.start()
            every(1, 16, lambda r: push_col(r).start())

        @pl.when(jnp.logical_not(is_first))
        def _():
            send_col.start()

        @pl.when(is_last)
        def _():
            every(0, 10, lambda r: push_far(r).start())

    def relay():
        @pl.when(near_relay)
        def _():
            pltpu.make_async_copy(rel_in, rel_in, rel_recv.at[0]).wait()
            pass_col.start()

        @pl.when(far_relay)
        def _():
            pltpu.make_async_copy(rel_far, rel_far, rel_recv.at[0]).wait()
            pass_far.start()

    def start_back():
        @pl.when(jnp.logical_not(is_last))
        def _():
            backs[0].start()
            backs[1].start()

    def relays_done():
        @pl.when(is_first)
        def _():
            own_col.wait_send()
            every(1, 16, lambda r: push_col(r).wait_send())
            far_back.wait_send()

        @pl.when(jnp.logical_not(is_first))
        def _():
            send_col.wait_send()

        @pl.when(is_last)
        def _():
            every(0, 10, lambda r: push_far(r).wait_send())
            for c in far_sends:
                c.wait_send()

        @pl.when(jnp.logical_not(is_last))
        def _():
            backs[0].wait_send()
            backs[1].wait_send()

        @pl.when(near_relay)
        def _():
            pass_col.wait_send()

        @pl.when(far_relay)
        def _():
            pass_far.wait_send()

    send_col = remote(field_h.at[pl.ds(0, 4)], col_in, halo_send.at[0], halo_recv.at[0], (west, lat))
    send_row = remote(row_out, row_in, halo_send.at[1], halo_recv.at[1], (lon, north))
    send_cor = remote(row_out.at[pl.ds(0, 16), :], cor_in, halo_send.at[2], halo_recv.at[2], (west, north))
    send_ids = [
        remote(reg_out, reg_e, halo_send.at[3], halo_recv.at[3], (west, lat)),
        remote(reg_out, reg_s, halo_send.at[4], halo_recv.at[4], (lon, north)),
        remote(reg_out, reg_se, halo_send.at[5], halo_recv.at[5], (west, north)),
    ]
    sub8 = lax.broadcasted_iota(jnp.int32, (8, D), 0)
    scale = LOG2E * 32 ** (-0.5)

    def send_halos():
        start_col()
        for _, c in z_sends[0:8]:
            c.start()
        loads[1].wait()
        reg_out[...] = jnp.zeros_like(reg_out)
        reg_out[0:18, 0:64] = region_v[...]
        for c in send_ids:
            c.start()

        @pl.when(is_last)
        def _():
            for c in far_sends[0:2]:
                c.start()

        loads[0].wait()
        tops = [field_v[c, 0:16, :].astype(F32)[0:8] for c in range(COLS)]
        packed = [jnp.where(sub8 < 4, tops[2 * i], swap4(tops[2 * i + 1])) for i in range(9)]
        packed.append(jnp.zeros_like(packed[0]))
        row_out[...] = jnp.concatenate(packed, axis=0).astype(BF16)
        send_row.start()
        send_cor.start()

        @pl.when(is_last)
        def _():
            far_sends[2].start()

    lane24 = lax.broadcasted_iota(jnp.int32, (24, 128), 1)
    lane64 = lax.broadcasted_iota(jnp.int32, (64, 128), 1)

    def id_rows(here, below):
        moved = jnp.where(lane24 < 60, pltpu.roll(here, 124, 1), pltpu.roll(below, 60, 1))
        tall = jnp.concatenate([moved, jnp.zeros((104, 128), F32)], axis=0)
        return tall.T[0:64]

    def hot_col(table, c):
        wide = jnp.broadcast_to(table[:, c : c + 1], (64, 128))
        return (wide == lane64.astype(F32)).astype(F32)

    def window_of(b, s):
        return 2 * b + s if s < 2 else 16 + b

    def put_ids(s, pos, top, low, bands):
        for b in bands:
            rows = [top[8 * b : 8 * b + 8], low[8 * b : 8 * b + 8]]
            idw[pl.ds(window_of(b, s) * WIN_PITCH + 16 * pos, 16), :] = jnp.concatenate(rows, axis=0).astype(BF16)

    def main_ids(below, bands):
        table = id_rows(reg_out[...].astype(F32), below)
        zero = jnp.zeros((64, 128), F32)
        for i, (a, z) in enumerate(PAIRS):
            first, second = hot_col(table, a + 4), hot_col(table, z + 4)
            if i < 4:
                put_ids(0, i, first, second, bands)
            elif i == 4:
                put_ids(0, 4, first, zero, bands)
                put_ids(1, 4, second, zero, bands)
            else:
                put_ids(1, i - 3, first, second, bands)

    def far_ids():
        table = id_rows(reg_out[...].astype(F32), reg_s[...].astype(F32))
        for i in (0, 1):
            put_ids(2, i, hot_col(table, 2 * i), hot_col(table, 2 * i + 1), range(8))
        table = id_rows(reg_f[...].astype(F32), reg_fs[...].astype(F32))
        put_ids(2, 2, hot_col(table, 13), hot_col(table, 14), range(8))
        put_ids(2, 3, hot_col(table, 15), hot_col(table, 16), range(8))
        put_ids(2, 4, hot_col(table, 17), jnp.zeros((64, 128), F32), range(8))

    def halo_ids():
        table = id_rows(reg_e[...].astype(F32), reg_se[...].astype(F32))
        for i in (0, 1):
            put_ids(1, i, hot_col(table, 2 * i), hot_col(table, 2 * i + 1), range(8))

    def gather_main():
        for i, pair in enumerate(PAIRS):
            rows = [field_v[c + 4].astype(F32)[4:60] for c in pair]
            block = jnp.concatenate(rows, axis=0)
            at = pl.ds(PAIR_AT + PAIR_ROWS * i, PAIR_ROWS)
            x_s[at, :] = block.astype(BF16)
            n_s[at, :] = norm(block)

    def scatter(part, i, res):
        lanes = part
        for b in range(7):
            first, second = res[8 * b : 8 * b + 8], res[56 + 8 * b : 64 + 8 * b]
            if i == 4:
                fill = jnp.zeros_like(first)
                for s, piece in ((0, first), (1, second)):
                    both = jnp.concatenate([piece, fill], axis=0).astype(BF16)
                    qw[pl.ds((2 * b + s) * WIN_PITCH + 64, 16), lanes] = both
            else:
                s, pos = (0, i) if i < 4 else (1, i - 3)
                both = jnp.concatenate([first, second], axis=0).astype(BF16)
                qw[pl.ds((2 * b + s) * WIN_PITCH + 16 * pos, 16), lanes] = both

    def gather_last():
        send_row.wait_recv()
        below = row_in[...].astype(F32)
        ready = {}
        for c in range(14):
            piece = below[16 + 8 * (c // 2) : 24 + 8 * (c // 2)]
            if c % 2 == 0:
                piece = swap4(piece)
            mine = swap4(field_v[c + 4, 48:64, :].astype(F32)[8:16])
            ready[c] = jnp.where(sub8 < 4, mine, piece)
        block = jnp.concatenate([ready[c] for c in LAST], axis=0)
        at = pl.ds(LAST_AT, PAIR_ROWS)
        x_s[at, :] = block.astype(BF16)
        n_s[at, :] = norm(block)

    def qkv_main():
        loads[3].wait()

        def step(n, carry):
            lanes = pl.ds(pl.multiple_of(n * 256, 256), 256)
            res = jnp.dot(n_s[pl.ds(LAST_AT, 896), :], wq_v[:, lanes], preferred_element_type=F32)
            for i in range(7):
                scatter(lanes, i, res[PAIR_ROWS * (i + 1) : PAIR_ROWS * (i + 2)])
            last = res[0:PAIR_ROWS]
            fill = jnp.zeros((8, 256), F32)
            qw[pl.ds(14 * WIN_PITCH, 80), lanes] = jnp.concatenate([last[0:72], fill], axis=0).astype(BF16)
            qw[pl.ds(15 * WIN_PITCH + 32, 48), lanes] = jnp.concatenate([last[72:112], fill], axis=0).astype(BF16)
            return carry

        lax.fori_loop(0, 6, step, 0)

    def gather_halo():
        send_cor.wait_recv()
        corner = cor_in[...].astype(F32)
        send_col.wait_recv()
        for c in range(4):
            piece = corner[8 * (c // 2) : 8 * (c // 2) + 8]
            piece = piece[0:4] if c % 2 == 0 else piece[4:8]
            block = jnp.concatenate([col_in[c].astype(F32)[4:64], piece], axis=0)
            at = pl.ds(64 * c, 64)
            x_s[at, :] = block.astype(BF16)
            n_s[at, :] = norm(block)

    def qkv_halo():
        def step(n, carry):
            lanes = pl.ds(pl.multiple_of(n * 256, 256), 256)
            res = jnp.dot(n_s[pl.ds(0, LAST_AT), :], wq_v[:, lanes], preferred_element_type=F32)
            for i in range(2):
                for b in range(8):
                    both = [res[64 * (2 * i + j) + 8 * b : 64 * (2 * i + j) + 8 * b + 8] for j in (0, 1)]
                    at = pl.ds((2 * b + 1) * WIN_PITCH + 16 * i, 16)
                    qw[at, lanes] = jnp.concatenate(both, axis=0).astype(BF16)
            return carry

        lax.fori_loop(0, 6, step, 0)

    lane256 = lax.broadcasted_iota(jnp.int32, (80, 256), 1)
    block_of = lax.rem(lane256, 128) // 32

    def window(w):
        at = pl.ds(pl.multiple_of(w * WIN_PITCH, 16), WIN_PITCH)
        zero80 = jnp.zeros((80, 256), BF16)
        zero128 = jnp.zeros((128, 128), BF16)
        fill = jnp.zeros((48, D), BF16)
        ids = idw[at, :]
        wide = jnp.concatenate([ids, jnp.zeros((48, 128), BF16)], axis=0)
        same = lax.dot_general(ids, wide, NT, preferred_element_type=F32)
        shut = (same[0:72] - 1.0) * 1e30
        query = jnp.concatenate([qw[at, 0:D], fill], axis=0).T
        value = jnp.concatenate([qw[at, 2 * D : 3 * D], fill], axis=0).T
        outs = [None] * HEADS
        for g in range(2):
            keys = qw[at, D + 256 * g : D + 256 * g + 256]
            a, b = query[256 * g : 256 * g + 128], query[256 * g + 128 : 256 * g + 256]
            sides = [jnp.concatenate([a, zero128], axis=1), jnp.concatenate([zero128, b], axis=1)]
            masked = jnp.concatenate([jnp.where(block_of == j, keys, zero80) for j in range(4)], axis=0)
            scores = jnp.dot(masked, jnp.concatenate(sides, axis=0), preferred_element_type=F32)
            for j in range(4):
                raised, sums = [], []
                for t in range(2):
                    head = 8 * g + 4 * t + j
                    s = scores[80 * j : 80 * j + 72, 128 * t : 128 * t + 128] * scale
                    s = s + bias_v[72 * head : 72 * head + 72, :] + shut
                    ex = jnp.exp2(s - jnp.max(s, axis=0, keepdims=True))
                    sums.append(1.0 / jnp.sum(ex, axis=0, keepdims=True))
                    raised.append(ex)
                both = [jnp.concatenate(raised, axis=-1), jnp.zeros((8, 256), F32)]
                probs = jnp.concatenate(both, axis=0).astype(BF16)
                at_v = 256 * g + 32 * j
                left = [value[at_v : at_v + 32, 0:80], value[at_v + 128 : at_v + 160, 0:80]]
                res = jnp.dot(jnp.concatenate(left, axis=0), probs, preferred_element_type=F32)
                outs[8 * g + j] = res[0:32, 0:128] * sums[0]
                outs[8 * g + 4 + j] = res[32:64, 128:256] * sums[1]
        att[pl.ds(pl.multiple_of(w * WIN_PITCH, 16), 72), :] = jnp.concatenate(outs, axis=0).T[0:72]

    def attention():
        def attend(i, carry):
            for u in range(4):
                window(8 * lax.rem(i, 2) + 2 * u + i // 2)

            @pl.when(i == 0)
            def _():
                spread((3, 4))

            @pl.when(i == 1)
            def _():
                share((1, 2))
                gather_halo()
                qkv_halo()

            @pl.when(i == 2)
            def _():
                share((3, 4))

            return carry

        lax.fori_loop(0, 4, attend, 0)

    def far_attention():
        def attend(i, carry):
            for u in range(4):
                window(4 * i + u)
            return carry

        lax.fori_loop(4, 6, attend, 0)

    def attended(w, pos):
        return att[w * WIN_PITCH + 8 * pos : w * WIN_PITCH + 8 * pos + 8, :]

    def order_halo(ref, s):
        for c in range(4):
            block = [attended(window_of(b, s), c) for b in range(8)]
            ref[64 * c : 64 * c + 64, :] = jnp.concatenate(block, axis=0).astype(BF16)

    def order_main():
        block = [att[14 * WIN_PITCH : 14 * WIN_PITCH + 72, :], att[15 * WIN_PITCH + 32 : 15 * WIN_PITCH + 72, :]]
        n_s[LAST_AT:PAIR_AT, :] = jnp.concatenate(block, axis=0).astype(BF16)
        for i, pair in enumerate(PAIRS):
            block = []
            for j in (0, 1):
                s, pos = (0, 2 * i + j) if i < 4 else (1, 2 * (i - 3) + j)
                if i == 4:
                    s, pos = j, 8
                block += [attended(2 * b + s, pos) for b in range(7)]
            n_s[PAIR_AT + 112 * i : PAIR_AT + 112 * i + 112, :] = jnp.concatenate(block, axis=0).astype(BF16)

    def project(start, size):
        at = pl.ds(start, size)
        mixed = x_s[at, :].astype(F32) + jnp.dot(n_s[at, :], wp_v[...], preferred_element_type=F32)
        mixed = mixed.astype(BF16)
        x_s[at, :] = mixed
        return mixed

    def raise_hidden(at, size, slots):
        for slot in slots:
            inner = jnp.dot(n_s[at, :], wu[slot].reshape(D, 256), preferred_element_type=F32)
            hid[0:size, 256 * slot : 256 * slot + 256] = gelu(inner).astype(BF16)

    def lower_hidden(size, low, high):
        weights = wd[low:high].reshape(256 * (high - low), D)
        return jnp.dot(hid[0:size, 256 * low : 256 * high], weights, preferred_element_type=F32)

    def mlp_near(start, size):
        at = pl.ds(start, size)
        n_s[at, :] = norm(project(start, size).astype(F32))
        raise_hidden(at, size, range(0, 5))
        acc[start - PAIR_AT : start - PAIR_AT + size, :] = x_s[at, :].astype(F32) + lower_hidden(size, 0, 5)

    def mlp_far(start, size):
        at = pl.ds(start, size)
        raise_hidden(at, size, range(5, 8))
        total = acc[start - PAIR_AT : start - PAIR_AT + size, :] + lower_hidden(size, 5, 8)
        out_t[at, :] = total.astype(BF16)

    def mlp_edge():
        at, size = pl.ds(0, PAIR_AT), PAIR_AT
        raise_hidden(at, size, range(8))
        out_t[at, :] = (x_e[...].astype(F32) + lower_hidden(size, 0, 8)).astype(BF16)

    backs = [
        remote(x_s.at[pl.ds(0, 256), :], ret_col, ret_send.at[0], ret_recv.at[0], (east, lat)),
        remote(back_cor, ret_cor, ret_send.at[1], ret_recv.at[1], (east, south)),
        remote(back_row, ret_row, ret_send.at[2], ret_recv.at[2], (lon, south)),
    ]

    def pack_ends(ref):
        ends = [ref[64 * c + 48 : 64 * c + 64, :].astype(F32)[8:16] for c in range(4)]
        packed = [jnp.where(sub8 < 4, swap4(ends[2 * i]), ends[2 * i + 1]) for i in range(2)]
        return jnp.concatenate(packed, axis=0).astype(BF16)

    def send_back_cols():
        loads[4].wait()
        order_halo(n_s, 1)
        project(0, 256)
        back_cor[...] = pack_ends(x_s)
        start_back()

    def far_rows(packed, i):
        piece = packed[8 * (i // 2) : 8 * (i // 2) + 8]
        return piece[0:4] if i % 2 == 0 else piece[4:8]

    def far_work():
        for c in (*far_sends, pass_far_all):
            c.wait_recv()
        far_ids()
        below = row_in[0:16, :].astype(F32)
        for c in range(4):
            block = jnp.concatenate([field_v[c].astype(F32)[4:64], far_rows(below, c)], axis=0)
            x_f[64 * c : 64 * c + 64, :] = block.astype(BF16)
            n_f[64 * c : 64 * c + 64, :] = norm(block)
        below = far_row[...].astype(F32)
        for k in range(5):
            block = jnp.concatenate([far_in[k].astype(F32)[4:64], far_rows(below, k + 1)], axis=0)
            n_f[256 + 64 * k : 320 + 64 * k, :] = norm(block)

        def step(n, carry):
            lanes = pl.ds(pl.multiple_of(n * 256, 256), 256)
            res = jnp.dot(n_f[...], wq_v[:, lanes], preferred_element_type=F32)
            for i in range(5):
                for b in range(8):
                    first = res[128 * i + 8 * b : 128 * i + 8 * b + 8]
                    second = res[128 * i + 64 + 8 * b : 128 * i + 72 + 8 * b] if i < 4 else jnp.zeros_like(first)
                    at = pl.ds((16 + b) * WIN_PITCH + 16 * i, 16)
                    qw[at, lanes] = jnp.concatenate([first, second], axis=0).astype(BF16)
            return carry

        lax.fori_loop(0, 6, step, 0)
        far_attention()
        order_halo(n_f, 2)
        mixed = x_f[...].astype(F32) + jnp.dot(n_f[0:256, :], wp_v[...], preferred_element_type=F32)
        ret_col[...] = mixed.astype(BF16)
        far_cor[...] = pack_ends(ret_col)
        far_back.start()

    def far_windows():
        @pl.when(is_first)
        def _():
            far_work()

    def send_back_rows():
        order_main()
        last = project(LAST_AT, PAIR_ROWS).astype(F32)
        packed = []
        for i in range(7):
            packed.append(jnp.where(sub8 < 4, swap4(last[16 * i : 16 * i + 8]), last[16 * i + 8 : 16 * i + 16]))
        packed.append(jnp.zeros_like(packed[0]))
        back_row[...] = jnp.concatenate(packed, axis=0).astype(BF16)
        backs[2].start()

    def head4(packed, i):
        piece = packed[8 * (i // 2) : 8 * (i // 2) + 8]
        return piece[0:4] if i % 2 == 0 else piece[4:8]

    def take_back():
        backs[2].wait_recv()
        above = ret_row[...].astype(F32)
        last = x_s[LAST_AT:PAIR_AT, :].astype(F32)
        block = []
        for k in range(14):
            block += [last[8 * k : 8 * k + 4], head4(above, k)]
        block = jnp.concatenate(block, axis=0)
        x_e[LAST_AT:PAIR_AT, :] = block.astype(BF16)
        n_s[LAST_AT:PAIR_AT, :] = norm(block)
        backs[1].wait_recv()
        above = ret_cor[...].astype(F32)

        @pl.when(jnp.logical_not(is_first))
        def _():
            backs[0].wait_recv()

        for c in range(4):
            block = jnp.concatenate([ret_col[64 * c : 64 * c + 64, :].astype(F32)[0:60], head4(above, c)], axis=0)
            x_e[64 * c : 64 * c + 64, :] = block.astype(BF16)
            n_s[64 * c : 64 * c + 64, :] = norm(block)

    def send_ids_done():
        for c in send_ids:
            c.wait_recv()

    send_halos()
    gather_main()
    for _, c in z_sends[8:]:
        c.start()
    gather_last()
    qkv_main()
    spread((1, 2))
    relay()
    send_ids_done()
    main_ids(reg_s[...].astype(F32), range(8))
    halo_ids()
    attention()
    send_back_cols()
    send_back_rows()
    for c in loads[5:7]:
        c.wait()
    await_weights((1, 2))
    mlp_near(368, 400)
    mlp_near(768, 384)
    await_weights((3, 4))
    mlp_far(368, 400)
    mlp_far(768, 384)
    stores = [local(out_t.at[pl.ds(PAIR_AT, 784), :], out_h.at[pl.ds(PAIR_AT, 784), :], 7)]
    stores[0].start()
    far_windows()
    take_back()
    mlp_edge()
    stores.append(local(out_t.at[pl.ds(0, PAIR_AT), :], out_h.at[pl.ds(0, PAIR_AT), :], 8))
    stores[1].start()
    for c in stores:
        c.wait()
    relays_done()
    for _, c in z_sends:
        c.wait_send()
    for group in range(1, 5):
        for c in xy_sends[group] + sib_sends[group]:
            c.wait_send()
    for c in (send_cor, send_row, *send_ids, backs[2]):
        c.wait_send()


def finish_kernel(tokens, out_h, out_v, sem):
    stores = []

    def store_col(c, parts):
        out_v[c] = jnp.concatenate(parts, axis=0).astype(BF16)
        found = pltpu.make_async_copy(out_v.at[c], out_h.at[c], sem.at[c])
        found.start()
        stores.append(found)

    for c in range(4):
        rows = tokens[64 * c : 64 * c + 64, :].astype(F32)
        store_col(c, [rows[60:64], rows[0:60]])
    ends = tokens[LAST_AT:PAIR_AT, :].astype(F32)
    for i, pair in enumerate(PAIRS):
        rows = tokens[PAIR_AT + 112 * i : PAIR_AT + 112 * i + 112, :].astype(F32)
        for j, c in enumerate(pair):
            k = LAST.index(c)
            store_col(c + 4, [ends[8 * k + 4 : 8 * k + 8], rows[56 * j : 56 * j + 56], ends[8 * k : 8 * k + 4]])
    for found in stores:
        found.wait()


def block(field, region, w_qkv, w_proj, w_up, w_down, position_bias):
    vm = pltpu.VMEM
    dma = pltpu.SemaphoreType.DMA
    scratch = [
        vm((COLS, ROWS, D), BF16),
        vm((COLS, ROWS), jnp.int32),
        vm((1152, D), BF16),
        vm((1152, D), BF16),
        vm((24 * WIN_PITCH, 3 * D), BF16),
        vm((24 * WIN_PITCH, 128), BF16),
        vm((24 * WIN_PITCH, D), F32),
        vm((D, 3 * D), BF16),
        vm((D, D), BF16),
        vm((8, 4, 2, 64, 256), BF16),
        vm((8, 4, 2, 32, D), BF16),
        vm((72, 128), F32),
        vm((128, 128), F32),
        vm((HEADS * 72, 128), F32),
        vm((HEADS, 72, 72), F32),
        vm((1152, D), BF16),
        vm((PAIR_AT, D), BF16),
        vm((784, D), F32),
        vm((784, 2048), BF16),
        vm((16, D), BF16),
        vm((32, D), BF16),
        vm((5, ROWS, D), BF16),
        vm((32, D), BF16),
        vm((24, 128), jnp.int32),
        vm((24, 128), jnp.int32),
        vm((16, D), BF16),
        vm((256, D), BF16),
        vm((576, D), BF16),
        vm((24, 128), jnp.int32),
        vm((24, 128), jnp.int32),
        vm((24, 128), jnp.int32),
        vm((24, 128), jnp.int32),
        vm((80, D), BF16),
        vm((4, ROWS, D), BF16),
        vm((80, D), BF16),
        vm((16, D), BF16),
        vm((64, D), BF16),
        vm((16, D), BF16),
        vm((256, D), BF16),
        vm((64, D), BF16),
        vm((16, D), BF16),
        dma((9,)),
        dma((6,)),
        dma((6,)),
        dma((3,)),
        dma((3,)),
        dma((16,)),
        dma((16,)),
        dma((24,)),
        dma((24,)),
        dma((8,)),
        dma((8,)),
        dma((17,)),
        dma((1,)),
        dma((4,)),
        dma((4,)),
    ]
    tokens = pl.pallas_call(
        kernel,
        out_shape=jax.ShapeDtypeStruct((1152, D), BF16),
        in_specs=[pl.BlockSpec(memory_space=pl.ANY)] * 7,
        out_specs=pl.BlockSpec(memory_space=pl.ANY),
        scratch_shapes=scratch,
        compiler_params=pltpu.CompilerParams(
            collective_id=0, has_side_effects=True, vmem_limit_bytes=58 * 1024 * 1024
        ),
    )(
        field.transpose(1, 0, 2), region.T, w_qkv, w_proj,
        w_up.reshape(4, 2, 64, 256), w_down.reshape(4, 2, 32, D), position_bias,
    )
    done = pl.pallas_call(
        finish_kernel,
        out_shape=jax.ShapeDtypeStruct((COLS, ROWS, D), BF16),
        in_specs=[pl.BlockSpec(memory_space=pltpu.VMEM)],
        out_specs=pl.BlockSpec(memory_space=pl.ANY),
        scratch_shapes=[vm((COLS, ROWS, D), BF16), dma((COLS,))],
        compiler_params=pltpu.CompilerParams(vmem_limit_bytes=16 * 1024 * 1024),
    )(tokens)
    return done.transpose(1, 0, 2)


def solution(mesh):
    placed = (P("lat", "lon", None), P("lat", "lon"), P(), P(), P(None, "lat"), P("lat", None), P())
    return jax.shard_map(
        block, mesh=mesh, in_specs=placed, out_specs=P("lat", "lon", None), check_vma=False
    )
```

```python
import jax
import jax.numpy as jnp
from jax import lax
from jax.experimental import pallas as pl
from jax.experimental.pallas import tpu as pltpu
from jax.sharding import PartitionSpec as P

MESH = pl.DeviceIdType.MESH
D = 512
HEADS = 16
ROWS = 64
COLS = 18
LOG2E = 1.4426950408889634
ORDER = (5, 6, 7, 8, 0, 1, 2, 3, 4)
PAIRS = ((5, 6), (7, 8), (0, 1), (2, 3), (4, 13), (9, 10), (11, 12))
LAST = (5, 6, 7, 8, 0, 1, 2, 3, 4, 9, 10, 11, 12, 13)
LAST_AT = 256
PAIR_AT = 368
PAIR_ROWS = 112
WIN_PITCH = 80
F32 = jnp.float32
BF16 = jnp.bfloat16
NT = (((1,), (1,)), ((), ()))


def norm(x):
    center = jnp.mean(x, axis=-1, keepdims=True)
    moved = x - center
    spread = jnp.mean(moved * moved, axis=-1, keepdims=True)
    return (moved * lax.rsqrt(spread + 1e-05)).astype(BF16)


def gelu(x):
    half = 0.5 * x
    return half + half * jnp.tanh(x * (0.7978845608028654 + 0.0356774081363001 * (x * x)))


def swap4(x):
    return jnp.concatenate([x[4:8], x[0:4]], axis=0)


def kernel(
    field_h, region_h, wqkv_h, wproj_h, wup_h, wdown_h, bias_h, out_h,
    field_v, region_v, x_s, n_s, qw, idw, att, wq_v, wp_v, wu, wd,
    braw, btmp, bias_v, bias_in, out_t, x_e, acc, hid, rel_in, rel_far,
    far_in, far_row, reg_f, reg_fs, far_cor, x_f, n_f,
    reg_out, reg_e, reg_s, reg_se, row_out, col_in, row_in, cor_in,
    back_row, back_cor, ret_col, ret_row, ret_cor,
    local_sem, halo_send, halo_recv, ret_send, ret_recv, z_send, z_recv, xy_send, xy_recv,
    sib_send, sib_recv, rel_send, rel_recv, far_send, far_recv,
):
    lon = lax.axis_index("lon")
    lat = lax.axis_index("lat")
    core = lax.rem(lon, 2)
    z_hi = lon // 32
    x, y = lax.rem(lon // 8, 4), lax.rem(lon // 2, 4)
    west, east = lax.rem(lon + 63, 64), lax.rem(lon + 1, 64)
    north, south = lax.rem(lat + 7, 8), lax.rem(lat + 1, 8)
    half = z_hi * 32
    other = 32 - half
    is_first = lax.rem(lon, 32) == 0
    is_last = lax.rem(lon, 32) == 31
    chip = lax.rem(lon, 32) // 2
    sib = (lon + 1 - 2 * core, lat)

    def along_z(steps):
        to = lat + steps + 16
        return (lax.rem(z_hi + to // 8, 2) * 32 + lax.rem(lon, 32), lax.rem(to, 8))

    def in_plane(to_x, to_y):
        return (half + lax.rem(to_x, 4) * 8 + lax.rem(to_y, 4) * 2 + core, lat)

    z_to = [along_z(steps) for steps in (1, -1, 2, -2, 3, -3, 4, -4)]
    x_to = [in_plane(x + steps, y) for steps in (1, 3, 2)]
    y_to = [in_plane(x, y + steps) for steps in (1, 3, 2)]

    def local(src, dst, i):
        return pltpu.make_async_copy(src, dst, local_sem.at[i])

    def remote(src, dst, ssem, rsem, dev):
        return pltpu.make_async_remote_copy(
            src_ref=src, dst_ref=dst, send_sem=ssem, recv_sem=rsem, device_id=dev, device_id_type=MESH
        )

    loads = [
        local(field_h, field_v, 0),
        local(region_h, region_v, 1),
        local(bias_h, bias_in, 2),
        local(wqkv_h, wq_v, 3),
        local(wproj_h, wp_v, 4),
        local(wup_h, wu.at[0], 5),
        local(wdown_h, wd.at[0], 6),
    ]
    for c in loads:
        c.start()

    partners = [(west, lat), (east, lat), (lon, north), (lon, south), (west, north), (east, south), (west, south), sib]
    partners += z_to + x_to + y_to
    barrier = pltpu.get_barrier_semaphore()

    def greet(dev):
        pl.semaphore_signal(barrier, inc=1, device_id=dev, device_id_type=MESH)

    def greet_plane(first, count):
        def step(i, carry):
            greet((first + 2 * i, lat))
            return carry

        lax.fori_loop(0, count, step, 0)

    for dev in partners:
        greet(dev)
    near_relay = jnp.logical_and(core == 0, jnp.logical_not(is_first))
    far_relay = jnp.logical_and(core == 1, chip < 10)

    @pl.when(is_first)
    def _():
        greet_plane(other + 1, 10)

    @pl.when(is_last)
    def _():
        greet_plane(other, 16)

    @pl.when(near_relay)
    def _():
        greet((half, lat))

    @pl.when(far_relay)
    def _():
        greet((half + 31, lat))

    more = jnp.where(jnp.logical_or(core == 0, far_relay), 1, 0)
    more = more + jnp.where(is_first, 15, 0) + jnp.where(is_last, 10, 0)
    def turn_biases():
        loads[2].wait()
        braw[...] = jnp.zeros_like(braw)

        def turn_bias(h, carry):
            braw[:, 0:72] = bias_in[h]
            first = [braw[pl.ds(c, 8, stride=9), :] for c in ORDER]
            first.append(jnp.zeros((56, 128), F32))
            btmp[...] = jnp.concatenate(first, axis=0).T
            second = [btmp[pl.ds(c, 8, stride=9), :] for c in ORDER]
            bias_v[pl.ds(pl.multiple_of(h * 72, 8), 72), :] = jnp.concatenate(second, axis=0) * LOG2E
            return carry

        lax.fori_loop(0, HEADS, turn_bias, 0)

    turn_biases()
    pl.semaphore_wait(barrier, len(partners) + more)

    z_sends = []
    for i, dev in enumerate(z_to):
        slot = min(i + 1, 7)
        if i != 7:
            z_sends.append((slot, remote(wup_h.at[x, core], wu.at[slot, x, core], z_send.at[2 * i], z_recv.at[2 * i], dev)))
        if i != 6:
            j = 2 * i + 1
            z_sends.append((slot, remote(wdown_h.at[y, core], wd.at[slot, y, core], z_send.at[j], z_recv.at[j], dev)))
    xy_sends, sib_sends = {}, {}
    for group in range(1, 5):
        slots = pl.ds(2 * group - 1, 2 if group < 4 else 1)
        mine_up, mine_down = wu.at[slots, x, core], wd.at[slots, y, core]
        found = []
        for j in range(3):
            i = (group - 1) * 6 + 2 * j
            found.append(remote(mine_up, mine_up, xy_send.at[i], xy_recv.at[i], x_to[j]))
            found.append(remote(mine_down, mine_down, xy_send.at[i + 1], xy_recv.at[i + 1], y_to[j]))
        xy_sends[group] = found
        found = []
        for kind, ref in enumerate((wu, wd)):
            i = (group - 1) * 2 + kind
            view = ref.at[slots, :, core]
            found.append(remote(view, view, sib_send.at[i], sib_recv.at[i], sib))
        sib_sends[group] = found

    def spread(groups):
        for group in groups:
            for slot, c in z_sends:
                if (slot + 1) // 2 == group:
                    c.wait_recv()
            for c in xy_sends[group]:
                c.start()

    def share(groups):
        for group in groups:
            for c in xy_sends[group]:
                c.wait_recv()
            for c in sib_sends[group]:
                c.start()

    def await_weights(groups):
        for group in groups:
            for c in sib_sends[group]:
                c.wait_recv()

    def piece(ref, r):
        return ref.at[r // 4, pl.ds(pl.multiple_of(lax.rem(r, 4) * 16, 16), 16)]

    def far_piece(ref, first, r):
        return ref.at[first + r // 2, pl.ds(pl.multiple_of(lax.rem(r, 2) * 32, 32), 32)]

    def push_col(r):
        return remote(piece(field_h, r), rel_in, rel_send.at[r], rel_recv.at[0], (half + 2 * r, lat))

    def push_far(r):
        return remote(far_piece(field_h, 13, r), rel_far, rel_send.at[r], rel_recv.at[0], (half + 1 + 2 * r, lat))

    own_col = remote(piece(field_h, 0), piece(col_in, 0), rel_send.at[16], halo_recv.at[0], (other + 31, lat))
    pass_col = remote(rel_in, piece(col_in, chip), rel_send.at[16], halo_recv.at[0], (other + 31, lat))
    near_chip = jnp.where(far_relay, chip, 0)
    pass_far = remote(rel_far, far_piece(far_in, 0, near_chip), rel_send.at[16], far_recv.at[0], (other, lat))
    far_sends = [
        remote(reg_out, reg_f, far_send.at[0], far_recv.at[1], (other, lat)),
        remote(reg_out, reg_fs, far_send.at[1], far_recv.at[2], (other, north)),
        remote(row_out.at[pl.ds(48, 32), :], far_row, far_send.at[2], far_recv.at[3], (other, north)),
    ]
    pass_far_all = remote(far_in, far_in, far_send.at[0], far_recv.at[0], (other, lat))
    far_back = remote(far_cor, ret_cor, far_send.at[3], ret_recv.at[1], (lon, south))

    def every(low, high, act):
        def step(r, carry):
            act(r)
            return carry

        lax.fori_loop(low, high, step, 0)

    def start_col():
        @pl.when(is_first)
        def _():
            own_col.start()
            every(1, 16, lambda r: push_col(r).start())

        @pl.when(jnp.logical_not(is_first))
        def _():
            send_col.start()

        @pl.when(is_last)
        def _():
            every(0, 10, lambda r: push_far(r).start())

    def relay():
        @pl.when(near_relay)
        def _():
            pltpu.make_async_copy(rel_in, rel_in, rel_recv.at[0]).wait()
            pass_col.start()

        @pl.when(far_relay)
        def _():
            pltpu.make_async_copy(rel_far, rel_far, rel_recv.at[0]).wait()
            pass_far.start()

    def start_back():
        @pl.when(jnp.logical_not(is_last))
        def _():
            backs[0].start()
            backs[1].start()

    def relays_done():
        @pl.when(is_first)
        def _():
            own_col.wait_send()
            every(1, 16, lambda r: push_col(r).wait_send())
            far_back.wait_send()

        @pl.when(jnp.logical_not(is_first))
        def _():
            send_col.wait_send()

        @pl.when(is_last)
        def _():
            every(0, 10, lambda r: push_far(r).wait_send())
            for c in far_sends:
                c.wait_send()

        @pl.when(jnp.logical_not(is_last))
        def _():
            backs[0].wait_send()
            backs[1].wait_send()

        @pl.when(near_relay)
        def _():
            pass_col.wait_send()

        @pl.when(far_relay)
        def _():
            pass_far.wait_send()

    send_col = remote(field_h.at[pl.ds(0, 4)], col_in, halo_send.at[0], halo_recv.at[0], (west, lat))
    send_row = remote(row_out, row_in, halo_send.at[1], halo_recv.at[1], (lon, north))
    send_cor = remote(row_out.at[pl.ds(0, 16), :], cor_in, halo_send.at[2], halo_recv.at[2], (west, north))
    send_ids = [
        remote(reg_out, reg_e, halo_send.at[3], halo_recv.at[3], (west, lat)),
        remote(reg_out, reg_s, halo_send.at[4], halo_recv.at[4], (lon, north)),
        remote(reg_out, reg_se, halo_send.at[5], halo_recv.at[5], (west, north)),
    ]
    sub8 = lax.broadcasted_iota(jnp.int32, (8, D), 0)
    scale = LOG2E * 32 ** (-0.5)

    def send_halos():
        start_col()
        loads[1].wait()
        reg_out[...] = jnp.zeros_like(reg_out)
        reg_out[0:18, 0:64] = region_v[...]
        for c in send_ids:
            c.start()

        @pl.when(is_last)
        def _():
            for c in far_sends[0:2]:
                c.start()

        loads[0].wait()
        tops = [field_v[c, 0:16, :].astype(F32)[0:8] for c in range(COLS)]
        packed = [jnp.where(sub8 < 4, tops[2 * i], swap4(tops[2 * i + 1])) for i in range(9)]
        packed.append(jnp.zeros_like(packed[0]))
        row_out[...] = jnp.concatenate(packed, axis=0).astype(BF16)
        send_row.start()
        send_cor.start()

        @pl.when(is_last)
        def _():
            far_sends[2].start()

        for _, c in z_sends[0:8]:
            c.start()

    lane24 = lax.broadcasted_iota(jnp.int32, (24, 128), 1)
    lane64 = lax.broadcasted_iota(jnp.int32, (64, 128), 1)

    def id_rows(here, below):
        moved = jnp.where(lane24 < 60, pltpu.roll(here, 124, 1), pltpu.roll(below, 60, 1))
        tall = jnp.concatenate([moved, jnp.zeros((104, 128), F32)], axis=0)
        return tall.T[0:64]

    def hot_col(table, c):
        wide = jnp.broadcast_to(table[:, c : c + 1], (64, 128))
        return (wide == lane64.astype(F32)).astype(F32)

    def window_of(b, s):
        return 2 * b + s if s < 2 else 16 + b

    def put_ids(s, pos, top, low, bands):
        for b in bands:
            rows = [top[8 * b : 8 * b + 8], low[8 * b : 8 * b + 8]]
            idw[pl.ds(window_of(b, s) * WIN_PITCH + 16 * pos, 16), :] = jnp.concatenate(rows, axis=0).astype(BF16)

    def main_ids(below, bands):
        table = id_rows(reg_out[...].astype(F32), below)
        zero = jnp.zeros((64, 128), F32)
        for i, (a, z) in enumerate(PAIRS):
            first, second = hot_col(table, a + 4), hot_col(table, z + 4)
            if i < 4:
                put_ids(0, i, first, second, bands)
            elif i == 4:
                put_ids(0, 4, first, zero, bands)
                put_ids(1, 4, second, zero, bands)
            else:
                put_ids(1, i - 3, first, second, bands)

    def far_ids():
        table = id_rows(reg_out[...].astype(F32), reg_s[...].astype(F32))
        for i in (0, 1):
            put_ids(2, i, hot_col(table, 2 * i), hot_col(table, 2 * i + 1), range(8))
        table = id_rows(reg_f[...].astype(F32), reg_fs[...].astype(F32))
        put_ids(2, 2, hot_col(table, 13), hot_col(table, 14), range(8))
        put_ids(2, 3, hot_col(table, 15), hot_col(table, 16), range(8))
        put_ids(2, 4, hot_col(table, 17), jnp.zeros((64, 128), F32), range(8))

    def halo_ids():
        table = id_rows(reg_e[...].astype(F32), reg_se[...].astype(F32))
        for i in (0, 1):
            put_ids(1, i, hot_col(table, 2 * i), hot_col(table, 2 * i + 1), range(8))

    def gather_main():
        for i, pair in enumerate(PAIRS):
            rows = [field_v[c + 4].astype(F32)[4:60] for c in pair]
            block = jnp.concatenate(rows, axis=0)
            at = pl.ds(PAIR_AT + PAIR_ROWS * i, PAIR_ROWS)
            x_s[at, :] = block.astype(BF16)
            n_s[at, :] = norm(block)

    def scatter(part, i, res):
        lanes = part
        for b in range(7):
            first, second = res[8 * b : 8 * b + 8], res[56 + 8 * b : 64 + 8 * b]
            if i == 4:
                fill = jnp.zeros_like(first)
                for s, piece in ((0, first), (1, second)):
                    both = jnp.concatenate([piece, fill], axis=0).astype(BF16)
                    qw[pl.ds((2 * b + s) * WIN_PITCH + 64, 16), lanes] = both
            else:
                s, pos = (0, i) if i < 4 else (1, i - 3)
                both = jnp.concatenate([first, second], axis=0).astype(BF16)
                qw[pl.ds((2 * b + s) * WIN_PITCH + 16 * pos, 16), lanes] = both

    def gather_last():
        send_row.wait_recv()
        below = row_in[...].astype(F32)
        ready = {}
        for c in range(14):
            piece = below[16 + 8 * (c // 2) : 24 + 8 * (c // 2)]
            if c % 2 == 0:
                piece = swap4(piece)
            mine = swap4(field_v[c + 4, 48:64, :].astype(F32)[8:16])
            ready[c] = jnp.where(sub8 < 4, mine, piece)
        block = jnp.concatenate([ready[c] for c in LAST], axis=0)
        at = pl.ds(LAST_AT, PAIR_ROWS)
        x_s[at, :] = block.astype(BF16)
        n_s[at, :] = norm(block)

    def qkv_main():
        loads[3].wait()

        def step(n, carry):
            lanes = pl.ds(pl.multiple_of(n * 256, 256), 256)
            res = jnp.dot(n_s[pl.ds(PAIR_AT, 784), :], wq_v[:, lanes], preferred_element_type=F32)
            for i in range(7):
                scatter(lanes, i, res[PAIR_ROWS * i : PAIR_ROWS * (i + 1)])
            return carry

        lax.fori_loop(0, 6, step, 0)

    def qkv_last():
        def step(n, carry):
            lanes = pl.ds(pl.multiple_of(n * 256, 256), 256)
            last = jnp.dot(n_s[pl.ds(LAST_AT, PAIR_ROWS), :], wq_v[:, lanes], preferred_element_type=F32)
            fill = jnp.zeros((8, 256), F32)
            qw[pl.ds(14 * WIN_PITCH, 80), lanes] = jnp.concatenate([last[0:72], fill], axis=0).astype(BF16)
            qw[pl.ds(15 * WIN_PITCH + 32, 48), lanes] = jnp.concatenate([last[72:112], fill], axis=0).astype(BF16)
            return carry

        lax.fori_loop(0, 6, step, 0)

    def gather_halo():
        send_cor.wait_recv()
        corner = cor_in[...].astype(F32)
        send_col.wait_recv()
        for c in range(4):
            piece = corner[8 * (c // 2) : 8 * (c // 2) + 8]
            piece = piece[0:4] if c % 2 == 0 else piece[4:8]
            block = jnp.concatenate([col_in[c].astype(F32)[4:64], piece], axis=0)
            at = pl.ds(64 * c, 64)
            x_s[at, :] = block.astype(BF16)
            n_s[at, :] = norm(block)

    def qkv_halo():
        def step(n, carry):
            lanes = pl.ds(pl.multiple_of(n * 256, 256), 256)
            res = jnp.dot(n_s[pl.ds(0, LAST_AT), :], wq_v[:, lanes], preferred_element_type=F32)
            for i in range(2):
                for b in range(8):
                    both = [res[64 * (2 * i + j) + 8 * b : 64 * (2 * i + j) + 8 * b + 8] for j in (0, 1)]
                    at = pl.ds((2 * b + 1) * WIN_PITCH + 16 * i, 16)
                    qw[at, lanes] = jnp.concatenate(both, axis=0).astype(BF16)
            return carry

        lax.fori_loop(0, 6, step, 0)

    lane256 = lax.broadcasted_iota(jnp.int32, (80, 256), 1)
    block_of = lax.rem(lane256, 128) // 32

    def window(w):
        at = pl.ds(pl.multiple_of(w * WIN_PITCH, 16), WIN_PITCH)
        zero80 = jnp.zeros((80, 256), BF16)
        zero128 = jnp.zeros((128, 128), BF16)
        fill = jnp.zeros((48, D), BF16)
        ids = idw[at, :]
        wide = jnp.concatenate([ids, jnp.zeros((48, 128), BF16)], axis=0)
        same = lax.dot_general(ids, wide, NT, preferred_element_type=F32)
        shut = (same[0:72] - 1.0) * 1e30
        query = jnp.concatenate([qw[at, 0:D], fill], axis=0).T
        value = jnp.concatenate([qw[at, 2 * D : 3 * D], fill], axis=0).T
        outs = [None] * HEADS
        for g in range(2):
            keys = qw[at, D + 256 * g : D + 256 * g + 256]
            a, b = query[256 * g : 256 * g + 128], query[256 * g + 128 : 256 * g + 256]
            sides = [jnp.concatenate([a, zero128], axis=1), jnp.concatenate([zero128, b], axis=1)]
            masked = jnp.concatenate([jnp.where(block_of == j, keys, zero80) for j in range(4)], axis=0)
            scores = jnp.dot(masked, jnp.concatenate(sides, axis=0), preferred_element_type=F32)
            for j in range(4):
                raised, sums = [], []
                for t in range(2):
                    head = 8 * g + 4 * t + j
                    s = scores[80 * j : 80 * j + 72, 128 * t : 128 * t + 128] * scale
                    s = s + bias_v[72 * head : 72 * head + 72, :] + shut
                    ex = jnp.exp2(s - jnp.max(s, axis=0, keepdims=True))
                    sums.append(1.0 / jnp.sum(ex, axis=0, keepdims=True))
                    raised.append(ex)
                both = [jnp.concatenate(raised, axis=-1), jnp.zeros((8, 256), F32)]
                probs = jnp.concatenate(both, axis=0).astype(BF16)
                at_v = 256 * g + 32 * j
                left = [value[at_v : at_v + 32, 0:80], value[at_v + 128 : at_v + 160, 0:80]]
                res = jnp.dot(jnp.concatenate(left, axis=0), probs, preferred_element_type=F32)
                outs[8 * g + j] = res[0:32, 0:128] * sums[0]
                outs[8 * g + 4 + j] = res[32:64, 128:256] * sums[1]
        att[pl.ds(pl.multiple_of(w * WIN_PITCH, 16), 72), :] = jnp.concatenate(outs, axis=0).T[0:72]

    def attention():
        def attend(i, carry):
            for u in range(4):
                window(8 * lax.rem(i, 2) + 2 * u + i // 2)

            @pl.when(i == 0)
            def _():
                spread((3, 4))
                gather_last()
                qkv_last()

            @pl.when(i == 1)
            def _():
                share((1, 2))
                gather_halo()
                qkv_halo()

            @pl.when(i == 2)
            def _():
                share((3, 4))

            return carry

        lax.fori_loop(0, 4, attend, 0)

    def far_attention():
        def attend(i, carry):
            for u in range(4):
                window(4 * i + u)
            return carry

        lax.fori_loop(4, 6, attend, 0)

    def attended(w, pos):
        return att[w * WIN_PITCH + 8 * pos : w * WIN_PITCH + 8 * pos + 8, :]

    def order_halo(ref, s):
        for c in range(4):
            block = [attended(window_of(b, s), c) for b in range(8)]
            ref[64 * c : 64 * c + 64, :] = jnp.concatenate(block, axis=0).astype(BF16)

    def order_main():
        block = [att[14 * WIN_PITCH : 14 * WIN_PITCH + 72, :], att[15 * WIN_PITCH + 32 : 15 * WIN_PITCH + 72, :]]
        n_s[LAST_AT:PAIR_AT, :] = jnp.concatenate(block, axis=0).astype(BF16)
        for i, pair in enumerate(PAIRS):
            block = []
            for j in (0, 1):
                s, pos = (0, 2 * i + j) if i < 4 else (1, 2 * (i - 3) + j)
                if i == 4:
                    s, pos = j, 8
                block += [attended(2 * b + s, pos) for b in range(7)]
            n_s[PAIR_AT + 112 * i : PAIR_AT + 112 * i + 112, :] = jnp.concatenate(block, axis=0).astype(BF16)

    def project(start, size):
        at = pl.ds(start, size)
        mixed = x_s[at, :].astype(F32) + jnp.dot(n_s[at, :], wp_v[...], preferred_element_type=F32)
        mixed = mixed.astype(BF16)
        x_s[at, :] = mixed
        return mixed

    def raise_hidden(at, size, slots):
        for slot in slots:
            inner = jnp.dot(n_s[at, :], wu[slot].reshape(D, 256), preferred_element_type=F32)
            hid[0:size, 256 * slot : 256 * slot + 256] = gelu(inner).astype(BF16)

    def lower_hidden(size, low, high):
        weights = wd[low:high].reshape(256 * (high - low), D)
        return jnp.dot(hid[0:size, 256 * low : 256 * high], weights, preferred_element_type=F32)

    def mlp_near(start, size):
        at = pl.ds(start, size)
        n_s[at, :] = norm(project(start, size).astype(F32))
        raise_hidden(at, size, range(0, 5))
        acc[start - PAIR_AT : start - PAIR_AT + size, :] = x_s[at, :].astype(F32) + lower_hidden(size, 0, 5)

    def mlp_far(start, size):
        at = pl.ds(start, size)
        raise_hidden(at, size, range(5, 8))
        total = acc[start - PAIR_AT : start - PAIR_AT + size, :] + lower_hidden(size, 5, 8)
        out_t[at, :] = total.astype(BF16)

    def mlp_edge():
        at, size = pl.ds(0, PAIR_AT), PAIR_AT
        raise_hidden(at, size, range(8))
        out_t[at, :] = (x_e[...].astype(F32) + lower_hidden(size, 0, 8)).astype(BF16)

    backs = [
        remote(x_s.at[pl.ds(0, 256), :], ret_col, ret_send.at[0], ret_recv.at[0], (east, lat)),
        remote(back_cor, ret_cor, ret_send.at[1], ret_recv.at[1], (east, south)),
        remote(back_row, ret_row, ret_send.at[2], ret_recv.at[2], (lon, south)),
    ]

    def pack_ends(ref):
        ends = [ref[64 * c + 48 : 64 * c + 64, :].astype(F32)[8:16] for c in range(4)]
        packed = [jnp.where(sub8 < 4, swap4(ends[2 * i]), ends[2 * i + 1]) for i in range(2)]
        return jnp.concatenate(packed, axis=0).astype(BF16)

    def send_back_cols():
        order_halo(n_s, 1)
        project(0, 256)
        back_cor[...] = pack_ends(x_s)
        start_back()

    def far_rows(packed, i):
        piece = packed[8 * (i // 2) : 8 * (i // 2) + 8]
        return piece[0:4] if i % 2 == 0 else piece[4:8]

    def far_work():
        for c in (*far_sends, pass_far_all):
            c.wait_recv()
        far_ids()
        below = row_in[0:16, :].astype(F32)
        for c in range(4):
            block = jnp.concatenate([field_v[c].astype(F32)[4:64], far_rows(below, c)], axis=0)
            x_f[64 * c : 64 * c + 64, :] = block.astype(BF16)
            n_f[64 * c : 64 * c + 64, :] = norm(block)
        below = far_row[...].astype(F32)
        for k in range(5):
            block = jnp.concatenate([far_in[k].astype(F32)[4:64], far_rows(below, k + 1)], axis=0)
            n_f[256 + 64 * k : 320 + 64 * k, :] = norm(block)

        def step(n, carry):
            lanes = pl.ds(pl.multiple_of(n * 256, 256), 256)
            res = jnp.dot(n_f[...], wq_v[:, lanes], preferred_element_type=F32)
            for i in range(5):
                for b in range(8):
                    first = res[128 * i + 8 * b : 128 * i + 8 * b + 8]
                    second = res[128 * i + 64 + 8 * b : 128 * i + 72 + 8 * b] if i < 4 else jnp.zeros_like(first)
                    at = pl.ds((16 + b) * WIN_PITCH + 16 * i, 16)
                    qw[at, lanes] = jnp.concatenate([first, second], axis=0).astype(BF16)
            return carry

        lax.fori_loop(0, 6, step, 0)
        far_attention()
        order_halo(n_f, 2)
        mixed = x_f[...].astype(F32) + jnp.dot(n_f[0:256, :], wp_v[...], preferred_element_type=F32)
        ret_col[...] = mixed.astype(BF16)
        far_cor[...] = pack_ends(ret_col)
        far_back.start()

    def far_windows():
        @pl.when(is_first)
        def _():
            far_work()

    def send_back_rows():
        order_main()
        last = project(LAST_AT, PAIR_ROWS).astype(F32)
        packed = []
        for i in range(7):
            packed.append(jnp.where(sub8 < 4, swap4(last[16 * i : 16 * i + 8]), last[16 * i + 8 : 16 * i + 16]))
        packed.append(jnp.zeros_like(packed[0]))
        back_row[...] = jnp.concatenate(packed, axis=0).astype(BF16)
        backs[2].start()

    def head4(packed, i):
        piece = packed[8 * (i // 2) : 8 * (i // 2) + 8]
        return piece[0:4] if i % 2 == 0 else piece[4:8]

    def take_back():
        backs[2].wait_recv()
        above = ret_row[...].astype(F32)
        last = x_s[LAST_AT:PAIR_AT, :].astype(F32)
        block = []
        for k in range(14):
            block += [last[8 * k : 8 * k + 4], head4(above, k)]
        block = jnp.concatenate(block, axis=0)
        x_e[LAST_AT:PAIR_AT, :] = block.astype(BF16)
        n_s[LAST_AT:PAIR_AT, :] = norm(block)
        backs[1].wait_recv()
        above = ret_cor[...].astype(F32)

        @pl.when(jnp.logical_not(is_first))
        def _():
            backs[0].wait_recv()

        for c in range(4):
            block = jnp.concatenate([ret_col[64 * c : 64 * c + 64, :].astype(F32)[0:60], head4(above, c)], axis=0)
            x_e[64 * c : 64 * c + 64, :] = block.astype(BF16)
            n_s[64 * c : 64 * c + 64, :] = norm(block)

    def send_ids_done():
        for c in send_ids:
            c.wait_recv()

    send_halos()
    gather_main()
    for _, c in z_sends[8:]:
        c.start()
    qkv_main()
    spread((1, 2))
    relay()
    send_ids_done()
    main_ids(reg_s[...].astype(F32), range(8))
    halo_ids()
    attention()
    loads[4].wait()
    send_back_rows()
    send_back_cols()
    far_windows()
    for c in loads[5:7]:
        c.wait()
    await_weights((1, 2))
    mlp_near(368, 400)
    mlp_near(768, 384)
    await_weights((3, 4))
    mlp_far(368, 400)
    mlp_far(768, 384)
    stores = [local(out_t.at[pl.ds(PAIR_AT, 784), :], out_h.at[pl.ds(PAIR_AT, 784), :], 7)]
    stores[0].start()
    take_back()
    mlp_edge()
    stores.append(local(out_t.at[pl.ds(0, PAIR_AT), :], out_h.at[pl.ds(0, PAIR_AT), :], 8))
    stores[1].start()
    for c in stores:
        c.wait()
    relays_done()
    for _, c in z_sends:
        c.wait_send()
    for group in range(1, 5):
        for c in xy_sends[group] + sib_sends[group]:
            c.wait_send()
    for c in (send_cor, send_row, *send_ids, backs[2]):
        c.wait_send()


def finish_kernel(tokens, out_h, out_v, sem):
    stores = []

    def store_col(c, parts):
        out_v[c] = jnp.concatenate(parts, axis=0).astype(BF16)
        found = pltpu.make_async_copy(out_v.at[c], out_h.at[c], sem.at[c])
        found.start()
        stores.append(found)

    for c in range(4):
        rows = tokens[64 * c : 64 * c + 64, :].astype(F32)
        store_col(c, [rows[60:64], rows[0:60]])
    ends = tokens[LAST_AT:PAIR_AT, :].astype(F32)
    for i, pair in enumerate(PAIRS):
        rows = tokens[PAIR_AT + 112 * i : PAIR_AT + 112 * i + 112, :].astype(F32)
        for j, c in enumerate(pair):
            k = LAST.index(c)
            store_col(c + 4, [ends[8 * k + 4 : 8 * k + 8], rows[56 * j : 56 * j + 56], ends[8 * k : 8 * k + 4]])
    for found in stores:
        found.wait()


def block(field, region, w_qkv, w_proj, w_up, w_down, position_bias):
    vm = pltpu.VMEM
    dma = pltpu.SemaphoreType.DMA
    scratch = [
        vm((COLS, ROWS, D), BF16),
        vm((COLS, ROWS), jnp.int32),
        vm((1152, D), BF16),
        vm((1152, D), BF16),
        vm((24 * WIN_PITCH, 3 * D), BF16),
        vm((24 * WIN_PITCH, 128), BF16),
        vm((24 * WIN_PITCH, D), F32),
        vm((D, 3 * D), BF16),
        vm((D, D), BF16),
        vm((8, 4, 2, 64, 256), BF16),
        vm((8, 4, 2, 32, D), BF16),
        vm((72, 128), F32),
        vm((128, 128), F32),
        vm((HEADS * 72, 128), F32),
        vm((HEADS, 72, 72), F32),
        vm((1152, D), BF16),
        vm((PAIR_AT, D), BF16),
        vm((784, D), F32),
        vm((784, 2048), BF16),
        vm((16, D), BF16),
        vm((32, D), BF16),
        vm((5, ROWS, D), BF16),
        vm((32, D), BF16),
        vm((24, 128), jnp.int32),
        vm((24, 128), jnp.int32),
        vm((16, D), BF16),
        vm((256, D), BF16),
        vm((576, D), BF16),
        vm((24, 128), jnp.int32),
        vm((24, 128), jnp.int32),
        vm((24, 128), jnp.int32),
        vm((24, 128), jnp.int32),
        vm((80, D), BF16),
        vm((4, ROWS, D), BF16),
        vm((80, D), BF16),
        vm((16, D), BF16),
        vm((64, D), BF16),
        vm((16, D), BF16),
        vm((256, D), BF16),
        vm((64, D), BF16),
        vm((16, D), BF16),
        dma((9,)),
        dma((6,)),
        dma((6,)),
        dma((3,)),
        dma((3,)),
        dma((16,)),
        dma((16,)),
        dma((24,)),
        dma((24,)),
        dma((8,)),
        dma((8,)),
        dma((17,)),
        dma((1,)),
        dma((4,)),
        dma((4,)),
    ]
    tokens = pl.pallas_call(
        kernel,
        out_shape=jax.ShapeDtypeStruct((1152, D), BF16),
        in_specs=[pl.BlockSpec(memory_space=pl.ANY)] * 7,
        out_specs=pl.BlockSpec(memory_space=pl.ANY),
        scratch_shapes=scratch,
        compiler_params=pltpu.CompilerParams(
            collective_id=0, has_side_effects=True, vmem_limit_bytes=58 * 1024 * 1024
        ),
    )(
        field.transpose(1, 0, 2), region.T, w_qkv, w_proj,
        w_up.reshape(4, 2, 64, 256), w_down.reshape(4, 2, 32, D), position_bias,
    )
    done = pl.pallas_call(
        finish_kernel,
        out_shape=jax.ShapeDtypeStruct((COLS, ROWS, D), BF16),
        in_specs=[pl.BlockSpec(memory_space=pltpu.VMEM)],
        out_specs=pl.BlockSpec(memory_space=pl.ANY),
        scratch_shapes=[vm((COLS, ROWS, D), BF16), dma((COLS,))],
        compiler_params=pltpu.CompilerParams(vmem_limit_bytes=16 * 1024 * 1024),
    )(tokens)
    return done.transpose(1, 0, 2)


def solution(mesh):
    placed = (P("lat", "lon", None), P("lat", "lon"), P(), P(), P(None, "lat"), P("lat", None), P())
    return jax.shard_map(
        block, mesh=mesh, in_specs=placed, out_specs=P("lat", "lon", None), check_vma=False
    )
```

```python
import jax
import jax.numpy as jnp
from jax import lax
from jax.experimental import pallas as pl
from jax.experimental.pallas import tpu as pltpu
from jax.sharding import PartitionSpec as P

MESH = pl.DeviceIdType.MESH
D = 512
HEADS = 16
ROWS = 64
COLS = 18
LOG2E = 1.4426950408889634
ORDER = (5, 6, 7, 8, 0, 1, 2, 3, 4)
PAIRS = ((5, 6), (7, 8), (0, 1), (2, 3), (4, 13), (9, 10), (11, 12))
LAST = (5, 6, 7, 8, 0, 1, 2, 3, 4, 9, 10, 11, 12, 13)
LAST_AT = 256
PAIR_AT = 368
PAIR_ROWS = 112
WIN_PITCH = 80
F32 = jnp.float32
BF16 = jnp.bfloat16
NT = (((1,), (1,)), ((), ()))


def norm(x):
    center = jnp.mean(x, axis=-1, keepdims=True)
    moved = x - center
    spread = jnp.mean(moved * moved, axis=-1, keepdims=True)
    return (moved * lax.rsqrt(spread + 1e-05)).astype(BF16)


def gelu(x):
    half = 0.5 * x
    return half + half * jnp.tanh(x * (0.7978845608028654 + 0.0356774081363001 * (x * x)))


def swap4(x):
    return jnp.concatenate([x[4:8], x[0:4]], axis=0)


def kernel(
    field_h, region_h, wqkv_h, wproj_h, wup_h, wdown_h, bias_h, out_h,
    field_v, region_v, x_s, n_s, qw, idw, att, wq_v, wp_v, wu, wd,
    braw, btmp, bias_v, bias_in, out_t, x_e, acc, hid, rel_in, rel_far,
    far_in, far_row, reg_f, reg_fs, far_cor, x_f, n_f,
    reg_out, reg_e, reg_s, reg_se, row_out, col_in, row_in, cor_in,
    back_row, back_cor, ret_col, ret_row, ret_cor,
    local_sem, halo_send, halo_recv, ret_send, ret_recv, z_send, z_recv, xy_send, xy_recv,
    sib_send, sib_recv, rel_send, rel_recv, far_send, far_recv,
):
    lon = lax.axis_index("lon")
    lat = lax.axis_index("lat")
    core = lax.rem(lon, 2)
    z_hi = lon // 32
    x, y = lax.rem(lon // 8, 4), lax.rem(lon // 2, 4)
    west, east = lax.rem(lon + 63, 64), lax.rem(lon + 1, 64)
    north, south = lax.rem(lat + 7, 8), lax.rem(lat + 1, 8)
    half = z_hi * 32
    other = 32 - half
    is_first = lax.rem(lon, 32) == 0
    is_last = lax.rem(lon, 32) == 31
    chip = lax.rem(lon, 32) // 2
    sib = (lon + 1 - 2 * core, lat)

    def along_z(steps):
        to = lat + steps + 16
        return (lax.rem(z_hi + to // 8, 2) * 32 + lax.rem(lon, 32), lax.rem(to, 8))

    def in_plane(to_x, to_y):
        return (half + lax.rem(to_x, 4) * 8 + lax.rem(to_y, 4) * 2 + core, lat)

    z_to = [along_z(steps) for steps in (1, -1, 2, -2, 3, -3, 4, -4)]
    x_to = [in_plane(x + steps, y) for steps in (1, 3, 2)]
    y_to = [in_plane(x, y + steps) for steps in (1, 3, 2)]

    def local(src, dst, i):
        return pltpu.make_async_copy(src, dst, local_sem.at[i])

    def remote(src, dst, ssem, rsem, dev):
        return pltpu.make_async_remote_copy(
            src_ref=src, dst_ref=dst, send_sem=ssem, recv_sem=rsem, device_id=dev, device_id_type=MESH
        )

    loads = [
        local(field_h, field_v, 0),
        local(region_h, region_v, 1),
        local(bias_h, bias_in, 2),
        local(wqkv_h, wq_v, 3),
        local(wproj_h, wp_v, 4),
        local(wup_h, wu.at[0], 5),
        local(wdown_h, wd.at[0], 6),
    ]
    for c in loads:
        c.start()

    partners = [(west, lat), (east, lat), (lon, north), (lon, south), (west, north), (east, south), (west, south), sib]
    partners += z_to + x_to + y_to
    barrier = pltpu.get_barrier_semaphore()

    def greet(dev):
        pl.semaphore_signal(barrier, inc=1, device_id=dev, device_id_type=MESH)

    def greet_plane(first, count):
        def step(i, carry):
            greet((first + 2 * i, lat))
            return carry

        lax.fori_loop(0, count, step, 0)

    for dev in partners:
        greet(dev)
    near_relay = jnp.logical_and(core == 0, jnp.logical_not(is_first))
    far_relay = jnp.logical_and(core == 1, chip < 10)

    @pl.when(is_first)
    def _():
        greet_plane(other + 1, 10)

    @pl.when(is_last)
    def _():
        greet_plane(other, 16)

    @pl.when(near_relay)
    def _():
        greet((half, lat))

    @pl.when(far_relay)
    def _():
        greet((half + 31, lat))

    more = jnp.where(jnp.logical_or(core == 0, far_relay), 1, 0)
    more = more + jnp.where(is_first, 15, 0) + jnp.where(is_last, 10, 0)
    def turn_biases():
        loads[2].wait()
        braw[...] = jnp.zeros_like(braw)

        def turn_bias(h, carry):
            braw[:, 0:72] = bias_in[h]
            first = [braw[pl.ds(c, 8, stride=9), :] for c in ORDER]
            first.append(jnp.zeros((56, 128), F32))
            btmp[...] = jnp.concatenate(first, axis=0).T
            second = [btmp[pl.ds(c, 8, stride=9), :] for c in ORDER]
            bias_v[pl.ds(pl.multiple_of(h * 72, 8), 72), :] = jnp.concatenate(second, axis=0) * LOG2E
            return carry

        lax.fori_loop(0, HEADS, turn_bias, 0)

    turn_biases()

    z_sends = []
    for i, dev in enumerate(z_to):
        slot = min(i + 1, 7)
        if i != 7:
            z_sends.append((slot, remote(wup_h.at[x, core], wu.at[slot, x, core], z_send.at[2 * i], z_recv.at[2 * i], dev)))
        if i != 6:
            j = 2 * i + 1
            z_sends.append((slot, remote(wdown_h.at[y, core], wd.at[slot, y, core], z_send.at[j], z_recv.at[j], dev)))
    xy_sends, sib_sends = {}, {}
    for group in range(1, 5):
        slots = pl.ds(2 * group - 1, 2 if group < 4 else 1)
        mine_up, mine_down = wu.at[slots, x, core], wd.at[slots, y, core]
        found = []
        for j in range(3):
            i = (group - 1) * 6 + 2 * j
            found.append(remote(mine_up, mine_up, xy_send.at[i], xy_recv.at[i], x_to[j]))
            found.append(remote(mine_down, mine_down, xy_send.at[i + 1], xy_recv.at[i + 1], y_to[j]))
        xy_sends[group] = found
        found = []
        for kind, ref in enumerate((wu, wd)):
            i = (group - 1) * 2 + kind
            view = ref.at[slots, :, core]
            found.append(remote(view, view, sib_send.at[i], sib_recv.at[i], sib))
        sib_sends[group] = found

    def spread(groups):
        for group in groups:
            for slot, c in z_sends:
                if (slot + 1) // 2 == group:
                    c.wait_recv()
            for c in xy_sends[group]:
                c.start()

    def share(groups):
        for group in groups:
            for c in xy_sends[group]:
                c.wait_recv()
            for c in sib_sends[group]:
                c.start()

    def await_weights(groups):
        for group in groups:
            for c in sib_sends[group]:
                c.wait_recv()

    def piece(ref, r):
        return ref.at[r // 4, pl.ds(pl.multiple_of(lax.rem(r, 4) * 16, 16), 16)]

    def far_piece(ref, first, r):
        return ref.at[first + r // 2, pl.ds(pl.multiple_of(lax.rem(r, 2) * 32, 32), 32)]

    def push_col(r):
        return remote(piece(field_h, r), rel_in, rel_send.at[r], rel_recv.at[0], (half + 2 * r, lat))

    def push_far(r):
        return remote(far_piece(field_h, 13, r), rel_far, rel_send.at[r], rel_recv.at[0], (half + 1 + 2 * r, lat))

    own_col = remote(piece(field_h, 0), piece(col_in, 0), rel_send.at[16], halo_recv.at[0], (other + 31, lat))
    pass_col = remote(rel_in, piece(col_in, chip), rel_send.at[16], halo_recv.at[0], (other + 31, lat))
    near_chip = jnp.where(far_relay, chip, 0)
    pass_far = remote(rel_far, far_piece(far_in, 0, near_chip), rel_send.at[16], far_recv.at[0], (other, lat))
    far_sends = [
        remote(reg_out, reg_f, far_send.at[0], far_recv.at[1], (other, lat)),
        remote(reg_out, reg_fs, far_send.at[1], far_recv.at[2], (other, north)),
        remote(row_out.at[pl.ds(48, 32), :], far_row, far_send.at[2], far_recv.at[3], (other, north)),
    ]
    pass_far_all = remote(far_in, far_in, far_send.at[0], far_recv.at[0], (other, lat))
    far_back = remote(far_cor, ret_cor, far_send.at[3], ret_recv.at[1], (lon, south))

    def every(low, high, act):
        def step(r, carry):
            act(r)
            return carry

        lax.fori_loop(low, high, step, 0)

    def start_col():
        @pl.when(is_first)
        def _():
            own_col.start()
            every(1, 16, lambda r: push_col(r).start())

        @pl.when(jnp.logical_not(is_first))
        def _():
            send_col.start()

        @pl.when(is_last)
        def _():
            every(0, 10, lambda r: push_far(r).start())

    def relay():
        @pl.when(near_relay)
        def _():
            pltpu.make_async_copy(rel_in, rel_in, rel_recv.at[0]).wait()
            pass_col.start()

        @pl.when(far_relay)
        def _():
            pltpu.make_async_copy(rel_far, rel_far, rel_recv.at[0]).wait()
            pass_far.start()

    def start_back():
        @pl.when(jnp.logical_not(is_last))
        def _():
            backs[0].start()
            backs[1].start()

    def relays_done():
        @pl.when(is_first)
        def _():
            own_col.wait_send()
            every(1, 16, lambda r: push_col(r).wait_send())
            far_back.wait_send()

        @pl.when(jnp.logical_not(is_first))
        def _():
            send_col.wait_send()

        @pl.when(is_last)
        def _():
            every(0, 10, lambda r: push_far(r).wait_send())
            for c in far_sends:
                c.wait_send()

        @pl.when(jnp.logical_not(is_last))
        def _():
            backs[0].wait_send()
            backs[1].wait_send()

        @pl.when(near_relay)
        def _():
            pass_col.wait_send()

        @pl.when(far_relay)
        def _():
            pass_far.wait_send()

    send_col = remote(field_h.at[pl.ds(0, 4)], col_in, halo_send.at[0], halo_recv.at[0], (west, lat))
    send_row = remote(row_out, row_in, halo_send.at[1], halo_recv.at[1], (lon, north))
    send_cor = remote(row_out.at[pl.ds(0, 16), :], cor_in, halo_send.at[2], halo_recv.at[2], (west, north))
    send_ids = [
        remote(reg_out, reg_e, halo_send.at[3], halo_recv.at[3], (west, lat)),
        remote(reg_out, reg_s, halo_send.at[4], halo_recv.at[4], (lon, north)),
        remote(reg_out, reg_se, halo_send.at[5], halo_recv.at[5], (west, north)),
    ]
    sub8 = lax.broadcasted_iota(jnp.int32, (8, D), 0)
    scale = LOG2E * 32 ** (-0.5)

    def send_halos():
        pl.semaphore_wait(barrier, len(partners) + more)
        start_col()
        for c in send_ids:
            c.start()

        @pl.when(is_last)
        def _():
            for c in far_sends[0:2]:
                c.start()

        tops = [field_v[c, 0:16, :].astype(F32)[0:8] for c in range(COLS)]
        packed = [jnp.where(sub8 < 4, tops[2 * i], swap4(tops[2 * i + 1])) for i in range(9)]
        packed.append(jnp.zeros_like(packed[0]))
        row_out[...] = jnp.concatenate(packed, axis=0).astype(BF16)
        send_row.start()
        send_cor.start()

        @pl.when(is_last)
        def _():
            far_sends[2].start()

        for _, c in z_sends[0:8]:
            c.start()

    lane24 = lax.broadcasted_iota(jnp.int32, (24, 128), 1)
    lane64 = lax.broadcasted_iota(jnp.int32, (64, 128), 1)

    def id_rows(here, below):
        moved = jnp.where(lane24 < 60, pltpu.roll(here, 124, 1), pltpu.roll(below, 60, 1))
        tall = jnp.concatenate([moved, jnp.zeros((104, 128), F32)], axis=0)
        return tall.T[0:64]

    def hot_col(table, c):
        wide = jnp.broadcast_to(table[:, c : c + 1], (64, 128))
        return (wide == lane64.astype(F32)).astype(F32)

    def window_of(b, s):
        return 2 * b + s if s < 2 else 16 + b

    def put_ids(s, pos, top, low, bands):
        for b in bands:
            rows = [top[8 * b : 8 * b + 8], low[8 * b : 8 * b + 8]]
            idw[pl.ds(window_of(b, s) * WIN_PITCH + 16 * pos, 16), :] = jnp.concatenate(rows, axis=0).astype(BF16)

    def main_ids(below, bands):
        table = id_rows(reg_out[...].astype(F32), below)
        zero = jnp.zeros((64, 128), F32)
        for i, (a, z) in enumerate(PAIRS):
            first, second = hot_col(table, a + 4), hot_col(table, z + 4)
            if i < 4:
                put_ids(0, i, first, second, bands)
            elif i == 4:
                put_ids(0, 4, first, zero, bands)
                put_ids(1, 4, second, zero, bands)
            else:
                put_ids(1, i - 3, first, second, bands)

    def far_ids():
        table = id_rows(reg_out[...].astype(F32), reg_s[...].astype(F32))
        for i in (0, 1):
            put_ids(2, i, hot_col(table, 2 * i), hot_col(table, 2 * i + 1), range(8))
        table = id_rows(reg_f[...].astype(F32), reg_fs[...].astype(F32))
        put_ids(2, 2, hot_col(table, 13), hot_col(table, 14), range(8))
        put_ids(2, 3, hot_col(table, 15), hot_col(table, 16), range(8))
        put_ids(2, 4, hot_col(table, 17), jnp.zeros((64, 128), F32), range(8))

    def halo_ids():
        table = id_rows(reg_e[...].astype(F32), reg_se[...].astype(F32))
        for i in (0, 1):
            put_ids(1, i, hot_col(table, 2 * i), hot_col(table, 2 * i + 1), range(8))

    def gather_main():
        for i, pair in enumerate(PAIRS):
            rows = [field_v[c + 4].astype(F32)[4:60] for c in pair]
            block = jnp.concatenate(rows, axis=0)
            at = pl.ds(PAIR_AT + PAIR_ROWS * i, PAIR_ROWS)
            x_s[at, :] = block.astype(BF16)
            n_s[at, :] = norm(block)

    def scatter(part, i, res):
        lanes = part
        for b in range(7):
            first, second = res[8 * b : 8 * b + 8], res[56 + 8 * b : 64 + 8 * b]
            if i == 4:
                fill = jnp.zeros_like(first)
                for s, piece in ((0, first), (1, second)):
                    both = jnp.concatenate([piece, fill], axis=0).astype(BF16)
                    qw[pl.ds((2 * b + s) * WIN_PITCH + 64, 16), lanes] = both
            else:
                s, pos = (0, i) if i < 4 else (1, i - 3)
                both = jnp.concatenate([first, second], axis=0).astype(BF16)
                qw[pl.ds((2 * b + s) * WIN_PITCH + 16 * pos, 16), lanes] = both

    def gather_last():
        send_row.wait_recv()
        below = row_in[...].astype(F32)
        ready = {}
        for c in range(14):
            piece = below[16 + 8 * (c // 2) : 24 + 8 * (c // 2)]
            if c % 2 == 0:
                piece = swap4(piece)
            mine = swap4(field_v[c + 4, 48:64, :].astype(F32)[8:16])
            ready[c] = jnp.where(sub8 < 4, mine, piece)
        block = jnp.concatenate([ready[c] for c in LAST], axis=0)
        at = pl.ds(LAST_AT, PAIR_ROWS)
        x_s[at, :] = block.astype(BF16)
        n_s[at, :] = norm(block)

    def qkv_main():
        def step(n, carry):
            lanes = pl.ds(pl.multiple_of(n * 256, 256), 256)
            res = jnp.dot(n_s[pl.ds(PAIR_AT, 784), :], wq_v[:, lanes], preferred_element_type=F32)
            for i in range(7):
                scatter(lanes, i, res[PAIR_ROWS * i : PAIR_ROWS * (i + 1)])
            return carry

        lax.fori_loop(0, 6, step, 0)

    def qkv_last():
        def step(n, carry):
            lanes = pl.ds(pl.multiple_of(n * 256, 256), 256)
            last = jnp.dot(n_s[pl.ds(LAST_AT, PAIR_ROWS), :], wq_v[:, lanes], preferred_element_type=F32)
            fill = jnp.zeros((8, 256), F32)
            qw[pl.ds(14 * WIN_PITCH, 80), lanes] = jnp.concatenate([last[0:72], fill], axis=0).astype(BF16)
            qw[pl.ds(15 * WIN_PITCH + 32, 48), lanes] = jnp.concatenate([last[72:112], fill], axis=0).astype(BF16)
            return carry

        lax.fori_loop(0, 6, step, 0)

    def gather_halo():
        send_cor.wait_recv()
        corner = cor_in[...].astype(F32)
        send_col.wait_recv()
        for c in range(4):
            piece = corner[8 * (c // 2) : 8 * (c // 2) + 8]
            piece = piece[0:4] if c % 2 == 0 else piece[4:8]
            block = jnp.concatenate([col_in[c].astype(F32)[4:64], piece], axis=0)
            at = pl.ds(64 * c, 64)
            x_s[at, :] = block.astype(BF16)
            n_s[at, :] = norm(block)

    def qkv_halo():
        def step(n, carry):
            lanes = pl.ds(pl.multiple_of(n * 256, 256), 256)
            res = jnp.dot(n_s[pl.ds(0, LAST_AT), :], wq_v[:, lanes], preferred_element_type=F32)
            for i in range(2):
                for b in range(8):
                    both = [res[64 * (2 * i + j) + 8 * b : 64 * (2 * i + j) + 8 * b + 8] for j in (0, 1)]
                    at = pl.ds((2 * b + 1) * WIN_PITCH + 16 * i, 16)
                    qw[at, lanes] = jnp.concatenate(both, axis=0).astype(BF16)
            return carry

        lax.fori_loop(0, 6, step, 0)

    lane256 = lax.broadcasted_iota(jnp.int32, (80, 256), 1)
    block_of = lax.rem(lane256, 128) // 32

    def window(w):
        at = pl.ds(pl.multiple_of(w * WIN_PITCH, 16), WIN_PITCH)
        zero80 = jnp.zeros((80, 256), BF16)
        zero128 = jnp.zeros((128, 128), BF16)
        fill = jnp.zeros((48, D), BF16)
        ids = idw[at, :]
        wide = jnp.concatenate([ids, jnp.zeros((48, 128), BF16)], axis=0)
        same = lax.dot_general(ids, wide, NT, preferred_element_type=F32)
        shut = (same[0:72] - 1.0) * 1e30
        query = jnp.concatenate([qw[at, 0:D], fill], axis=0).T
        value = jnp.concatenate([qw[at, 2 * D : 3 * D], fill], axis=0).T
        outs = [None] * HEADS
        for g in range(2):
            keys = qw[at, D + 256 * g : D + 256 * g + 256]
            a, b = query[256 * g : 256 * g + 128], query[256 * g + 128 : 256 * g + 256]
            sides = [jnp.concatenate([a, zero128], axis=1), jnp.concatenate([zero128, b], axis=1)]
            masked = jnp.concatenate([jnp.where(block_of == j, keys, zero80) for j in range(4)], axis=0)
            scores = jnp.dot(masked, jnp.concatenate(sides, axis=0), preferred_element_type=F32)
            for j in range(4):
                raised, sums = [], []
                for t in range(2):
                    head = 8 * g + 4 * t + j
                    s = scores[80 * j : 80 * j + 72, 128 * t : 128 * t + 128] * scale
                    s = s + bias_v[72 * head : 72 * head + 72, :] + shut
                    ex = jnp.exp2(s - jnp.max(s, axis=0, keepdims=True))
                    sums.append(1.0 / jnp.sum(ex, axis=0, keepdims=True))
                    raised.append(ex)
                both = [jnp.concatenate(raised, axis=-1), jnp.zeros((8, 256), F32)]
                probs = jnp.concatenate(both, axis=0).astype(BF16)
                at_v = 256 * g + 32 * j
                left = [value[at_v : at_v + 32, 0:80], value[at_v + 128 : at_v + 160, 0:80]]
                res = jnp.dot(jnp.concatenate(left, axis=0), probs, preferred_element_type=F32)
                outs[8 * g + j] = res[0:32, 0:128] * sums[0]
                outs[8 * g + 4 + j] = res[32:64, 128:256] * sums[1]
        att[pl.ds(pl.multiple_of(w * WIN_PITCH, 16), 72), :] = jnp.concatenate(outs, axis=0).T[0:72]

    def attention():
        def attend(i, carry):
            for u in range(4):
                window(8 * lax.rem(i, 2) + 2 * u + i // 2)

            @pl.when(i == 0)
            def _():
                spread((3, 4))
                gather_last()
                qkv_last()

            @pl.when(i == 1)
            def _():
                share((1, 2))
                gather_halo()
                qkv_halo()

            @pl.when(i == 2)
            def _():
                share((3, 4))

            return carry

        lax.fori_loop(0, 4, attend, 0)

    def far_attention():
        def attend(i, carry):
            for u in range(4):
                window(4 * i + u)
            return carry

        lax.fori_loop(4, 6, attend, 0)

    def attended(w, pos):
        return att[w * WIN_PITCH + 8 * pos : w * WIN_PITCH + 8 * pos + 8, :]

    def order_halo(ref, s):
        for c in range(4):
            block = [attended(window_of(b, s), c) for b in range(8)]
            ref[64 * c : 64 * c + 64, :] = jnp.concatenate(block, axis=0).astype(BF16)

    def order_main():
        block = [att[14 * WIN_PITCH : 14 * WIN_PITCH + 72, :], att[15 * WIN_PITCH + 32 : 15 * WIN_PITCH + 72, :]]
        n_s[LAST_AT:PAIR_AT, :] = jnp.concatenate(block, axis=0).astype(BF16)
        for i, pair in enumerate(PAIRS):
            block = []
            for j in (0, 1):
                s, pos = (0, 2 * i + j) if i < 4 else (1, 2 * (i - 3) + j)
                if i == 4:
                    s, pos = j, 8
                block += [attended(2 * b + s, pos) for b in range(7)]
            n_s[PAIR_AT + 112 * i : PAIR_AT + 112 * i + 112, :] = jnp.concatenate(block, axis=0).astype(BF16)

    def project(start, size):
        at = pl.ds(start, size)
        mixed = x_s[at, :].astype(F32) + jnp.dot(n_s[at, :], wp_v[...], preferred_element_type=F32)
        mixed = mixed.astype(BF16)
        x_s[at, :] = mixed
        return mixed

    def raise_hidden(at, size, slots):
        for slot in slots:
            inner = jnp.dot(n_s[at, :], wu[slot].reshape(D, 256), preferred_element_type=F32)
            hid[0:size, 256 * slot : 256 * slot + 256] = gelu(inner).astype(BF16)

    def lower_hidden(size, low, high):
        weights = wd[low:high].reshape(256 * (high - low), D)
        return jnp.dot(hid[0:size, 256 * low : 256 * high], weights, preferred_element_type=F32)

    def mlp_near(start, size):
        at = pl.ds(start, size)
        n_s[at, :] = norm(project(start, size).astype(F32))
        raise_hidden(at, size, range(0, 5))
        acc[start - PAIR_AT : start - PAIR_AT + size, :] = x_s[at, :].astype(F32) + lower_hidden(size, 0, 5)

    def mlp_far(start, size):
        at = pl.ds(start, size)
        raise_hidden(at, size, range(5, 8))
        total = acc[start - PAIR_AT : start - PAIR_AT + size, :] + lower_hidden(size, 5, 8)
        out_t[at, :] = total.astype(BF16)

    def mlp_edge():
        at, size = pl.ds(0, PAIR_AT), PAIR_AT
        raise_hidden(at, size, range(8))
        out_t[at, :] = (x_e[...].astype(F32) + lower_hidden(size, 0, 8)).astype(BF16)

    backs = [
        remote(x_s.at[pl.ds(0, 256), :], ret_col, ret_send.at[0], ret_recv.at[0], (east, lat)),
        remote(back_cor, ret_cor, ret_send.at[1], ret_recv.at[1], (east, south)),
        remote(back_row, ret_row, ret_send.at[2], ret_recv.at[2], (lon, south)),
    ]

    def pack_ends(ref):
        ends = [ref[64 * c + 48 : 64 * c + 64, :].astype(F32)[8:16] for c in range(4)]
        packed = [jnp.where(sub8 < 4, swap4(ends[2 * i]), ends[2 * i + 1]) for i in range(2)]
        return jnp.concatenate(packed, axis=0).astype(BF16)

    def send_back_cols():
        order_halo(n_s, 1)
        project(0, 256)
        back_cor[...] = pack_ends(x_s)
        start_back()

    def far_rows(packed, i):
        piece = packed[8 * (i // 2) : 8 * (i // 2) + 8]
        return piece[0:4] if i % 2 == 0 else piece[4:8]

    def far_work():
        for c in (*far_sends, pass_far_all):
            c.wait_recv()
        far_ids()
        below = row_in[0:16, :].astype(F32)
        for c in range(4):
            block = jnp.concatenate([field_v[c].astype(F32)[4:64], far_rows(below, c)], axis=0)
            x_f[64 * c : 64 * c + 64, :] = block.astype(BF16)
            n_f[64 * c : 64 * c + 64, :] = norm(block)
        below = far_row[...].astype(F32)
        for k in range(5):
            block = jnp.concatenate([far_in[k].astype(F32)[4:64], far_rows(below, k + 1)], axis=0)
            n_f[256 + 64 * k : 320 + 64 * k, :] = norm(block)

        def step(n, carry):
            lanes = pl.ds(pl.multiple_of(n * 256, 256), 256)
            res = jnp.dot(n_f[...], wq_v[:, lanes], preferred_element_type=F32)
            for i in range(5):
                for b in range(8):
                    first = res[128 * i + 8 * b : 128 * i + 8 * b + 8]
                    second = res[128 * i + 64 + 8 * b : 128 * i + 72 + 8 * b] if i < 4 else jnp.zeros_like(first)
                    at = pl.ds((16 + b) * WIN_PITCH + 16 * i, 16)
                    qw[at, lanes] = jnp.concatenate([first, second], axis=0).astype(BF16)
            return carry

        lax.fori_loop(0, 6, step, 0)
        far_attention()
        order_halo(n_f, 2)
        mixed = x_f[...].astype(F32) + jnp.dot(n_f[0:256, :], wp_v[...], preferred_element_type=F32)
        ret_col[...] = mixed.astype(BF16)
        far_cor[...] = pack_ends(ret_col)
        far_back.start()

    def far_windows():
        @pl.when(is_first)
        def _():
            far_work()

    def send_back_rows():
        order_main()
        last = project(LAST_AT, PAIR_ROWS).astype(F32)
        packed = []
        for i in range(7):
            packed.append(jnp.where(sub8 < 4, swap4(last[16 * i : 16 * i + 8]), last[16 * i + 8 : 16 * i + 16]))
        packed.append(jnp.zeros_like(packed[0]))
        back_row[...] = jnp.concatenate(packed, axis=0).astype(BF16)
        backs[2].start()

    def head4(packed, i):
        piece = packed[8 * (i // 2) : 8 * (i // 2) + 8]
        return piece[0:4] if i % 2 == 0 else piece[4:8]

    def take_back():
        backs[2].wait_recv()
        above = ret_row[...].astype(F32)
        last = x_s[LAST_AT:PAIR_AT, :].astype(F32)
        block = []
        for k in range(14):
            block += [last[8 * k : 8 * k + 4], head4(above, k)]
        block = jnp.concatenate(block, axis=0)
        x_e[LAST_AT:PAIR_AT, :] = block.astype(BF16)
        n_s[LAST_AT:PAIR_AT, :] = norm(block)
        backs[1].wait_recv()
        above = ret_cor[...].astype(F32)

        @pl.when(jnp.logical_not(is_first))
        def _():
            backs[0].wait_recv()

        for c in range(4):
            block = jnp.concatenate([ret_col[64 * c : 64 * c + 64, :].astype(F32)[0:60], head4(above, c)], axis=0)
            x_e[64 * c : 64 * c + 64, :] = block.astype(BF16)
            n_s[64 * c : 64 * c + 64, :] = norm(block)

    def send_ids_done():
        for c in send_ids:
            c.wait_recv()

    early = jnp.logical_or(is_first, jnp.logical_and(z_hi == 0, lat < 5))
    turn = jnp.where(early, 0, 1)
    loads[1].wait()
    reg_out[...] = jnp.zeros_like(reg_out)
    reg_out[0:18, 0:64] = region_v[...]
    loads[0].wait()
    loads[3].wait()

    def opening(k, carry):
        @pl.when(k == 1 - turn)
        def _():
            send_halos()

        @pl.when(k == 1)
        def _():
            for _, c in z_sends[8:]:
                c.start()

        @pl.when(k == turn)
        def _():
            gather_main()
            qkv_main()

        return carry

    lax.fori_loop(0, 2, opening, 0)
    spread((1, 2))
    relay()
    send_ids_done()
    main_ids(reg_s[...].astype(F32), range(8))
    halo_ids()
    attention()
    loads[4].wait()
    send_back_rows()
    send_back_cols()
    for c in loads[5:7]:
        c.wait()
    await_weights((1, 2))
    mlp_near(368, 400)
    mlp_near(768, 384)
    far_windows()
    await_weights((3, 4))
    mlp_far(368, 400)
    mlp_far(768, 384)
    stores = [local(out_t.at[pl.ds(PAIR_AT, 784), :], out_h.at[pl.ds(PAIR_AT, 784), :], 7)]
    stores[0].start()
    take_back()
    mlp_edge()
    stores.append(local(out_t.at[pl.ds(0, PAIR_AT), :], out_h.at[pl.ds(0, PAIR_AT), :], 8))
    stores[1].start()
    for c in stores:
        c.wait()
    relays_done()
    for _, c in z_sends:
        c.wait_send()
    for group in range(1, 5):
        for c in xy_sends[group] + sib_sends[group]:
            c.wait_send()
    for c in (send_cor, send_row, *send_ids, backs[2]):
        c.wait_send()


def finish_kernel(tokens, out_h, out_v, sem):
    stores = []

    def store_col(c, parts):
        out_v[c] = jnp.concatenate(parts, axis=0).astype(BF16)
        found = pltpu.make_async_copy(out_v.at[c], out_h.at[c], sem.at[c])
        found.start()
        stores.append(found)

    for c in range(4):
        rows = tokens[64 * c : 64 * c + 64, :].astype(F32)
        store_col(c, [rows[60:64], rows[0:60]])
    ends = tokens[LAST_AT:PAIR_AT, :].astype(F32)
    for i, pair in enumerate(PAIRS):
        rows = tokens[PAIR_AT + 112 * i : PAIR_AT + 112 * i + 112, :].astype(F32)
        for j, c in enumerate(pair):
            k = LAST.index(c)
            store_col(c + 4, [ends[8 * k + 4 : 8 * k + 8], rows[56 * j : 56 * j + 56], ends[8 * k : 8 * k + 4]])
    for found in stores:
        found.wait()


def block(field, region, w_qkv, w_proj, w_up, w_down, position_bias):
    vm = pltpu.VMEM
    dma = pltpu.SemaphoreType.DMA
    scratch = [
        vm((COLS, ROWS, D), BF16),
        vm((COLS, ROWS), jnp.int32),
        vm((1152, D), BF16),
        vm((1152, D), BF16),
        vm((24 * WIN_PITCH, 3 * D), BF16),
        vm((24 * WIN_PITCH, 128), BF16),
        vm((24 * WIN_PITCH, D), F32),
        vm((D, 3 * D), BF16),
        vm((D, D), BF16),
        vm((8, 4, 2, 64, 256), BF16),
        vm((8, 4, 2, 32, D), BF16),
        vm((72, 128), F32),
        vm((128, 128), F32),
        vm((HEADS * 72, 128), F32),
        vm((HEADS, 72, 72), F32),
        vm((1152, D), BF16),
        vm((PAIR_AT, D), BF16),
        vm((784, D), F32),
        vm((784, 2048), BF16),
        vm((16, D), BF16),
        vm((32, D), BF16),
        vm((5, ROWS, D), BF16),
        vm((32, D), BF16),
        vm((24, 128), jnp.int32),
        vm((24, 128), jnp.int32),
        vm((16, D), BF16),
        vm((256, D), BF16),
        vm((576, D), BF16),
        vm((24, 128), jnp.int32),
        vm((24, 128), jnp.int32),
        vm((24, 128), jnp.int32),
        vm((24, 128), jnp.int32),
        vm((80, D), BF16),
        vm((4, ROWS, D), BF16),
        vm((80, D), BF16),
        vm((16, D), BF16),
        vm((64, D), BF16),
        vm((16, D), BF16),
        vm((256, D), BF16),
        vm((64, D), BF16),
        vm((16, D), BF16),
        dma((9,)),
        dma((6,)),
        dma((6,)),
        dma((3,)),
        dma((3,)),
        dma((16,)),
        dma((16,)),
        dma((24,)),
        dma((24,)),
        dma((8,)),
        dma((8,)),
        dma((17,)),
        dma((1,)),
        dma((4,)),
        dma((4,)),
    ]
    tokens = pl.pallas_call(
        kernel,
        out_shape=jax.ShapeDtypeStruct((1152, D), BF16),
        in_specs=[pl.BlockSpec(memory_space=pl.ANY)] * 7,
        out_specs=pl.BlockSpec(memory_space=pl.ANY),
        scratch_shapes=scratch,
        compiler_params=pltpu.CompilerParams(
            collective_id=0, has_side_effects=True, vmem_limit_bytes=58 * 1024 * 1024
        ),
    )(
        field.transpose(1, 0, 2), region.T, w_qkv, w_proj,
        w_up.reshape(4, 2, 64, 256), w_down.reshape(4, 2, 32, D), position_bias,
    )
    done = pl.pallas_call(
        finish_kernel,
        out_shape=jax.ShapeDtypeStruct((COLS, ROWS, D), BF16),
        in_specs=[pl.BlockSpec(memory_space=pltpu.VMEM)],
        out_specs=pl.BlockSpec(memory_space=pl.ANY),
        scratch_shapes=[vm((COLS, ROWS, D), BF16), dma((COLS,))],
        compiler_params=pltpu.CompilerParams(vmem_limit_bytes=16 * 1024 * 1024),
    )(tokens)
    return done.transpose(1, 0, 2)


def solution(mesh):
    placed = (P("lat", "lon", None), P("lat", "lon"), P(), P(), P(None, "lat"), P("lat", None), P())
    return jax.shard_map(
        block, mesh=mesh, in_specs=placed, out_specs=P("lat", "lon", None), check_vma=False
    )
```
